32 devices in a mesh: grp: 4 (over y, core), blk: 8 (over z, x).
Axes of the slice: x: 2, y: 2, z: 4, core: 2. Of those that a mesh axis runs over, the one named last changes fastest.
Arguments:
- main_hidden: bfloat16 [1024, 3072], P('blk', 'grp'), may hold values from -6 to 6
- ctrl_query: bfloat16 [1024, 1536], P('blk', 'grp'), may hold values from -150 to 150
- ctrl_key: bfloat16 [1024, 1536], P('blk', 'grp'), may hold values from -6 to 6
- ctrl_value: bfloat16 [1024, 1536], P('blk', 'grp'), may hold values from -6 to 6
- w_out: bfloat16 [1536, 3072], P('grp'), may hold values from -1 to 1
- d_mixed: bfloat16 [1024, 3072], P('blk', 'grp'), may hold values from -3 to 3
- control_slot: int32 [1024], P('blk'), may hold values from 0 to 1023, as said below
Outputs:
- main_mixed: bfloat16 [1024, 3072], P('blk', 'grp')
- d_query: bfloat16 [1024, 1536], P('blk', 'grp')
- d_key: bfloat16 [1024, 1536], P('blk', 'grp')
- d_value: bfloat16 [1024, 1536], P('blk', 'grp')
- d_w_out: float32 [1536, 3072], P('grp', 'blk')
The draws below stay inside these ranges and needn't reach their ends.
Inputs may be any that keep to these rules, and one draw needn't show every extreme that they name: `control_slot`: A permutation of the token positions. Every aligned block of 128 entries sends exactly 16 of its tokens into each aligned block of 128 control positions.
All inputs are finite; a program needn't handle non-finite values.
Results may differ from the reference program's by a relative error of at most 0.038.
Values may be sent and summed in bfloat16 or wider, within the bound.
A program may use at most 128 MiB of HBM per device.

```python
import math
import jax
import jax.numpy as jnp
from jax import lax

D = 3072
HD = 128
HEAD_GRP = 3
TOK_DEV = 128
HEADS = 12
HC = 1536
SEQ = 1024
N_GRP = 4


def shared_keys(key):
    return jnp.clip(jax.random.normal(key, (SEQ, HEADS * HD), jnp.float32), -6.0, 6.0)


def draw_ctrl_key(key, part):
    shared = shared_keys(key)
    return shared.astype(jnp.bfloat16)


def draw_ctrl_query(key, part):
    key = jax.random.fold_in(key, 23)
    drawn_rows = 2.0 * jnp.clip(jax.random.normal(key, (SEQ, HEADS * HD), jnp.float32), -6.0, 6.0)
    return drawn_rows.astype(jnp.bfloat16)


def draw_control_slot(key, part):
    key = jax.random.fold_in(key, 37)
    key_peers, key_slots = jax.random.split(key)
    blocks = SEQ // TOK_DEV
    per_peer = TOK_DEV // blocks
    peer_scores = jax.random.randint(key_peers, (blocks, blocks), 0, 1 << 16) * blocks + jnp.arange(blocks)[None, :]
    peer_order = jnp.argsort(peer_scores, axis=1).astype(jnp.int32)
    slot_scores = jax.random.randint(key_slots, (blocks, TOK_DEV), 0, 1 << 12) * TOK_DEV + jnp.arange(TOK_DEV)[None, :]
    slot_order = jnp.argsort(slot_scores, axis=1).astype(jnp.int32)
    positions = jnp.arange(SEQ)
    source = positions // TOK_DEV
    local = positions % TOK_DEV
    target = peer_order[source, local // per_peer]
    within = slot_order[target, source * per_peer + local % per_peer]
    return (target * TOK_DEV + within).astype(jnp.int32)


def shard_levels(own_key, shape, shards, low, high):
    def one(dim, blocks):
        steps = jax.random.uniform(jax.random.fold_in(jax.random.fold_in(own_key, 6), dim), (blocks,), jnp.float32, low / len(shards), high / len(shards))
        return jnp.repeat(jnp.exp(steps), shape[dim] // blocks).reshape((-1,) + (1,) * (len(shape) - dim - 1))

    level = one(*shards[0])
    for cut in shards[1:]:
        level = level * one(*cut)
    return level


def bell_draw(own_key, extent, scale, reach, shards=(), dtype=jnp.bfloat16):
    loudness = shard_levels(own_key, extent, shards, -0.22, 0.18) if shards else 1.0
    result = jax.random.normal(own_key, extent, jnp.float32) * scale * loudness
    return jnp.minimum(jnp.maximum(result, -reach), reach).astype(dtype)


def setup_inputs(seed: int = 0) -> dict:
    splits = jax.random.split(jax.random.key(seed), 8)
    return {
        "main_hidden": bell_draw(splits[0], (SEQ, D), 0.5, 6.0, ((0, 8), (1, 4))),
        "ctrl_query": draw_ctrl_query(jax.random.fold_in(splits[7], 71), 0),
        "ctrl_key": draw_ctrl_key(jax.random.fold_in(splits[7], 71), 0),
        "ctrl_value": bell_draw(splits[3], (SEQ, HC), 1.0, 6.0, ((0, 8), (1, 4))),
        "w_out": bell_draw(splits[4], (HC, D), (3.0 * HC ** -0.5), 1.0, ((0, 4),)),
        "d_mixed": bell_draw(splits[5], (SEQ, D), 0.2, 3.0, ((0, 8), (1, 4))),
        "control_slot": draw_control_slot(jax.random.fold_in(splits[7], 71), 0),
    }


def split_heads(matrix):
    return matrix.reshape(SEQ, HEADS, HD).transpose(1, 0, 2)

def merge_heads(tensor):
    return tensor.transpose(1, 0, 2).reshape(SEQ, HEADS * HD)

def reference(main_hidden, ctrl_query, ctrl_key, ctrl_value, w_out, d_mixed, control_slot):
    score_scale = 1.0 / math.sqrt(HD)
    block_rows = min(512, SEQ)
    block_count = SEQ // block_rows
    query_heads = split_heads(ctrl_query)
    key_heads = split_heads(ctrl_key)
    value_heads = split_heads(ctrl_value)

    def head_forward(operands):
        query_one, key_one, value_one = operands

        def one_block(query_rows):
            scores = jnp.dot(query_rows, key_one.T, preferred_element_type=jnp.float32) * score_scale
            row_peak = lax.optimization_barrier(jnp.max(scores, axis=1, keepdims=True))
            log_norm = row_peak + jnp.log(lax.optimization_barrier(jnp.sum(jnp.exp(scores - row_peak), axis=1, keepdims=True)))
            soft_weights = jnp.exp(scores - log_norm).astype(jnp.bfloat16)
            return (jnp.dot(soft_weights, value_one, preferred_element_type=jnp.float32), log_norm[:, 0])
        outputs, log_norm = lax.map(one_block, query_one.reshape(block_count, block_rows, HD))
        return (outputs.reshape(SEQ, HD), log_norm.reshape(SEQ))
    head_out, log_norms = lax.map(head_forward, (query_heads, key_heads, value_heads))
    attended = merge_heads(head_out).astype(jnp.bfloat16)
    head_cols = HEAD_GRP * HD
    residual = jnp.zeros((SEQ, D), jnp.float32)
    for group_idx in range(N_GRP):
        lower = group_idx * head_cols
        partial_term = jnp.dot(attended[:, lower:lower + head_cols], w_out[lower:lower + head_cols], preferred_element_type=jnp.float32).astype(jnp.bfloat16)
        residual = residual + lax.optimization_barrier(partial_term).astype(jnp.float32)
    main_mixed = (main_hidden.astype(jnp.float32) + residual[control_slot]).astype(jnp.bfloat16)
    d_control = jnp.zeros((SEQ, D), jnp.bfloat16).at[control_slot].set(d_mixed)
    d_attended = jnp.dot(d_control, w_out.T, preferred_element_type=jnp.float32).astype(jnp.bfloat16)
    d_w_out = jnp.dot(attended.T, d_control, preferred_element_type=jnp.float32)
    row_delta = lax.optimization_barrier(jnp.sum((d_attended.astype(jnp.float32) * attended.astype(jnp.float32)).reshape(SEQ, HEADS, HD), axis=2)).T
    d_heads = split_heads(d_attended)

    def head_backward(operands):
        query_one, key_one, value_one, grad_one, norm_one, delta_one = operands

        def one_block(totals, block_data):
            key_grad, value_grad = totals
            query_rows, grad_rows, norm_rows, delta_rows = block_data
            scores = jnp.dot(query_rows, key_one.T, preferred_element_type=jnp.float32) * score_scale
            soft_weights = jnp.exp(scores - norm_rows[:, None])
            d_probs = jnp.dot(grad_rows, value_one.T, preferred_element_type=jnp.float32)
            d_scores = (soft_weights * (d_probs - delta_rows[:, None])).astype(jnp.bfloat16)
            query_grad = jnp.dot(d_scores, key_one, preferred_element_type=jnp.float32) * score_scale
            key_grad = key_grad + jnp.dot(d_scores.T, query_rows, preferred_element_type=jnp.float32) * score_scale
            value_grad = value_grad + jnp.dot(soft_weights.astype(jnp.bfloat16).T, grad_rows, preferred_element_type=jnp.float32)
            return ((key_grad, value_grad), query_grad)
        zero_rows = jnp.zeros((SEQ, HD), jnp.float32)
        blocks_in = (query_one.reshape(block_count, block_rows, HD), grad_one.reshape(block_count, block_rows, HD), norm_one.reshape(block_count, block_rows), delta_one.reshape(block_count, block_rows))
        (key_grad, value_grad), query_grad = lax.scan(one_block, (zero_rows, zero_rows), blocks_in)
        return (query_grad.reshape(SEQ, HD), key_grad, value_grad)
    query_grad, key_grad, value_grad = lax.map(head_backward, (query_heads, key_heads, value_heads, d_heads, log_norms, row_delta))
    return (main_mixed, merge_heads(query_grad).astype(jnp.bfloat16), merge_heads(key_grad).astype(jnp.bfloat16), merge_heads(value_grad).astype(jnp.bfloat16), d_w_out)
```

```python
import math

import jax
import jax.numpy as jnp
from jax import lax
from jax.sharding import PartitionSpec as P

HD = 128
HEAD_GRP = 3


def on_device(main_hidden, ctrl_query, ctrl_key, ctrl_value, w_out, d_mixed, control_slot):
    rows_dev = ctrl_query.shape[0]
    feature_cols = d_mixed.shape[1]
    blocks = lax.axis_size("blk")
    per_peer = rows_dev // blocks
    score_scale = 1.0 / math.sqrt(HD)
    whole_key, whole_value = (
        lax.all_gather(ctrl_key, "blk", axis=0, tiled=True),
        lax.all_gather(ctrl_value, "blk", axis=0, tiled=True),
    )
    outputs = []
    norm_list = []
    for head_idx in range(HEAD_GRP):
        columns = slice(head_idx * HD, (head_idx + 1) * HD)
        scores = (
            jnp.dot(
                ctrl_query[:, columns], whole_key[:, columns].T, preferred_element_type=jnp.float32
            )
            * score_scale
        )
        row_peak = jnp.max(scores, axis=1, keepdims=True)
        log_norm = row_peak + jnp.log(jnp.sum(jnp.exp(scores - row_peak), axis=1, keepdims=True))
        soft_weights = jnp.exp(scores - log_norm).astype(jnp.bfloat16)
        outputs.append(
            jnp.dot(soft_weights, whole_value[:, columns], preferred_element_type=jnp.float32)
        )
        norm_list.append(log_norm[:, 0])
    attended = jnp.concatenate(outputs, axis=1).astype(jnp.bfloat16)
    log_norms = jnp.stack(norm_list, axis=1)
    target = control_slot // rows_dev
    within = control_slot % rows_dev
    sort_order = jnp.argsort(target)
    inverse = jnp.argsort(sort_order)
    send_within = within[sort_order].reshape(blocks, per_peer)
    arrived, arrived_grad = (
        lax.all_to_all(send_within, "blk", split_axis=0, concat_axis=0, tiled=True),
        lax.all_to_all(
            d_mixed[sort_order].reshape(blocks, per_peer, feature_cols),
            "blk",
            split_axis=0,
            concat_axis=0,
            tiled=True,
        ),
    )
    placed = arrived.reshape(rows_dev)
    grad_rows = jnp.zeros_like(d_mixed).at[placed].set(arrived_grad.reshape(rows_dev, feature_cols))
    residual = lax.psum_scatter(
        jnp.dot(attended, w_out, preferred_element_type=jnp.float32).astype(jnp.bfloat16),
        "grp",
        scatter_dimension=1,
        tiled=True,
    ).astype(jnp.float32)
    returned = lax.all_to_all(
        residual[placed].reshape(blocks, per_peer, feature_cols),
        "blk",
        split_axis=0,
        concat_axis=0,
        tiled=True,
    )
    residual = returned.reshape(rows_dev, feature_cols)[inverse]
    main_mixed = (main_hidden.astype(jnp.float32) + residual).astype(jnp.bfloat16)
    grad_full = lax.all_gather(grad_rows, "grp", axis=1, tiled=True)
    d_proj = jnp.dot(grad_full, w_out.T, preferred_element_type=jnp.float32).astype(jnp.bfloat16)
    d_w_out = lax.psum_scatter(
        jnp.dot(attended.T, grad_full, preferred_element_type=jnp.float32),
        "blk",
        scatter_dimension=1,
        tiled=True,
    )
    row_delta = jnp.sum(
        (d_proj.astype(jnp.float32) * attended.astype(jnp.float32)).reshape(rows_dev, HEAD_GRP, HD),
        axis=2,
    )
    all_norms, all_delta = (
        lax.all_gather(log_norms, "blk", axis=0, tiled=True),
        lax.all_gather(row_delta, "blk", axis=0, tiled=True),
    )
    query_grads = []
    for head_idx in range(HEAD_GRP):
        columns = slice(head_idx * HD, (head_idx + 1) * HD)
        scores = (
            jnp.dot(
                ctrl_query[:, columns], whole_key[:, columns].T, preferred_element_type=jnp.float32
            )
            * score_scale
        )
        soft_weights = jnp.exp(scores - log_norms[:, head_idx : head_idx + 1])
        d_probs = jnp.dot(
            d_proj[:, columns], whole_value[:, columns].T, preferred_element_type=jnp.float32
        )
        d_scores = (soft_weights * (d_probs - row_delta[:, head_idx : head_idx + 1])).astype(
            jnp.bfloat16
        )
        query_grads.append(
            jnp.dot(d_scores, whole_key[:, columns], preferred_element_type=jnp.float32)
            * score_scale
        )
    d_query = jnp.concatenate(query_grads, axis=1).astype(jnp.bfloat16)
    query_piece = lax.all_gather(ctrl_query, "blk", axis=0, tiled=True)
    grad_piece = lax.all_gather(d_proj, "blk", axis=0, tiled=True)
    key_terms = []
    value_terms = []
    for head_idx in range(HEAD_GRP):
        columns = slice(head_idx * HD, (head_idx + 1) * HD)
        scores = (
            jnp.dot(
                query_piece[:, columns], ctrl_key[:, columns].T, preferred_element_type=jnp.float32
            )
            * score_scale
        )
        soft_weights = jnp.exp(scores - all_norms[:, head_idx : head_idx + 1])
        d_probs = jnp.dot(
            grad_piece[:, columns], ctrl_value[:, columns].T, preferred_element_type=jnp.float32
        )
        d_scores = (soft_weights * (d_probs - all_delta[:, head_idx : head_idx + 1])).astype(
            jnp.bfloat16
        )
        key_terms.append(
            jnp.dot(d_scores.T, query_piece[:, columns], preferred_element_type=jnp.float32)
            * score_scale
        )
        value_terms.append(
            jnp.dot(
                soft_weights.astype(jnp.bfloat16).T,
                grad_piece[:, columns],
                preferred_element_type=jnp.float32,
            )
        )
    key_grad = jnp.concatenate(key_terms, axis=1)
    value_grad = jnp.concatenate(value_terms, axis=1)
    return (
        main_mixed,
        d_query,
        key_grad.astype(jnp.bfloat16),
        value_grad.astype(jnp.bfloat16),
        d_w_out,
    )


def on_device_small(main_hidden, ctrl_query, ctrl_key, ctrl_value, w_out, d_mixed, control_slot):
    f32, bf16 = jnp.float32, jnp.bfloat16
    rows_dev = ctrl_query.shape[0]
    blocks = lax.axis_size("blk")
    seq = rows_dev * blocks
    width = ctrl_query.shape[1]
    cols = w_out.shape[1] // blocks
    score_scale = 1.0 / math.sqrt(HD)
    me = lax.axis_index("blk")

    qkv = lax.all_gather(
        jnp.concatenate([ctrl_query, ctrl_key, ctrl_value], axis=1), "blk", axis=0, tiled=True
    )
    grad_full = lax.all_gather(d_mixed, "grp", axis=1, tiled=True)
    slots = lax.all_gather(control_slot, "blk", axis=0, tiled=True)
    to_main = (slots[:, None] == lax.broadcasted_iota(jnp.int32, (seq, seq), 1)).astype(bf16)
    d_proj_main = jnp.dot(grad_full, w_out.T, preferred_element_type=f32).astype(bf16)
    grad_cols = lax.all_to_all(
        grad_full.reshape(rows_dev, blocks, cols), "blk", split_axis=1, concat_axis=0, tiled=True
    ).reshape(seq, cols)
    d_proj_main = lax.all_gather(d_proj_main, "blk", axis=0, tiled=True)
    d_proj_all = jnp.dot(to_main.T, d_proj_main, preferred_element_type=f32).astype(bf16)

    whole_query, whole_key, whole_value = (qkv[:, i * width : (i + 1) * width] for i in range(3))
    outs, norms, weights = [], [], []
    for h in range(HEAD_GRP):
        c = slice(h * HD, (h + 1) * HD)
        scores = jnp.dot(ctrl_query[:, c], whole_key[:, c].T, preferred_element_type=f32) * score_scale
        peak = jnp.max(scores, axis=1, keepdims=True)
        log_norm = peak + jnp.log(jnp.sum(jnp.exp(scores - peak), axis=1, keepdims=True))
        p = jnp.exp(scores - log_norm)
        outs.append(jnp.dot(p.astype(bf16), whole_value[:, c], preferred_element_type=f32))
        norms.append(log_norm)
        weights.append(p)
    attended = jnp.concatenate(outs, axis=1).astype(bf16)
    norms = jnp.concatenate(norms, axis=1)
    attended_all = lax.all_gather(attended, "blk", axis=0, tiled=True)
    norms_all = lax.all_gather(norms, "blk", axis=0, tiled=True)

    attended_main = jnp.dot(to_main, attended_all, preferred_element_type=f32).astype(bf16)
    own_main = lax.dynamic_slice_in_dim(attended_main, me * rows_dev, rows_dev, 0)
    partial = jnp.dot(own_main, w_out, preferred_element_type=f32).astype(bf16)
    residual = lax.psum_scatter(partial, "grp", scatter_dimension=1, tiled=True)
    main_mixed = (main_hidden.astype(f32) + residual.astype(f32)).astype(bf16)
    d_w_out = jnp.dot(attended_main.T, grad_cols, preferred_element_type=f32)

    delta_all = jnp.sum(
        (d_proj_all.astype(f32) * attended_all.astype(f32)).reshape(seq, HEAD_GRP, HD), axis=2
    )
    d_proj = lax.dynamic_slice_in_dim(d_proj_all, me * rows_dev, rows_dev, 0)
    delta = lax.dynamic_slice_in_dim(delta_all, me * rows_dev, rows_dev, 0)
    dq, dk, dv = [], [], []
    for h in range(HEAD_GRP):
        c = slice(h * HD, (h + 1) * HD)
        d_probs = jnp.dot(d_proj[:, c], whole_value[:, c].T, preferred_element_type=f32)
        d_scores = (weights[h] * (d_probs - delta[:, h : h + 1])).astype(bf16)
        dq.append(jnp.dot(d_scores, whole_key[:, c], preferred_element_type=f32) * score_scale)
        scores = jnp.dot(whole_query[:, c], ctrl_key[:, c].T, preferred_element_type=f32) * score_scale
        p = jnp.exp(scores - norms_all[:, h : h + 1])
        d_probs = jnp.dot(d_proj_all[:, c], ctrl_value[:, c].T, preferred_element_type=f32)
        d_scores = (p * (d_probs - delta_all[:, h : h + 1])).astype(bf16)
        dk.append(jnp.dot(d_scores.T, whole_query[:, c], preferred_element_type=f32) * score_scale)
        dv.append(jnp.dot(p.astype(bf16).T, d_proj_all[:, c], preferred_element_type=f32))
    dq, dk, dv = (jnp.concatenate(x, axis=1).astype(bf16) for x in (dq, dk, dv))
    return main_mixed, dq, dk, dv, d_w_out


def solution(mesh):
    in_specs = (
        P("blk", "grp"),
        P("blk", "grp"),
        P("blk", "grp"),
        P("blk", "grp"),
        P("grp", None),
        P("blk", "grp"),
        P("blk"),
    )
    out_specs = (
        P("blk", "grp"),
        P("blk", "grp"),
        P("blk", "grp"),
        P("blk", "grp"),
        P("grp", "blk"),
    )
    body = on_device_small if mesh.shape["blk"] <= 8 else on_device
    return jax.shard_map(
        body, mesh=mesh, in_specs=in_specs, out_specs=out_specs, check_vma=False
    )
```

```python
import functools
import math

import jax
import jax.numpy as jnp
from jax import lax
from jax.experimental import pallas as pl
from jax.experimental.pallas import tpu as pltpu
from jax.sharding import PartitionSpec as P

HD = 128
HEAD_GRP = 3


def on_device(main_hidden, ctrl_query, ctrl_key, ctrl_value, w_out, d_mixed, control_slot):
    rows_dev = ctrl_query.shape[0]
    feature_cols = d_mixed.shape[1]
    blocks = lax.axis_size("blk")
    per_peer = rows_dev // blocks
    score_scale = 1.0 / math.sqrt(HD)
    whole_key, whole_value = (
        lax.all_gather(ctrl_key, "blk", axis=0, tiled=True),
        lax.all_gather(ctrl_value, "blk", axis=0, tiled=True),
    )
    outputs = []
    norm_list = []
    for head_idx in range(HEAD_GRP):
        columns = slice(head_idx * HD, (head_idx + 1) * HD)
        scores = (
            jnp.dot(
                ctrl_query[:, columns], whole_key[:, columns].T, preferred_element_type=jnp.float32
            )
            * score_scale
        )
        row_peak = jnp.max(scores, axis=1, keepdims=True)
        log_norm = row_peak + jnp.log(jnp.sum(jnp.exp(scores - row_peak), axis=1, keepdims=True))
        soft_weights = jnp.exp(scores - log_norm).astype(jnp.bfloat16)
        outputs.append(
            jnp.dot(soft_weights, whole_value[:, columns], preferred_element_type=jnp.float32)
        )
        norm_list.append(log_norm[:, 0])
    attended = jnp.concatenate(outputs, axis=1).astype(jnp.bfloat16)
    log_norms = jnp.stack(norm_list, axis=1)
    target = control_slot // rows_dev
    within = control_slot % rows_dev
    sort_order = jnp.argsort(target)
    inverse = jnp.argsort(sort_order)
    send_within = within[sort_order].reshape(blocks, per_peer)
    arrived, arrived_grad = (
        lax.all_to_all(send_within, "blk", split_axis=0, concat_axis=0, tiled=True),
        lax.all_to_all(
            d_mixed[sort_order].reshape(blocks, per_peer, feature_cols),
            "blk",
            split_axis=0,
            concat_axis=0,
            tiled=True,
        ),
    )
    placed = arrived.reshape(rows_dev)
    grad_rows = jnp.zeros_like(d_mixed).at[placed].set(arrived_grad.reshape(rows_dev, feature_cols))
    residual = lax.psum_scatter(
        jnp.dot(attended, w_out, preferred_element_type=jnp.float32).astype(jnp.bfloat16),
        "grp",
        scatter_dimension=1,
        tiled=True,
    ).astype(jnp.float32)
    returned = lax.all_to_all(
        residual[placed].reshape(blocks, per_peer, feature_cols),
        "blk",
        split_axis=0,
        concat_axis=0,
        tiled=True,
    )
    residual = returned.reshape(rows_dev, feature_cols)[inverse]
    main_mixed = (main_hidden.astype(jnp.float32) + residual).astype(jnp.bfloat16)
    grad_full = lax.all_gather(grad_rows, "grp", axis=1, tiled=True)
    d_proj = jnp.dot(grad_full, w_out.T, preferred_element_type=jnp.float32).astype(jnp.bfloat16)
    d_w_out = lax.psum_scatter(
        jnp.dot(attended.T, grad_full, preferred_element_type=jnp.float32),
        "blk",
        scatter_dimension=1,
        tiled=True,
    )
    row_delta = jnp.sum(
        (d_proj.astype(jnp.float32) * attended.astype(jnp.float32)).reshape(rows_dev, HEAD_GRP, HD),
        axis=2,
    )
    all_norms, all_delta = (
        lax.all_gather(log_norms, "blk", axis=0, tiled=True),
        lax.all_gather(row_delta, "blk", axis=0, tiled=True),
    )
    query_grads = []
    for head_idx in range(HEAD_GRP):
        columns = slice(head_idx * HD, (head_idx + 1) * HD)
        scores = (
            jnp.dot(
                ctrl_query[:, columns], whole_key[:, columns].T, preferred_element_type=jnp.float32
            )
            * score_scale
        )
        soft_weights = jnp.exp(scores - log_norms[:, head_idx : head_idx + 1])
        d_probs = jnp.dot(
            d_proj[:, columns], whole_value[:, columns].T, preferred_element_type=jnp.float32
        )
        d_scores = (soft_weights * (d_probs - row_delta[:, head_idx : head_idx + 1])).astype(
            jnp.bfloat16
        )
        query_grads.append(
            jnp.dot(d_scores, whole_key[:, columns], preferred_element_type=jnp.float32)
            * score_scale
        )
    d_query = jnp.concatenate(query_grads, axis=1).astype(jnp.bfloat16)
    query_piece = lax.all_gather(ctrl_query, "blk", axis=0, tiled=True)
    grad_piece = lax.all_gather(d_proj, "blk", axis=0, tiled=True)
    key_terms = []
    value_terms = []
    for head_idx in range(HEAD_GRP):
        columns = slice(head_idx * HD, (head_idx + 1) * HD)
        scores = (
            jnp.dot(
                query_piece[:, columns], ctrl_key[:, columns].T, preferred_element_type=jnp.float32
            )
            * score_scale
        )
        soft_weights = jnp.exp(scores - all_norms[:, head_idx : head_idx + 1])
        d_probs = jnp.dot(
            grad_piece[:, columns], ctrl_value[:, columns].T, preferred_element_type=jnp.float32
        )
        d_scores = (soft_weights * (d_probs - all_delta[:, head_idx : head_idx + 1])).astype(
            jnp.bfloat16
        )
        key_terms.append(
            jnp.dot(d_scores.T, query_piece[:, columns], preferred_element_type=jnp.float32)
            * score_scale
        )
        value_terms.append(
            jnp.dot(
                soft_weights.astype(jnp.bfloat16).T,
                grad_piece[:, columns],
                preferred_element_type=jnp.float32,
            )
        )
    key_grad = jnp.concatenate(key_terms, axis=1)
    value_grad = jnp.concatenate(value_terms, axis=1)
    return (
        main_mixed,
        d_query,
        key_grad.astype(jnp.bfloat16),
        value_grad.astype(jnp.bfloat16),
        d_w_out,
    )


F32, BF16 = jnp.float32, jnp.bfloat16


def dot(a, b, ca, cb):
    return lax.dot_general(a, b, (((ca,), (cb,)), ((), ())), preferred_element_type=F32)


def fused_kernel(
    hidden_ref, q_ref, k_ref, v_ref, w_ref, dm_ref, slot_ref,
    mixed_ref, dq_ref, dk_ref, dv_ref, dw_ref,
    dm_full, qkv_in, slots_in, dp_send, do_in, do_ctrl, d_cols,
    probs, place, att_ctrl, att_send, att_all, rs_send, rs_in,
    dk_acc, dv_acc, grad_send, grad_in,
    s_dm, s_qkv, s_slot, s_do, s_ca, s_cb, s_at, s_ag, s_rs, s_gr,
    r_dm, r_qkv, r_slot, r_do, r_ca, r_cb, r_at, r_ag, r_rs, r_gr,
):
    g = lax.axis_index("grp")
    b = lax.axis_index("blk")
    n_grp, blocks = dm_full.shape[0], qkv_in.shape[1]
    rows, feat = dm_ref.shape
    cols = d_cols.shape[3]
    quarter = rows // n_grp
    seq = rows * blocks
    chunks = 4
    per = blocks // chunks
    step = seq // chunks
    scale = 1.0 / math.sqrt(HD)
    c = g % 2
    z, x = b // 2, b % 2
    nz = blocks // 2
    mate = b + 1 - 2 * x
    owners = [2 + 2 * c, 5 - 2 * c, 7 * c]
    mine = jnp.where(b == owners[1], 1, jnp.where(b == owners[2], 2, 0))
    is_owner = (b == owners[0]) | (b == owners[1]) | (b == owners[2])
    pending = []

    def remote(src, dst, ss, rs, dev):
        return pltpu.make_async_remote_copy(
            src_ref=src, dst_ref=dst, send_sem=ss, recv_sem=rs,
            device_id=dev, device_id_type=pl.DeviceIdType.MESH,
        )

    def send(cond, make):
        pl.when(cond)(lambda: make().start())
        pending.append((cond, make))

    def arrive(cond, make):
        pl.when(cond)(lambda: make().wait_recv())

    barrier = pltpu.get_barrier_semaphore()
    for d in range(1, n_grp):
        pl.semaphore_signal(
            barrier, inc=1, device_id={"grp": (g + d) % n_grp}, device_id_type=pl.DeviceIdType.MESH
        )
    for d in range(1, blocks):
        pl.semaphore_signal(
            barrier, inc=1, device_id={"blk": (b + d) % blocks}, device_id_type=pl.DeviceIdType.MESH
        )
    pl.semaphore_wait(barrier, n_grp + blocks - 2)

    for p in range(n_grp):
        send(g != p, lambda p=p: remote(dm_ref, dm_full.at[g], s_dm.at[p], r_dm.at[g], {"grp": p}))
    for i, ref in enumerate((q_ref, k_ref, v_ref)):
        for h in range(HEAD_GRP):
            tile = (slice(None), slice(h * HD, (h + 1) * HD))
            send(
                b != owners[h],
                lambda i=i, ref=ref, h=h, tile=tile: remote(
                    ref.at[tile], qkv_in.at[i, b], s_qkv.at[i, h], r_qkv.at[i, b], {"blk": owners[h]}
                ),
            )

            @pl.when(b == owners[h])
            def _(i=i, ref=ref, tile=tile):
                qkv_in[i, b] = ref[tile]

    for h in range(HEAD_GRP):
        send(
            b != owners[h],
            lambda h=h: remote(
                slot_ref, slots_in.at[b], s_slot.at[h], r_slot.at[b], {"blk": owners[h]}
            ),
        )
    slots_in[b] = slot_ref[...]
    dm_full[g] = dm_ref[...]

    for p in range(n_grp):
        arrive(g != p, lambda p=p: remote(dm_ref, dm_full.at[p], s_dm.at[p], r_dm.at[p], {"grp": p}))
    d_proj = jnp.zeros((rows, HEAD_GRP * HD), F32)
    for p in range(n_grp):
        d_proj = d_proj + dot(dm_full[p], w_ref[:, p * feat : (p + 1) * feat], 1, 1)
    d_proj = d_proj.astype(BF16)
    for h in range(HEAD_GRP):
        dp_send[h] = d_proj[:, h * HD : (h + 1) * HD]
        send(
            b != owners[h],
            lambda h=h: remote(
                dp_send.at[h], do_in.at[b], s_do.at[h], r_do.at[b], {"blk": owners[h]}
            ),
        )

        @pl.when(b == owners[h])
        def _(h=h):
            do_in[b] = dp_send[h]

    my_rows = pl.ds(pl.multiple_of(g * quarter, quarter), quarter)
    for t in range(blocks):
        lo = t * cols
        view = (lo // feat, my_rows, slice(lo % feat, lo % feat + cols))
        send(
            b != t,
            lambda t=t, view=view: remote(
                dm_full.at[view], d_cols.at[g, b], s_ca.at[t], r_ca.at[b], {"blk": t}
            ),
        )

        @pl.when(b == t)
        def _(view=view):
            d_cols[g, b] = dm_full[view]

    @pl.when(is_owner)
    def _():
        for t in range(blocks):

            @pl.when(b != t)
            def _(t=t):
                remote(slot_ref, slots_in.at[t], s_slot.at[0], r_slot.at[t], {"blk": t}).wait_recv()
                for i in range(3):
                    remote(
                        qkv_in.at[i, t], qkv_in.at[i, t], s_qkv.at[i, 0], r_qkv.at[i, t], {"blk": t}
                    ).wait_recv()

        slot_row = jnp.concatenate([slots_in[t] for t in range(blocks)], axis=1)

        def forward(i, carry):
            qc = qkv_in[0, pl.ds(i * per, per)].reshape(step, HD)
            raw = dot(qc, qkv_in[1].reshape(seq, HD), 1, 1)
            peak = jnp.max(raw, axis=1, keepdims=True)
            e = jnp.exp2((raw - peak) * (scale * math.log2(math.e)))
            p = (e * (1.0 / jnp.sum(e, axis=1, keepdims=True))).astype(BF16)
            probs[i] = p
            att_ctrl[i] = dot(p, qkv_in[2].reshape(seq, HD), 1, 0).astype(BF16)
            at = lax.broadcasted_iota(jnp.int32, (step, seq), 0) + i * step
            place[i] = jnp.where(at == slot_row, 1.0, 0.0).astype(BF16)
            return carry

        lax.fori_loop(0, chunks, forward, 0)
        att_main = dot(place[...].reshape(seq, seq), att_ctrl[...].reshape(seq, HD), 0, 0)
        att_send[...] = att_main.astype(BF16).reshape(blocks, rows, HD)
        att_all[b, mine] = att_send[b]

    for t in range(blocks):
        send(
            is_owner & (b != t),
            lambda t=t: remote(
                att_send.at[t], att_all.at[t, mine], s_at.at[t], r_at.at[mine], {"blk": t}
            ),
        )

    for t in range(blocks):
        arrive(
            b != t,
            lambda t=t: remote(
                d_cols.at[g, t], d_cols.at[g, t], s_ca.at[t], r_ca.at[t], {"blk": t}
            ),
        )
    for p in range(n_grp):
        send(
            g != p,
            lambda p=p: remote(d_cols.at[g], d_cols.at[g], s_cb.at[p], r_cb.at[g], {"grp": p}),
        )

    for h in range(HEAD_GRP):
        arrive(
            b != owners[h],
            lambda h=h: remote(
                att_all.at[b, h], att_all.at[b, h], s_at.at[0], r_at.at[h], {"blk": owners[h]}
            ),
        )

    def pass_on(cond, slot, dev, sem):
        send(
            cond,
            lambda: remote(att_all.at[slot], att_all.at[slot], s_ag.at[sem], r_ag.at[slot], {"blk": dev}),
        )

    def landed(cond, slot):
        arrive(
            cond,
            lambda: remote(att_all.at[slot], att_all.at[slot], s_ag.at[0], r_ag.at[slot], {"blk": mate}),
        )

    always = b >= 0
    pass_on(z < nz - 1, b, b + 2, 0)
    pass_on(z > 0, b, b - 2, 1)
    pass_on(always, b, mate, 2)

    def gather_step(s):
        if s >= nz:
            return
        low, high = z >= s, z + s < nz
        landed(low, b - 2 * s)
        pass_on(low & (z < nz - 1), b - 2 * s, b + 2, 4 * s)
        pass_on(low, b - 2 * s, mate, 4 * s + 1)
        landed(high, b + 2 * s)
        pass_on(high & (z > 0), b + 2 * s, b - 2, 4 * s + 2)
        pass_on(high, b + 2 * s, mate, 4 * s + 3)

    own = jnp.concatenate([att_all[b, h] for h in range(HEAD_GRP)], axis=1)
    for p in range(n_grp):
        rs_send[p] = dot(own, w_ref[:, p * feat : (p + 1) * feat], 1, 0).astype(BF16)
        send(g != p, lambda p=p: remote(rs_send.at[p], rs_in.at[g], s_rs.at[p], r_rs.at[g], {"grp": p}))
    rs_in[g] = rs_send[g]

    for i in range(chunks):

        @pl.when(is_owner)
        def _(i=i):
            if i == 0:
                for t in range(blocks):

                    @pl.when(b != t)
                    def _(t=t):
                        remote(
                            do_in.at[t], do_in.at[t], s_do.at[0], r_do.at[t], {"blk": t}
                        ).wait_recv()

            do = dot(place[i], do_in[...].reshape(seq, HD), 1, 0)
            delta = jnp.sum(do * att_ctrl[i].astype(F32), axis=1, keepdims=True)
            do = do.astype(BF16)
            p = probs[i]
            d_probs = dot(do, qkv_in[2].reshape(seq, HD), 1, 1)
            ds = (p.astype(F32) * (d_probs - delta)).astype(BF16)
            dq = (dot(ds, qkv_in[1].reshape(seq, HD), 1, 0) * scale).astype(BF16)
            grad_send[0, pl.ds(i * per, per)] = dq.reshape(per, rows, HD)
            qc = qkv_in[0, pl.ds(i * per, per)].reshape(step, HD)
            dk = dot(ds, qc, 0, 0)
            dv = dot(p, do, 0, 0)
            if i == 0:
                dk_acc[...] = dk
                dv_acc[...] = dv
            elif i < chunks - 1:
                dk_acc[...] += dk
                dv_acc[...] += dv
            else:
                dk = ((dk_acc[...] + dk) * scale).astype(BF16)
                grad_send[1] = dk.reshape(blocks, rows, HD)
                grad_send[2] = (dv_acc[...] + dv).astype(BF16).reshape(blocks, rows, HD)

        for t in range(i * per, (i + 1) * per):
            send(
                is_owner & (b != t),
                lambda t=t: remote(
                    grad_send.at[0, t], grad_in.at[0, mine], s_gr.at[0, t], r_gr.at[0, mine], {"blk": t}
                ),
            )
        if i == chunks - 1:
            for n in (1, 2):
                for t in range(blocks):
                    send(
                        is_owner & (b != t),
                        lambda n=n, t=t: remote(
                            grad_send.at[n, t], grad_in.at[n, mine], s_gr.at[n, t],
                            r_gr.at[n, mine], {"blk": t},
                        ),
                    )
        gather_step(i + 1)

    @pl.when(is_owner)
    def _():
        for n in range(3):
            grad_in[n, mine] = grad_send[n, b]

    for p in range(n_grp):
        arrive(g != p, lambda p=p: remote(rs_in.at[p], rs_in.at[p], s_rs.at[p], r_rs.at[p], {"grp": p}))
    total = rs_in[0].astype(F32)
    for p in range(1, n_grp):
        total = total + rs_in[p].astype(F32)
    mixed_ref[...] = (hidden_ref[...].astype(F32) + total).astype(BF16)

    for p in range(n_grp):
        arrive(g != p, lambda p=p: remote(d_cols.at[p], d_cols.at[p], s_cb.at[p], r_cb.at[p], {"grp": p}))
    for j in range(nz):
        landed(always, 2 * j + 1 - x)
    grads = d_cols[...].reshape(seq, cols)
    for h in range(HEAD_GRP):
        att = jnp.concatenate(
            [
                att_all[:, h, p * quarter : (p + 1) * quarter, :].reshape(blocks * quarter, HD)
                for p in range(n_grp)
            ],
            axis=0,
        )
        dw_ref[h * HD : (h + 1) * HD, :] = dot(att, grads, 0, 0)

    for n, out in enumerate((dq_ref, dk_ref, dv_ref)):
        for h in range(HEAD_GRP):
            arrive(
                b != owners[h],
                lambda n=n, h=h: remote(
                    grad_in.at[n, h], grad_in.at[n, h], s_gr.at[n, 0], r_gr.at[n, h], {"blk": owners[h]}
                ),
            )
            out[:, h * HD : (h + 1) * HD] = grad_in[n, h]

    for cond, make in pending:
        pl.when(cond)(lambda make=make: make().wait_send())


def on_device_fused(main_hidden, ctrl_query, ctrl_key, ctrl_value, w_out, d_mixed, control_slot):
    n_grp, blocks = lax.axis_size("grp"), lax.axis_size("blk")
    rows, feat = d_mixed.shape
    width, model = w_out.shape
    cols = model // blocks
    seq = rows * blocks
    step = seq // 4
    dma = pltpu.SemaphoreType.DMA
    sems = [
        dma((n_grp,)), dma((3, HEAD_GRP)), dma((HEAD_GRP,)), dma((HEAD_GRP,)), dma((blocks,)),
        dma((n_grp,)), dma((blocks,)), dma((2 * blocks,)), dma((n_grp,)), dma((3, blocks)),
        dma((n_grp,)), dma((3, blocks)), dma((blocks,)), dma((blocks,)), dma((blocks,)),
        dma((n_grp,)), dma((HEAD_GRP,)), dma((blocks,)), dma((n_grp,)), dma((3, HEAD_GRP)),
    ]
    vmem = pl.BlockSpec(memory_space=pltpu.VMEM)
    tile = jax.ShapeDtypeStruct((rows, width), BF16)
    return pl.pallas_call(
        fused_kernel,
        out_shape=(
            jax.ShapeDtypeStruct((rows, feat), BF16), tile, tile, tile,
            jax.ShapeDtypeStruct((width, cols), F32),
        ),
        in_specs=[vmem] * 7,
        out_specs=[vmem] * 5,
        scratch_shapes=[
            pltpu.VMEM((n_grp, rows, feat), BF16),
            pltpu.VMEM((3, blocks, rows, HD), BF16),
            pltpu.VMEM((blocks, 1, rows), jnp.int32),
            pltpu.VMEM((HEAD_GRP, rows, HD), BF16),
            pltpu.VMEM((blocks, rows, HD), BF16),
            pltpu.VMEM((blocks, rows, HD), BF16),
            pltpu.VMEM((n_grp, blocks, rows // n_grp, cols), BF16),
            pltpu.VMEM((4, step, seq), BF16),
            pltpu.VMEM((4, step, seq), BF16),
            pltpu.VMEM((4, step, HD), BF16),
            pltpu.VMEM((blocks, rows, HD), BF16),
            pltpu.VMEM((blocks, HEAD_GRP, rows, HD), BF16),
            pltpu.VMEM((n_grp, rows, feat), BF16),
            pltpu.VMEM((n_grp, rows, feat), BF16),
            pltpu.VMEM((seq, HD), F32),
            pltpu.VMEM((seq, HD), F32),
            pltpu.VMEM((3, blocks, rows, HD), BF16),
            pltpu.VMEM((3, HEAD_GRP, rows, HD), BF16),
        ] + sems,
        compiler_params=pltpu.CompilerParams(
            collective_id=0, has_side_effects=True, vmem_limit_bytes=48 * 2**20
        ),
        cost_estimate=pl.CostEstimate(
            flops=2 * 5 * seq * seq * HD, bytes_accessed=16 * 2**20, transcendentals=seq * seq
        ),
    )(
        main_hidden, ctrl_query, ctrl_key, ctrl_value, w_out, d_mixed,
        control_slot.reshape(1, rows),
    )


def solution(mesh):
    in_specs = (
        P("blk", "grp"),
        P("blk", "grp"),
        P("blk", "grp"),
        P("blk", "grp"),
        P("grp", None),
        P("blk", "grp"),
        P("blk"),
    )
    out_specs = (
        P("blk", "grp"),
        P("blk", "grp"),
        P("blk", "grp"),
        P("blk", "grp"),
        P("grp", "blk"),
    )
    body = on_device_fused if mesh.shape["blk"] == 8 else on_device
    return jax.shard_map(
        body, mesh=mesh, in_specs=in_specs, out_specs=out_specs, check_vma=False
    )
```

```python
import functools
import math

import jax
import jax.numpy as jnp
from jax import lax
from jax.experimental import pallas as pl
from jax.experimental.pallas import tpu as pltpu
from jax.sharding import PartitionSpec as P

HD = 128
HEAD_GRP = 3


def on_device(main_hidden, ctrl_query, ctrl_key, ctrl_value, w_out, d_mixed, control_slot):
    rows_dev = ctrl_query.shape[0]
    feature_cols = d_mixed.shape[1]
    blocks = lax.axis_size("blk")
    per_peer = rows_dev // blocks
    score_scale = 1.0 / math.sqrt(HD)
    whole_key, whole_value = (
        lax.all_gather(ctrl_key, "blk", axis=0, tiled=True),
        lax.all_gather(ctrl_value, "blk", axis=0, tiled=True),
    )
    outputs = []
    norm_list = []
    for head_idx in range(HEAD_GRP):
        columns = slice(head_idx * HD, (head_idx + 1) * HD)
        scores = (
            jnp.dot(
                ctrl_query[:, columns], whole_key[:, columns].T, preferred_element_type=jnp.float32
            )
            * score_scale
        )
        row_peak = jnp.max(scores, axis=1, keepdims=True)
        log_norm = row_peak + jnp.log(jnp.sum(jnp.exp(scores - row_peak), axis=1, keepdims=True))
        soft_weights = jnp.exp(scores - log_norm).astype(jnp.bfloat16)
        outputs.append(
            jnp.dot(soft_weights, whole_value[:, columns], preferred_element_type=jnp.float32)
        )
        norm_list.append(log_norm[:, 0])
    attended = jnp.concatenate(outputs, axis=1).astype(jnp.bfloat16)
    log_norms = jnp.stack(norm_list, axis=1)
    target = control_slot // rows_dev
    within = control_slot % rows_dev
    sort_order = jnp.argsort(target)
    inverse = jnp.argsort(sort_order)
    send_within = within[sort_order].reshape(blocks, per_peer)
    arrived, arrived_grad = (
        lax.all_to_all(send_within, "blk", split_axis=0, concat_axis=0, tiled=True),
        lax.all_to_all(
            d_mixed[sort_order].reshape(blocks, per_peer, feature_cols),
            "blk",
            split_axis=0,
            concat_axis=0,
            tiled=True,
        ),
    )
    placed = arrived.reshape(rows_dev)
    grad_rows = jnp.zeros_like(d_mixed).at[placed].set(arrived_grad.reshape(rows_dev, feature_cols))
    residual = lax.psum_scatter(
        jnp.dot(attended, w_out, preferred_element_type=jnp.float32).astype(jnp.bfloat16),
        "grp",
        scatter_dimension=1,
        tiled=True,
    ).astype(jnp.float32)
    returned = lax.all_to_all(
        residual[placed].reshape(blocks, per_peer, feature_cols),
        "blk",
        split_axis=0,
        concat_axis=0,
        tiled=True,
    )
    residual = returned.reshape(rows_dev, feature_cols)[inverse]
    main_mixed = (main_hidden.astype(jnp.float32) + residual).astype(jnp.bfloat16)
    grad_full = lax.all_gather(grad_rows, "grp", axis=1, tiled=True)
    d_proj = jnp.dot(grad_full, w_out.T, preferred_element_type=jnp.float32).astype(jnp.bfloat16)
    d_w_out = lax.psum_scatter(
        jnp.dot(attended.T, grad_full, preferred_element_type=jnp.float32),
        "blk",
        scatter_dimension=1,
        tiled=True,
    )
    row_delta = jnp.sum(
        (d_proj.astype(jnp.float32) * attended.astype(jnp.float32)).reshape(rows_dev, HEAD_GRP, HD),
        axis=2,
    )
    all_norms, all_delta = (
        lax.all_gather(log_norms, "blk", axis=0, tiled=True),
        lax.all_gather(row_delta, "blk", axis=0, tiled=True),
    )
    query_grads = []
    for head_idx in range(HEAD_GRP):
        columns = slice(head_idx * HD, (head_idx + 1) * HD)
        scores = (
            jnp.dot(
                ctrl_query[:, columns], whole_key[:, columns].T, preferred_element_type=jnp.float32
            )
            * score_scale
        )
        soft_weights = jnp.exp(scores - log_norms[:, head_idx : head_idx + 1])
        d_probs = jnp.dot(
            d_proj[:, columns], whole_value[:, columns].T, preferred_element_type=jnp.float32
        )
        d_scores = (soft_weights * (d_probs - row_delta[:, head_idx : head_idx + 1])).astype(
            jnp.bfloat16
        )
        query_grads.append(
            jnp.dot(d_scores, whole_key[:, columns], preferred_element_type=jnp.float32)
            * score_scale
        )
    d_query = jnp.concatenate(query_grads, axis=1).astype(jnp.bfloat16)
    query_piece = lax.all_gather(ctrl_query, "blk", axis=0, tiled=True)
    grad_piece = lax.all_gather(d_proj, "blk", axis=0, tiled=True)
    key_terms = []
    value_terms = []
    for head_idx in range(HEAD_GRP):
        columns = slice(head_idx * HD, (head_idx + 1) * HD)
        scores = (
            jnp.dot(
                query_piece[:, columns], ctrl_key[:, columns].T, preferred_element_type=jnp.float32
            )
            * score_scale
        )
        soft_weights = jnp.exp(scores - all_norms[:, head_idx : head_idx + 1])
        d_probs = jnp.dot(
            grad_piece[:, columns], ctrl_value[:, columns].T, preferred_element_type=jnp.float32
        )
        d_scores = (soft_weights * (d_probs - all_delta[:, head_idx : head_idx + 1])).astype(
            jnp.bfloat16
        )
        key_terms.append(
            jnp.dot(d_scores.T, query_piece[:, columns], preferred_element_type=jnp.float32)
            * score_scale
        )
        value_terms.append(
            jnp.dot(
                soft_weights.astype(jnp.bfloat16).T,
                grad_piece[:, columns],
                preferred_element_type=jnp.float32,
            )
        )
    key_grad = jnp.concatenate(key_terms, axis=1)
    value_grad = jnp.concatenate(value_terms, axis=1)
    return (
        main_mixed,
        d_query,
        key_grad.astype(jnp.bfloat16),
        value_grad.astype(jnp.bfloat16),
        d_w_out,
    )


F32, BF16 = jnp.float32, jnp.bfloat16


def dot(a, b, ca, cb):
    return lax.dot_general(a, b, (((ca,), (cb,)), ((), ())), preferred_element_type=F32)


def fused_kernel(
    hidden_hbm, q_ref, k_ref, v_ref, w_hbm, dm_ref, slot_ref,
    mixed_out, dq_out, dk_out, dv_out, dw_out, mixed_ref, dw_ref, hidden_ref, w_ref,
    dm_full, qkv_in, slots_in, dp_send, do_in, do_ctrl, d_cols,
    probs, place, att_ctrl, att_send, att_all, rs_send, rs_in,
    dk_acc, dv_acc, grad_send, grad_in,
    s_dm, s_qkv, s_slot, s_do, s_ca, s_cb, s_at, s_ag, s_rs, s_gr, s_in, s_out,
    r_dm, r_qkv, r_slot, r_do, r_ca, r_cb, r_at, r_ag, r_rs, r_gr,
):
    g = lax.axis_index("grp")
    b = lax.axis_index("blk")
    n_grp, blocks = dm_full.shape[0], qkv_in.shape[1]
    rows, feat = dm_ref.shape
    cols = d_cols.shape[3]
    quarter = rows // n_grp
    seq = rows * blocks
    chunks = 4
    per = blocks // chunks
    step = seq // chunks
    scale = 1.0 / math.sqrt(HD)
    c = g % 2
    z, x = b // 2, b % 2
    nz = blocks // 2
    mate = b + 1 - 2 * x
    owners = [2 + 2 * c, 5 - 2 * c, 7 * c]
    mine = jnp.where(b == owners[1], 1, jnp.where(b == owners[2], 2, 0))
    is_owner = (b == owners[0]) | (b == owners[1]) | (b == owners[2])
    pending = []
    writes = []

    def write(src, dst):
        copy = pltpu.make_async_copy(src, dst, s_out.at[len(writes)])
        copy.start()
        writes.append(copy)

    def remote(src, dst, ss, rs, dev):
        return pltpu.make_async_remote_copy(
            src_ref=src, dst_ref=dst, send_sem=ss, recv_sem=rs,
            device_id=dev, device_id_type=pl.DeviceIdType.MESH,
        )

    def send(cond, make):
        pl.when(cond)(lambda: make().start())
        pending.append((cond, make))

    def arrive(cond, make):
        pl.when(cond)(lambda: make().wait_recv())

    loads = [
        pltpu.make_async_copy(dm_ref, dm_full.at[g], s_in.at[0]),
        pltpu.make_async_copy(w_hbm, w_ref, s_in.at[1]),
        pltpu.make_async_copy(slot_ref, slots_in.at[b], s_in.at[2]),
        pltpu.make_async_copy(hidden_hbm, hidden_ref, s_in.at[3]),
    ]
    for load in loads:
        load.start()

    def own_tile(i, ref, tile):
        return pltpu.make_async_copy(ref.at[tile], qkv_in.at[i, b], s_in.at[4 + i])

    barrier = pltpu.get_barrier_semaphore()
    for d in range(1, n_grp):
        pl.semaphore_signal(
            barrier, inc=1, device_id={"grp": (g + d) % n_grp}, device_id_type=pl.DeviceIdType.MESH
        )
    for d in range(1, blocks):
        pl.semaphore_signal(
            barrier, inc=1, device_id={"blk": (b + d) % blocks}, device_id_type=pl.DeviceIdType.MESH
        )
    pl.semaphore_wait(barrier, n_grp + blocks - 2)

    for p in range(n_grp):
        send(g != p, lambda p=p: remote(dm_ref, dm_full.at[g], s_dm.at[p], r_dm.at[g], {"grp": p}))
    for i, ref in enumerate((q_ref, k_ref, v_ref)):
        for h in range(HEAD_GRP):
            tile = (slice(None), slice(h * HD, (h + 1) * HD))
            send(
                b != owners[h],
                lambda i=i, ref=ref, h=h, tile=tile: remote(
                    ref.at[tile], qkv_in.at[i, b], s_qkv.at[i, h], r_qkv.at[i, b], {"blk": owners[h]}
                ),
            )

            @pl.when(b == owners[h])
            def _(i=i, ref=ref, tile=tile):
                own_tile(i, ref, tile).start()

    for h in range(HEAD_GRP):
        send(
            b != owners[h],
            lambda h=h: remote(
                slot_ref, slots_in.at[b], s_slot.at[h], r_slot.at[b], {"blk": owners[h]}
            ),
        )

    for p in range(n_grp):
        arrive(g != p, lambda p=p: remote(dm_ref, dm_full.at[p], s_dm.at[p], r_dm.at[p], {"grp": p}))
    loads[0].wait()
    loads[1].wait()
    d_proj = jnp.zeros((rows, HEAD_GRP * HD), F32)
    for p in range(n_grp):
        d_proj = d_proj + dot(dm_full[p], w_ref[:, p * feat : (p + 1) * feat], 1, 1)
    d_proj = d_proj.astype(BF16)
    for h in range(HEAD_GRP):
        dp_send[h] = d_proj[:, h * HD : (h + 1) * HD]
        send(
            b != owners[h],
            lambda h=h: remote(
                dp_send.at[h], do_in.at[b], s_do.at[h], r_do.at[b], {"blk": owners[h]}
            ),
        )

        @pl.when(b == owners[h])
        def _(h=h):
            do_in[b] = dp_send[h]

    my_rows = pl.ds(pl.multiple_of(g * quarter, quarter), quarter)
    for t in range(blocks):
        lo = t * cols
        view = (lo // feat, my_rows, slice(lo % feat, lo % feat + cols))
        send(
            b != t,
            lambda t=t, view=view: remote(
                dm_full.at[view], d_cols.at[g, b], s_ca.at[t], r_ca.at[b], {"blk": t}
            ),
        )

        @pl.when(b == t)
        def _(view=view):
            d_cols[g, b] = dm_full[view]

    loads[2].wait()

    @pl.when(is_owner)
    def _():
        for t in range(blocks):

            @pl.when(b != t)
            def _(t=t):
                remote(slot_ref, slots_in.at[t], s_slot.at[0], r_slot.at[t], {"blk": t}).wait_recv()
                for i in range(3):
                    remote(
                        qkv_in.at[i, t], qkv_in.at[i, t], s_qkv.at[i, 0], r_qkv.at[i, t], {"blk": t}
                    ).wait_recv()

        for i, ref in enumerate((q_ref, k_ref, v_ref)):
            own_tile(i, ref, (slice(None), slice(0, HD))).wait()

        slot_row = jnp.concatenate([slots_in[t] for t in range(blocks)], axis=1)

        def forward(i, carry):
            qc = qkv_in[0, pl.ds(i * per, per)].reshape(step, HD)
            raw = dot(qc, qkv_in[1].reshape(seq, HD), 1, 1)
            peak = jnp.max(raw, axis=1, keepdims=True)
            e = jnp.exp2((raw - peak) * (scale * math.log2(math.e)))
            p = (e * (1.0 / jnp.sum(e, axis=1, keepdims=True))).astype(BF16)
            probs[i] = p
            att_ctrl[i] = dot(p, qkv_in[2].reshape(seq, HD), 1, 0).astype(BF16)
            at = lax.broadcasted_iota(jnp.int32, (step, seq), 0) + i * step
            place[i] = jnp.where(at == slot_row, 1.0, 0.0).astype(BF16)
            return carry

        lax.fori_loop(0, chunks, forward, 0)
        att_main = dot(place[...].reshape(seq, seq), att_ctrl[...].reshape(seq, HD), 0, 0)
        att_send[...] = att_main.astype(BF16).reshape(blocks, rows, HD)
        att_all[b, mine] = att_send[b]

    for t in range(blocks):
        send(
            is_owner & (b != t),
            lambda t=t: remote(
                att_send.at[t], att_all.at[t, mine], s_at.at[t], r_at.at[mine], {"blk": t}
            ),
        )

    for t in range(blocks):
        arrive(
            b != t,
            lambda t=t: remote(
                d_cols.at[g, t], d_cols.at[g, t], s_ca.at[t], r_ca.at[t], {"blk": t}
            ),
        )
    for p in range(n_grp):
        send(
            g != p,
            lambda p=p: remote(d_cols.at[g], d_cols.at[g], s_cb.at[p], r_cb.at[g], {"grp": p}),
        )

    for h in range(HEAD_GRP):
        arrive(
            b != owners[h],
            lambda h=h: remote(
                att_all.at[b, h], att_all.at[b, h], s_at.at[0], r_at.at[h], {"blk": owners[h]}
            ),
        )

    def pass_on(cond, slot, dev, sem):
        send(
            cond,
            lambda: remote(att_all.at[slot], att_all.at[slot], s_ag.at[sem], r_ag.at[slot], {"blk": dev}),
        )

    def landed(cond, slot):
        arrive(
            cond,
            lambda: remote(att_all.at[slot], att_all.at[slot], s_ag.at[0], r_ag.at[slot], {"blk": mate}),
        )

    always = b >= 0
    pass_on(z < nz - 1, b, b + 2, 0)
    pass_on(z > 0, b, b - 2, 1)
    pass_on(always, b, mate, 2)

    def gather_step(s):
        if s >= nz:
            return
        low, high = z >= s, z + s < nz
        landed(low, b - 2 * s)
        pass_on(low & (z < nz - 1), b - 2 * s, b + 2, 4 * s)
        pass_on(low, b - 2 * s, mate, 4 * s + 1)
        landed(high, b + 2 * s)
        pass_on(high & (z > 0), b + 2 * s, b - 2, 4 * s + 2)
        pass_on(high, b + 2 * s, mate, 4 * s + 3)

    own = jnp.concatenate([att_all[b, h] for h in range(HEAD_GRP)], axis=1)
    for p in range(n_grp):
        rs_send[p] = dot(own, w_ref[:, p * feat : (p + 1) * feat], 1, 0).astype(BF16)
        send(g != p, lambda p=p: remote(rs_send.at[p], rs_in.at[g], s_rs.at[p], r_rs.at[g], {"grp": p}))
    rs_in[g] = rs_send[g]

    for i in range(chunks):

        @pl.when(is_owner)
        def _(i=i):
            if i == 0:
                for t in range(blocks):

                    @pl.when(b != t)
                    def _(t=t):
                        remote(
                            do_in.at[t], do_in.at[t], s_do.at[0], r_do.at[t], {"blk": t}
                        ).wait_recv()

            do = dot(place[i], do_in[...].reshape(seq, HD), 1, 0)
            delta = jnp.sum(do * att_ctrl[i].astype(F32), axis=1, keepdims=True)
            do = do.astype(BF16)
            p = probs[i]
            d_probs = dot(do, qkv_in[2].reshape(seq, HD), 1, 1)
            ds = (p.astype(F32) * (d_probs - delta)).astype(BF16)
            dq = (dot(ds, qkv_in[1].reshape(seq, HD), 1, 0) * scale).astype(BF16)
            grad_send[0, pl.ds(i * per, per)] = dq.reshape(per, rows, HD)
            qc = qkv_in[0, pl.ds(i * per, per)].reshape(step, HD)
            dk = dot(ds, qc, 0, 0)
            dv = dot(p, do, 0, 0)
            if i == 0:
                dk_acc[...] = dk
                dv_acc[...] = dv
            elif i < chunks - 1:
                dk_acc[...] += dk
                dv_acc[...] += dv
            else:
                dk = ((dk_acc[...] + dk) * scale).astype(BF16)
                grad_send[1] = dk.reshape(blocks, rows, HD)
                grad_send[2] = (dv_acc[...] + dv).astype(BF16).reshape(blocks, rows, HD)

        for t in range(i * per, (i + 1) * per):
            send(
                is_owner & (b != t),
                lambda t=t: remote(
                    grad_send.at[0, t], grad_in.at[0, mine], s_gr.at[0, t], r_gr.at[0, mine], {"blk": t}
                ),
            )
        if i == chunks - 1:
            for n in (1, 2):
                for t in range(blocks):
                    send(
                        is_owner & (b != t),
                        lambda n=n, t=t: remote(
                            grad_send.at[n, t], grad_in.at[n, mine], s_gr.at[n, t],
                            r_gr.at[n, mine], {"blk": t},
                        ),
                    )
        gather_step(i + 1)

    @pl.when(is_owner)
    def _():
        for n in range(3):
            grad_in[n, mine] = grad_send[n, b]

    for p in range(n_grp):
        arrive(g != p, lambda p=p: remote(rs_in.at[p], rs_in.at[p], s_rs.at[p], r_rs.at[p], {"grp": p}))
    loads[3].wait()
    total = rs_in[0].astype(F32)
    for p in range(1, n_grp):
        total = total + rs_in[p].astype(F32)
    mixed_ref[...] = (hidden_ref[...].astype(F32) + total).astype(BF16)
    write(mixed_ref, mixed_out)

    for p in range(n_grp):
        arrive(g != p, lambda p=p: remote(d_cols.at[p], d_cols.at[p], s_cb.at[p], r_cb.at[p], {"grp": p}))
    for j in range(nz):
        landed(always, 2 * j + 1 - x)
    grads = d_cols[...].reshape(seq, cols)
    for h in range(HEAD_GRP):
        att = jnp.concatenate(
            [
                att_all[:, h, p * quarter : (p + 1) * quarter, :].reshape(blocks * quarter, HD)
                for p in range(n_grp)
            ],
            axis=0,
        )
        dw_ref[h] = dot(att, grads, 0, 0)
        write(dw_ref.at[h], dw_out.at[h * HD : (h + 1) * HD])

    for n, out in enumerate((dq_out, dk_out, dv_out)):
        for h in range(HEAD_GRP):
            arrive(
                b != owners[h],
                lambda n=n, h=h: remote(
                    grad_in.at[n, h], grad_in.at[n, h], s_gr.at[n, 0], r_gr.at[n, h], {"blk": owners[h]}
                ),
            )
            write(grad_in.at[n, h], out.at[:, h * HD : (h + 1) * HD])

    for copy in writes:
        copy.wait()
    for cond, make in pending:
        pl.when(cond)(lambda make=make: make().wait_send())


def write_kernel(*refs):
    sems = refs[10]
    copies = [pltpu.make_async_copy(refs[i], refs[5 + i], sems.at[i]) for i in range(5)]
    for copy in copies:
        copy.start()
    for copy in copies:
        copy.wait()


def on_device_fused(main_hidden, ctrl_query, ctrl_key, ctrl_value, w_out, d_mixed, control_slot):
    n_grp, blocks = lax.axis_size("grp"), lax.axis_size("blk")
    rows, feat = d_mixed.shape
    width, model = w_out.shape
    cols = model // blocks
    seq = rows * blocks
    step = seq // 4
    dma = pltpu.SemaphoreType.DMA
    sems = [
        dma((n_grp,)), dma((3, HEAD_GRP)), dma((HEAD_GRP,)), dma((HEAD_GRP,)), dma((blocks,)),
        dma((n_grp,)), dma((blocks,)), dma((2 * blocks,)), dma((n_grp,)), dma((3, blocks)), dma((7,)), dma((16,)),
        dma((n_grp,)), dma((3, blocks)), dma((blocks,)), dma((blocks,)), dma((blocks,)),
        dma((n_grp,)), dma((HEAD_GRP,)), dma((blocks,)), dma((n_grp,)), dma((3, HEAD_GRP)),
    ]
    hbm = pl.BlockSpec(memory_space=pltpu.HBM)
    tile = jax.ShapeDtypeStruct((rows, width), BF16)
    results = pl.pallas_call(
        fused_kernel,
        out_shape=(
            jax.ShapeDtypeStruct((rows, feat), BF16), tile, tile, tile,
            jax.ShapeDtypeStruct((width, cols), F32),
        ),
        in_specs=[hbm] * 7,
        out_specs=[hbm] * 5,
        scratch_shapes=[
            pltpu.VMEM((rows, feat), BF16),
            pltpu.VMEM((HEAD_GRP, HD, cols), F32),
            pltpu.VMEM((rows, feat), BF16),
            pltpu.VMEM((width, model), BF16),
            pltpu.VMEM((n_grp, rows, feat), BF16),
            pltpu.VMEM((3, blocks, rows, HD), BF16),
            pltpu.VMEM((blocks, 1, rows), jnp.int32),
            pltpu.VMEM((HEAD_GRP, rows, HD), BF16),
            pltpu.VMEM((blocks, rows, HD), BF16),
            pltpu.VMEM((blocks, rows, HD), BF16),
            pltpu.VMEM((n_grp, blocks, rows // n_grp, cols), BF16),
            pltpu.VMEM((4, step, seq), BF16),
            pltpu.VMEM((4, step, seq), BF16),
            pltpu.VMEM((4, step, HD), BF16),
            pltpu.VMEM((blocks, rows, HD), BF16),
            pltpu.VMEM((blocks, HEAD_GRP, rows, HD), BF16),
            pltpu.VMEM((n_grp, rows, feat), BF16),
            pltpu.VMEM((n_grp, rows, feat), BF16),
            pltpu.VMEM((seq, HD), F32),
            pltpu.VMEM((seq, HD), F32),
            pltpu.VMEM((3, blocks, rows, HD), BF16),
            pltpu.VMEM((3, HEAD_GRP, rows, HD), BF16),
        ] + sems,
        compiler_params=pltpu.CompilerParams(
            collective_id=0, has_side_effects=True, vmem_limit_bytes=60 * 2**20
        ),
        cost_estimate=pl.CostEstimate(
            flops=2 * 5 * seq * seq * HD, bytes_accessed=16 * 2**20, transcendentals=seq * seq
        ),
    )(
        main_hidden, ctrl_query, ctrl_key, ctrl_value, w_out, d_mixed,
        control_slot.reshape(1, rows),
    )
    return pl.pallas_call(
        write_kernel,
        out_shape=tuple(jax.ShapeDtypeStruct(r.shape, r.dtype) for r in results),
        in_specs=[hbm] * 5,
        out_specs=[hbm] * 5,
        scratch_shapes=[dma((5,))],
        compiler_params=pltpu.CompilerParams(vmem_limit_bytes=60 * 2**20),
    )(*results)


def solution(mesh):
    in_specs = (
        P("blk", "grp"),
        P("blk", "grp"),
        P("blk", "grp"),
        P("blk", "grp"),
        P("grp", None),
        P("blk", "grp"),
        P("blk"),
    )
    out_specs = (
        P("blk", "grp"),
        P("blk", "grp"),
        P("blk", "grp"),
        P("blk", "grp"),
        P("grp", "blk"),
    )
    body = on_device_fused if mesh.shape["blk"] == 8 else on_device
    return jax.shard_map(
        body, mesh=mesh, in_specs=in_specs, out_specs=out_specs, check_vma=False
    )
```

```python
import functools
import math

import jax
import jax.numpy as jnp
from jax import lax
from jax.experimental import pallas as pl
from jax.experimental.pallas import tpu as pltpu
from jax.sharding import PartitionSpec as P

HD = 128
HEAD_GRP = 3


def on_device(main_hidden, ctrl_query, ctrl_key, ctrl_value, w_out, d_mixed, control_slot):
    rows_dev = ctrl_query.shape[0]
    feature_cols = d_mixed.shape[1]
    blocks = lax.axis_size("blk")
    per_peer = rows_dev // blocks
    score_scale = 1.0 / math.sqrt(HD)
    whole_key, whole_value = (
        lax.all_gather(ctrl_key, "blk", axis=0, tiled=True),
        lax.all_gather(ctrl_value, "blk", axis=0, tiled=True),
    )
    outputs = []
    norm_list = []
    for head_idx in range(HEAD_GRP):
        columns = slice(head_idx * HD, (head_idx + 1) * HD)
        scores = (
            jnp.dot(
                ctrl_query[:, columns], whole_key[:, columns].T, preferred_element_type=jnp.float32
            )
            * score_scale
        )
        row_peak = jnp.max(scores, axis=1, keepdims=True)
        log_norm = row_peak + jnp.log(jnp.sum(jnp.exp(scores - row_peak), axis=1, keepdims=True))
        soft_weights = jnp.exp(scores - log_norm).astype(jnp.bfloat16)
        outputs.append(
            jnp.dot(soft_weights, whole_value[:, columns], preferred_element_type=jnp.float32)
        )
        norm_list.append(log_norm[:, 0])
    attended = jnp.concatenate(outputs, axis=1).astype(jnp.bfloat16)
    log_norms = jnp.stack(norm_list, axis=1)
    target = control_slot // rows_dev
    within = control_slot % rows_dev
    sort_order = jnp.argsort(target)
    inverse = jnp.argsort(sort_order)
    send_within = within[sort_order].reshape(blocks, per_peer)
    arrived, arrived_grad = (
        lax.all_to_all(send_within, "blk", split_axis=0, concat_axis=0, tiled=True),
        lax.all_to_all(
            d_mixed[sort_order].reshape(blocks, per_peer, feature_cols),
            "blk",
            split_axis=0,
            concat_axis=0,
            tiled=True,
        ),
    )
    placed = arrived.reshape(rows_dev)
    grad_rows = jnp.zeros_like(d_mixed).at[placed].set(arrived_grad.reshape(rows_dev, feature_cols))
    residual = lax.psum_scatter(
        jnp.dot(attended, w_out, preferred_element_type=jnp.float32).astype(jnp.bfloat16),
        "grp",
        scatter_dimension=1,
        tiled=True,
    ).astype(jnp.float32)
    returned = lax.all_to_all(
        residual[placed].reshape(blocks, per_peer, feature_cols),
        "blk",
        split_axis=0,
        concat_axis=0,
        tiled=True,
    )
    residual = returned.reshape(rows_dev, feature_cols)[inverse]
    main_mixed = (main_hidden.astype(jnp.float32) + residual).astype(jnp.bfloat16)
    grad_full = lax.all_gather(grad_rows, "grp", axis=1, tiled=True)
    d_proj = jnp.dot(grad_full, w_out.T, preferred_element_type=jnp.float32).astype(jnp.bfloat16)
    d_w_out = lax.psum_scatter(
        jnp.dot(attended.T, grad_full, preferred_element_type=jnp.float32),
        "blk",
        scatter_dimension=1,
        tiled=True,
    )
    row_delta = jnp.sum(
        (d_proj.astype(jnp.float32) * attended.astype(jnp.float32)).reshape(rows_dev, HEAD_GRP, HD),
        axis=2,
    )
    all_norms, all_delta = (
        lax.all_gather(log_norms, "blk", axis=0, tiled=True),
        lax.all_gather(row_delta, "blk", axis=0, tiled=True),
    )
    query_grads = []
    for head_idx in range(HEAD_GRP):
        columns = slice(head_idx * HD, (head_idx + 1) * HD)
        scores = (
            jnp.dot(
                ctrl_query[:, columns], whole_key[:, columns].T, preferred_element_type=jnp.float32
            )
            * score_scale
        )
        soft_weights = jnp.exp(scores - log_norms[:, head_idx : head_idx + 1])
        d_probs = jnp.dot(
            d_proj[:, columns], whole_value[:, columns].T, preferred_element_type=jnp.float32
        )
        d_scores = (soft_weights * (d_probs - row_delta[:, head_idx : head_idx + 1])).astype(
            jnp.bfloat16
        )
        query_grads.append(
            jnp.dot(d_scores, whole_key[:, columns], preferred_element_type=jnp.float32)
            * score_scale
        )
    d_query = jnp.concatenate(query_grads, axis=1).astype(jnp.bfloat16)
    query_piece = lax.all_gather(ctrl_query, "blk", axis=0, tiled=True)
    grad_piece = lax.all_gather(d_proj, "blk", axis=0, tiled=True)
    key_terms = []
    value_terms = []
    for head_idx in range(HEAD_GRP):
        columns = slice(head_idx * HD, (head_idx + 1) * HD)
        scores = (
            jnp.dot(
                query_piece[:, columns], ctrl_key[:, columns].T, preferred_element_type=jnp.float32
            )
            * score_scale
        )
        soft_weights = jnp.exp(scores - all_norms[:, head_idx : head_idx + 1])
        d_probs = jnp.dot(
            grad_piece[:, columns], ctrl_value[:, columns].T, preferred_element_type=jnp.float32
        )
        d_scores = (soft_weights * (d_probs - all_delta[:, head_idx : head_idx + 1])).astype(
            jnp.bfloat16
        )
        key_terms.append(
            jnp.dot(d_scores.T, query_piece[:, columns], preferred_element_type=jnp.float32)
            * score_scale
        )
        value_terms.append(
            jnp.dot(
                soft_weights.astype(jnp.bfloat16).T,
                grad_piece[:, columns],
                preferred_element_type=jnp.float32,
            )
        )
    key_grad = jnp.concatenate(key_terms, axis=1)
    value_grad = jnp.concatenate(value_terms, axis=1)
    return (
        main_mixed,
        d_query,
        key_grad.astype(jnp.bfloat16),
        value_grad.astype(jnp.bfloat16),
        d_w_out,
    )


F32, BF16 = jnp.float32, jnp.bfloat16


def dot(a, b, ca, cb):
    return lax.dot_general(a, b, (((ca,), (cb,)), ((), ())), preferred_element_type=F32)


def fused_kernel(
    hidden_hbm, q_ref, k_ref, v_ref, w_hbm, dm_ref, slot_ref,
    mixed_out, dq_out, dk_out, dv_out, dw_out, mixed_ref, dw_ref, hidden_ref, w_ref,
    dm_full, qkv_in, slots_in, dp_send, do_in, q_main, d_cols,
    probs, place, place_t, dq_main, att_send, att_all, rs_send, rs_pass, rs_in,
    dk_acc, dv_acc, grad_send, grad_in,
    s_dm, s_qkv, s_slot, s_do, s_ca, s_cb, s_at, s_ag, s_rs, s_gr, s_in, s_out,
    r_dm, r_qkv, r_slot, r_do, r_ca, r_cb, r_at, r_ag, r_rs, r_gr,
):
    g = lax.axis_index("grp")
    b = lax.axis_index("blk")
    n_grp, blocks = dm_full.shape[0], qkv_in.shape[1]
    rows, feat = dm_ref.shape
    cols = d_cols.shape[3]
    quarter = rows // n_grp
    seq = rows * blocks
    chunks = 4
    per = blocks // chunks
    step = seq // chunks
    scale = 1.0 / math.sqrt(HD)
    c = g % 2
    z, x = b // 2, b % 2
    nz = blocks // 2
    mate = b + 1 - 2 * x
    core_mate, y_mate, diagonal = g + 1 - 2 * c, (g + 2) % n_grp, n_grp - 1 - g
    owners = [2 + 2 * c, 5 - 2 * c, 7 * c]
    mine = jnp.where(b == owners[1], 1, jnp.where(b == owners[2], 2, 0))
    is_owner = (b == owners[0]) | (b == owners[1]) | (b == owners[2])
    always = b >= 0
    pending = []
    writes = []

    def write(src, dst):
        copy = pltpu.make_async_copy(src, dst, s_out.at[len(writes)])
        copy.start()
        writes.append(copy)

    def remote(src, dst, ss, rs, dev):
        return pltpu.make_async_remote_copy(
            src_ref=src, dst_ref=dst, send_sem=ss, recv_sem=rs,
            device_id=dev, device_id_type=pl.DeviceIdType.MESH,
        )

    def send(cond, make):
        pl.when(cond)(lambda: make().start())
        pending.append((cond, make))

    def arrive(cond, make):
        pl.when(cond)(lambda: make().wait_recv())

    loads = [
        pltpu.make_async_copy(dm_ref, dm_full.at[g], s_in.at[0]),
        pltpu.make_async_copy(w_hbm, w_ref, s_in.at[1]),
        pltpu.make_async_copy(slot_ref, slots_in.at[b], s_in.at[2]),
        pltpu.make_async_copy(hidden_hbm, hidden_ref, s_in.at[3]),
    ]
    for load in loads:
        load.start()

    def own_tile(i, ref, tile):
        return pltpu.make_async_copy(ref.at[tile], qkv_in.at[i, b], s_in.at[4 + i])

    barrier = pltpu.get_barrier_semaphore()
    for d in range(1, n_grp):
        pl.semaphore_signal(
            barrier, inc=1, device_id={"grp": (g + d) % n_grp}, device_id_type=pl.DeviceIdType.MESH
        )
    for d in range(1, blocks):
        pl.semaphore_signal(
            barrier, inc=1, device_id={"blk": (b + d) % blocks}, device_id_type=pl.DeviceIdType.MESH
        )
    pl.semaphore_wait(barrier, n_grp + blocks - 2)

    def relay(src, buf, slot, dev, ss, rs):
        send(always, lambda: remote(src, buf.at[slot], ss, rs.at[slot], {"grp": dev}))

    def relayed(buf, slot, ss, rs):
        arrive(always, lambda: remote(buf.at[slot], buf.at[slot], ss.at[0], rs.at[slot], {"grp": y_mate}))

    relay(dm_ref, dm_full, g, y_mate, s_dm.at[0], r_dm)
    relay(dm_ref, dm_full, g, core_mate, s_dm.at[1], r_dm)
    for i, ref in enumerate((q_ref, k_ref, v_ref)):
        for h in range(HEAD_GRP):
            tile = (slice(None), slice(h * HD, (h + 1) * HD))
            send(
                b != owners[h],
                lambda i=i, ref=ref, h=h, tile=tile: remote(
                    ref.at[tile], qkv_in.at[i, b], s_qkv.at[i, h], r_qkv.at[i, b], {"blk": owners[h]}
                ),
            )

            @pl.when(b == owners[h])
            def _(i=i, ref=ref, tile=tile):
                own_tile(i, ref, tile).start()

    for h in range(HEAD_GRP):
        send(
            b != owners[h],
            lambda h=h: remote(
                slot_ref, slots_in.at[b], s_slot.at[h], r_slot.at[b], {"blk": owners[h]}
            ),
        )

    loads[2].wait()

    @pl.when(is_owner)
    def _():
        for t in range(blocks):

            @pl.when(b != t)
            def _(t=t):
                remote(slot_ref, slots_in.at[t], s_slot.at[0], r_slot.at[t], {"blk": t}).wait_recv()

        slot_row = jnp.concatenate([slots_in[t] for t in range(blocks)], axis=1)
        slot_col = jnp.transpose(jnp.broadcast_to(slot_row.astype(F32), (8, seq)))[:, :1]
        lane = lax.broadcasted_iota(jnp.int32, (step, seq), 1)
        for i in range(chunks):
            at = lax.broadcasted_iota(jnp.int32, (step, seq), 0) + i * step
            place[i] = jnp.where(at == slot_row, 1.0, 0.0).astype(BF16)
            want = slot_col[i * step : (i + 1) * step].astype(jnp.int32)
            place_t[i] = jnp.where(lane == want, 1.0, 0.0).astype(BF16)

    def features(p):
        lo = pl.multiple_of(p * feat, HD)
        return dot(dm_full[p], w_ref[:, pl.ds(lo, feat)], 1, 1)

    loads[0].wait()
    loads[1].wait()
    d_proj = features(g)
    relayed(dm_full, y_mate, s_dm, r_dm)
    relay(dm_full.at[y_mate], dm_full, y_mate, core_mate, s_dm.at[2], r_dm)
    d_proj = d_proj + features(y_mate)
    relayed(dm_full, core_mate, s_dm, r_dm)
    d_proj = d_proj + features(core_mate)
    relayed(dm_full, diagonal, s_dm, r_dm)
    d_proj = (d_proj + features(diagonal)).astype(BF16)
    for h in range(HEAD_GRP):
        dp_send[h] = d_proj[:, h * HD : (h + 1) * HD]
        send(
            b != owners[h],
            lambda h=h: remote(
                dp_send.at[h], do_in.at[b], s_do.at[h], r_do.at[b], {"blk": owners[h]}
            ),
        )

        @pl.when(b == owners[h])
        def _(h=h):
            do_in[b] = dp_send[h]

    my_rows = pl.ds(pl.multiple_of(g * quarter, quarter), quarter)
    for t in range(blocks):
        lo = t * cols
        view = (lo // feat, my_rows, slice(lo % feat, lo % feat + cols))
        send(
            b != t,
            lambda t=t, view=view: remote(
                dm_full.at[view], d_cols.at[g, b], s_ca.at[t], r_ca.at[b], {"blk": t}
            ),
        )

        @pl.when(b == t)
        def _(view=view):
            d_cols[g, b] = dm_full[view]

    def own_part(i, ref):
        for t in range(blocks):

            @pl.when(b != t)
            def _(t=t):
                remote(
                    qkv_in.at[i, t], qkv_in.at[i, t], s_qkv.at[i, 0], r_qkv.at[i, t], {"blk": t}
                ).wait_recv()

        own_tile(i, ref, (slice(None), slice(0, HD))).wait()

    @pl.when(is_owner)
    def _():
        own_part(0, q_ref)
        for i in range(chunks):
            q_main[i] = dot(place_t[i], qkv_in[0].reshape(seq, HD), 1, 0).astype(BF16)
        own_part(1, k_ref)
        own_part(2, v_ref)

    for i in range(chunks):

        @pl.when(is_owner)
        def _(i=i):
            raw = dot(q_main[i], qkv_in[1].reshape(seq, HD), 1, 1)
            peak = jnp.max(raw, axis=1, keepdims=True)
            e = jnp.exp2((raw - peak) * (scale * math.log2(math.e)))
            p = (e * (1.0 / jnp.sum(e, axis=1, keepdims=True))).astype(BF16)
            probs[i] = p
            att = dot(p, qkv_in[2].reshape(seq, HD), 1, 0).astype(BF16)
            att_send[i * per : (i + 1) * per] = att.reshape(per, rows, HD)

        for t in range(i * per, (i + 1) * per):
            send(
                is_owner & (b != t),
                lambda t=t: remote(
                    att_send.at[t], att_all.at[t, mine], s_at.at[t], r_at.at[mine], {"blk": t}
                ),
            )

    @pl.when(is_owner)
    def _():
        att_all[b, mine] = att_send[b]

    for t in range(blocks):
        arrive(
            b != t,
            lambda t=t: remote(
                d_cols.at[g, t], d_cols.at[g, t], s_ca.at[t], r_ca.at[t], {"blk": t}
            ),
        )
    relay(d_cols.at[g], d_cols, g, y_mate, s_cb.at[0], r_cb)
    relay(d_cols.at[g], d_cols, g, core_mate, s_cb.at[1], r_cb)

    def backward(i):
        @pl.when(is_owner)
        def _():
            for t in range(i * per, (i + 1) * per):

                @pl.when(b != t)
                def _(t=t):
                    remote(do_in.at[t], do_in.at[t], s_do.at[0], r_do.at[t], {"blk": t}).wait_recv()

            do = do_in[i * per : (i + 1) * per].reshape(step, HD)
            att = att_send[i * per : (i + 1) * per].reshape(step, HD)
            delta = jnp.sum(do.astype(F32) * att.astype(F32), axis=1, keepdims=True)
            p = probs[i]
            d_probs = dot(do, qkv_in[2].reshape(seq, HD), 1, 1)
            ds = (p.astype(F32) * (d_probs - delta)).astype(BF16)
            dq_main[i] = (dot(ds, qkv_in[1].reshape(seq, HD), 1, 0) * scale).astype(BF16)
            dk = dot(ds, q_main[i], 0, 0)
            dv = dot(p, do, 0, 0)
            if i == 0:
                dk_acc[...] = dk
                dv_acc[...] = dv
            elif i < chunks - 1:
                dk_acc[...] += dk
                dv_acc[...] += dv
            else:
                dk = ((dk_acc[...] + dk) * scale).astype(BF16)
                grad_send[1] = dk.reshape(blocks, rows, HD)
                grad_send[2] = (dv_acc[...] + dv).astype(BF16).reshape(blocks, rows, HD)

    def send_grads(n):
        for t in range(blocks):
            send(
                is_owner & (b != t),
                lambda t=t: remote(
                    grad_send.at[n, t], grad_in.at[n, mine], s_gr.at[n, t], r_gr.at[n, mine], {"blk": t}
                ),
            )

    backward(0)
    for h in range(HEAD_GRP):
        arrive(
            b != owners[h],
            lambda h=h: remote(
                att_all.at[b, h], att_all.at[b, h], s_at.at[0], r_at.at[h], {"blk": owners[h]}
            ),
        )

    def pass_on(cond, slot, dev, sem):
        send(
            cond,
            lambda: remote(att_all.at[slot], att_all.at[slot], s_ag.at[sem], r_ag.at[slot], {"blk": dev}),
        )

    def landed(cond, slot):
        arrive(
            cond,
            lambda: remote(att_all.at[slot], att_all.at[slot], s_ag.at[0], r_ag.at[slot], {"blk": mate}),
        )

    pass_on(z < nz - 1, b, b + 2, 0)
    pass_on(z > 0, b, b - 2, 1)
    pass_on(always, b, mate, 2)

    def gather_step(s):
        if s >= nz:
            return
        low, high = z >= s, z + s < nz
        landed(low, b - 2 * s)
        pass_on(low & (z < nz - 1), b - 2 * s, b + 2, 4 * s)
        pass_on(low, b - 2 * s, mate, 4 * s + 1)
        landed(high, b + 2 * s)
        pass_on(high & (z > 0), b + 2 * s, b - 2, 4 * s + 2)
        pass_on(high, b + 2 * s, mate, 4 * s + 3)

    backward(1)
    gather_step(1)
    relayed(d_cols, y_mate, s_cb, r_cb)
    relay(d_cols.at[y_mate], d_cols, y_mate, core_mate, s_cb.at[2], r_cb)

    own = jnp.concatenate([att_all[b, h] for h in range(HEAD_GRP)], axis=1)
    for p in range(n_grp):
        rs_send[p] = dot(own, w_ref[:, p * feat : (p + 1) * feat], 1, 0).astype(BF16)
    for n, p in enumerate((diagonal, core_mate)):
        send(
            always,
            lambda n=n, p=p: remote(
                rs_send.at[p], rs_in.at[n], s_rs.at[n], r_rs.at[n], {"grp": core_mate}
            ),
        )

    def rs_landed(n):
        arrive(always, lambda: remote(rs_in.at[n], rs_in.at[n], s_rs.at[0], r_rs.at[n], {"grp": y_mate}))

    backward(2)
    gather_step(2)
    rs_landed(0)
    rs_pass[...] = (rs_send[y_mate].astype(F32) + rs_in[0].astype(F32)).astype(BF16)
    send(
        always,
        lambda: remote(rs_pass, rs_in.at[2], s_rs.at[2], r_rs.at[2], {"grp": y_mate}),
    )
    backward(3)
    send_grads(1)
    send_grads(2)

    @pl.when(is_owner)
    def _():
        turned = dot(place[...].reshape(seq, seq), dq_main[...].reshape(seq, HD), 1, 0)
        grad_send[0] = turned.astype(BF16).reshape(blocks, rows, HD)

    send_grads(0)
    gather_step(3)

    @pl.when(is_owner)
    def _():
        for n in range(3):
            grad_in[n, mine] = grad_send[n, b]

    rs_landed(1)
    rs_landed(2)
    loads[3].wait()
    total = rs_send[g].astype(F32) + rs_in[1].astype(F32) + rs_in[2].astype(F32)
    mixed_ref[...] = (hidden_ref[...].astype(F32) + total).astype(BF16)
    write(mixed_ref, mixed_out)

    relayed(d_cols, core_mate, s_cb, r_cb)
    relayed(d_cols, diagonal, s_cb, r_cb)
    for j in range(nz):
        landed(always, 2 * j + 1 - x)
    grads = d_cols[...].reshape(seq, cols)
    for h in range(HEAD_GRP):
        att = jnp.concatenate(
            [
                att_all[:, h, p * quarter : (p + 1) * quarter, :].reshape(blocks * quarter, HD)
                for p in range(n_grp)
            ],
            axis=0,
        )
        dw_ref[h] = dot(att, grads, 0, 0)
        write(dw_ref.at[h], dw_out.at[h * HD : (h + 1) * HD])

    for n, out in enumerate((dq_out, dk_out, dv_out)):
        for h in range(HEAD_GRP):
            arrive(
                b != owners[h],
                lambda n=n, h=h: remote(
                    grad_in.at[n, h], grad_in.at[n, h], s_gr.at[n, 0], r_gr.at[n, h], {"blk": owners[h]}
                ),
            )
            write(grad_in.at[n, h], out.at[:, h * HD : (h + 1) * HD])

    for copy in writes:
        copy.wait()
    for cond, make in pending:
        pl.when(cond)(lambda make=make: make().wait_send())


def write_kernel(*refs):
    srcs, dsts, held, into, out = refs[:5], refs[5:10], refs[10:15], refs[15], refs[16]
    loads = [pltpu.make_async_copy(srcs[i], held[i], into.at[i]) for i in range(5)]
    stores = [pltpu.make_async_copy(held[i], dsts[i], out.at[i]) for i in range(5)]
    for load in loads:
        load.start()
    for load, store in zip(loads, stores):
        load.wait()
        store.start()
    for store in stores:
        store.wait()


def on_device_fused(main_hidden, ctrl_query, ctrl_key, ctrl_value, w_out, d_mixed, control_slot):
    n_grp, blocks = lax.axis_size("grp"), lax.axis_size("blk")
    rows, feat = d_mixed.shape
    width, model = w_out.shape
    cols = model // blocks
    seq = rows * blocks
    step = seq // 4
    dma = pltpu.SemaphoreType.DMA
    sems = [
        dma((n_grp,)), dma((3, HEAD_GRP)), dma((HEAD_GRP,)), dma((HEAD_GRP,)), dma((blocks,)),
        dma((n_grp,)), dma((blocks,)), dma((2 * blocks,)), dma((n_grp,)), dma((3, blocks)), dma((7,)), dma((16,)),
        dma((n_grp,)), dma((3, blocks)), dma((blocks,)), dma((blocks,)), dma((blocks,)),
        dma((n_grp,)), dma((HEAD_GRP,)), dma((blocks,)), dma((n_grp,)), dma((3, HEAD_GRP)),
    ]
    hbm = pl.BlockSpec(memory_space=pltpu.HBM)
    tile = jax.ShapeDtypeStruct((rows, width), BF16)
    results = pl.pallas_call(
        fused_kernel,
        out_shape=(
            jax.ShapeDtypeStruct((rows, feat), BF16), tile, tile, tile,
            jax.ShapeDtypeStruct((width, cols), F32),
        ),
        in_specs=[hbm] * 7,
        out_specs=[hbm] * 5,
        scratch_shapes=[
            pltpu.VMEM((rows, feat), BF16),
            pltpu.VMEM((HEAD_GRP, HD, cols), F32),
            pltpu.VMEM((rows, feat), BF16),
            pltpu.VMEM((width, model), BF16),
            pltpu.VMEM((n_grp, rows, feat), BF16),
            pltpu.VMEM((3, blocks, rows, HD), BF16),
            pltpu.VMEM((blocks, 1, rows), jnp.int32),
            pltpu.VMEM((HEAD_GRP, rows, HD), BF16),
            pltpu.VMEM((blocks, rows, HD), BF16),
            pltpu.VMEM((4, step, HD), BF16),
            pltpu.VMEM((n_grp, blocks, rows // n_grp, cols), BF16),
            pltpu.VMEM((4, step, seq), BF16),
            pltpu.VMEM((4, step, seq), BF16),
            pltpu.VMEM((4, step, seq), BF16),
            pltpu.VMEM((4, step, HD), BF16),
            pltpu.VMEM((blocks, rows, HD), BF16),
            pltpu.VMEM((blocks, HEAD_GRP, rows, HD), BF16),
            pltpu.VMEM((n_grp, rows, feat), BF16),
            pltpu.VMEM((rows, feat), BF16),
            pltpu.VMEM((3, rows, feat), BF16),
            pltpu.VMEM((seq, HD), F32),
            pltpu.VMEM((seq, HD), F32),
            pltpu.VMEM((3, blocks, rows, HD), BF16),
            pltpu.VMEM((3, HEAD_GRP, rows, HD), BF16),
        ] + sems,
        compiler_params=pltpu.CompilerParams(
            collective_id=0, has_side_effects=True, vmem_limit_bytes=60 * 2**20
        ),
        cost_estimate=pl.CostEstimate(
            flops=2 * 5 * seq * seq * HD, bytes_accessed=16 * 2**20, transcendentals=seq * seq
        ),
    )(
        main_hidden, ctrl_query, ctrl_key, ctrl_value, w_out, d_mixed,
        control_slot.reshape(1, rows),
    )
    return pl.pallas_call(
        write_kernel,
        out_shape=tuple(jax.ShapeDtypeStruct(r.shape, r.dtype) for r in results),
        in_specs=[hbm] * 5,
        out_specs=[hbm] * 5,
        scratch_shapes=[pltpu.VMEM(r.shape, r.dtype) for r in results] + [dma((5,)), dma((5,))],
        compiler_params=pltpu.CompilerParams(vmem_limit_bytes=60 * 2**20),
    )(*results)


def solution(mesh):
    in_specs = (
        P("blk", "grp"),
        P("blk", "grp"),
        P("blk", "grp"),
        P("blk", "grp"),
        P("grp", None),
        P("blk", "grp"),
        P("blk"),
    )
    out_specs = (
        P("blk", "grp"),
        P("blk", "grp"),
        P("blk", "grp"),
        P("blk", "grp"),
        P("grp", "blk"),
    )
    body = on_device_fused if mesh.shape["blk"] == 8 else on_device
    return jax.shard_map(
        body, mesh=mesh, in_specs=in_specs, out_specs=out_specs, check_vma=False
    )
```

```python
import functools
import math

import jax
import jax.numpy as jnp
from jax import lax
from jax.experimental import pallas as pl
from jax.experimental.pallas import tpu as pltpu
from jax.sharding import PartitionSpec as P

HD = 128
HEAD_GRP = 3


def on_device(main_hidden, ctrl_query, ctrl_key, ctrl_value, w_out, d_mixed, control_slot):
    rows_dev = ctrl_query.shape[0]
    feature_cols = d_mixed.shape[1]
    blocks = lax.axis_size("blk")
    per_peer = rows_dev // blocks
    score_scale = 1.0 / math.sqrt(HD)
    whole_key, whole_value = (
        lax.all_gather(ctrl_key, "blk", axis=0, tiled=True),
        lax.all_gather(ctrl_value, "blk", axis=0, tiled=True),
    )
    outputs = []
    norm_list = []
    for head_idx in range(HEAD_GRP):
        columns = slice(head_idx * HD, (head_idx + 1) * HD)
        scores = (
            jnp.dot(
                ctrl_query[:, columns], whole_key[:, columns].T, preferred_element_type=jnp.float32
            )
            * score_scale
        )
        row_peak = jnp.max(scores, axis=1, keepdims=True)
        log_norm = row_peak + jnp.log(jnp.sum(jnp.exp(scores - row_peak), axis=1, keepdims=True))
        soft_weights = jnp.exp(scores - log_norm).astype(jnp.bfloat16)
        outputs.append(
            jnp.dot(soft_weights, whole_value[:, columns], preferred_element_type=jnp.float32)
        )
        norm_list.append(log_norm[:, 0])
    attended = jnp.concatenate(outputs, axis=1).astype(jnp.bfloat16)
    log_norms = jnp.stack(norm_list, axis=1)
    target = control_slot // rows_dev
    within = control_slot % rows_dev
    sort_order = jnp.argsort(target)
    inverse = jnp.argsort(sort_order)
    send_within = within[sort_order].reshape(blocks, per_peer)
    arrived, arrived_grad = (
        lax.all_to_all(send_within, "blk", split_axis=0, concat_axis=0, tiled=True),
        lax.all_to_all(
            d_mixed[sort_order].reshape(blocks, per_peer, feature_cols),
            "blk",
            split_axis=0,
            concat_axis=0,
            tiled=True,
        ),
    )
    placed = arrived.reshape(rows_dev)
    grad_rows = jnp.zeros_like(d_mixed).at[placed].set(arrived_grad.reshape(rows_dev, feature_cols))
    residual = lax.psum_scatter(
        jnp.dot(attended, w_out, preferred_element_type=jnp.float32).astype(jnp.bfloat16),
        "grp",
        scatter_dimension=1,
        tiled=True,
    ).astype(jnp.float32)
    returned = lax.all_to_all(
        residual[placed].reshape(blocks, per_peer, feature_cols),
        "blk",
        split_axis=0,
        concat_axis=0,
        tiled=True,
    )
    residual = returned.reshape(rows_dev, feature_cols)[inverse]
    main_mixed = (main_hidden.astype(jnp.float32) + residual).astype(jnp.bfloat16)
    grad_full = lax.all_gather(grad_rows, "grp", axis=1, tiled=True)
    d_proj = jnp.dot(grad_full, w_out.T, preferred_element_type=jnp.float32).astype(jnp.bfloat16)
    d_w_out = lax.psum_scatter(
        jnp.dot(attended.T, grad_full, preferred_element_type=jnp.float32),
        "blk",
        scatter_dimension=1,
        tiled=True,
    )
    row_delta = jnp.sum(
        (d_proj.astype(jnp.float32) * attended.astype(jnp.float32)).reshape(rows_dev, HEAD_GRP, HD),
        axis=2,
    )
    all_norms, all_delta = (
        lax.all_gather(log_norms, "blk", axis=0, tiled=True),
        lax.all_gather(row_delta, "blk", axis=0, tiled=True),
    )
    query_grads = []
    for head_idx in range(HEAD_GRP):
        columns = slice(head_idx * HD, (head_idx + 1) * HD)
        scores = (
            jnp.dot(
                ctrl_query[:, columns], whole_key[:, columns].T, preferred_element_type=jnp.float32
            )
            * score_scale
        )
        soft_weights = jnp.exp(scores - log_norms[:, head_idx : head_idx + 1])
        d_probs = jnp.dot(
            d_proj[:, columns], whole_value[:, columns].T, preferred_element_type=jnp.float32
        )
        d_scores = (soft_weights * (d_probs - row_delta[:, head_idx : head_idx + 1])).astype(
            jnp.bfloat16
        )
        query_grads.append(
            jnp.dot(d_scores, whole_key[:, columns], preferred_element_type=jnp.float32)
            * score_scale
        )
    d_query = jnp.concatenate(query_grads, axis=1).astype(jnp.bfloat16)
    query_piece = lax.all_gather(ctrl_query, "blk", axis=0, tiled=True)
    grad_piece = lax.all_gather(d_proj, "blk", axis=0, tiled=True)
    key_terms = []
    value_terms = []
    for head_idx in range(HEAD_GRP):
        columns = slice(head_idx * HD, (head_idx + 1) * HD)
        scores = (
            jnp.dot(
                query_piece[:, columns], ctrl_key[:, columns].T, preferred_element_type=jnp.float32
            )
            * score_scale
        )
        soft_weights = jnp.exp(scores - all_norms[:, head_idx : head_idx + 1])
        d_probs = jnp.dot(
            grad_piece[:, columns], ctrl_value[:, columns].T, preferred_element_type=jnp.float32
        )
        d_scores = (soft_weights * (d_probs - all_delta[:, head_idx : head_idx + 1])).astype(
            jnp.bfloat16
        )
        key_terms.append(
            jnp.dot(d_scores.T, query_piece[:, columns], preferred_element_type=jnp.float32)
            * score_scale
        )
        value_terms.append(
            jnp.dot(
                soft_weights.astype(jnp.bfloat16).T,
                grad_piece[:, columns],
                preferred_element_type=jnp.float32,
            )
        )
    key_grad = jnp.concatenate(key_terms, axis=1)
    value_grad = jnp.concatenate(value_terms, axis=1)
    return (
        main_mixed,
        d_query,
        key_grad.astype(jnp.bfloat16),
        value_grad.astype(jnp.bfloat16),
        d_w_out,
    )


F32, BF16 = jnp.float32, jnp.bfloat16


def dot(a, b, ca, cb):
    return lax.dot_general(a, b, (((ca,), (cb,)), ((), ())), preferred_element_type=F32)


def fused_kernel(
    hidden_hbm, q_ref, k_ref, v_ref, w_hbm, dm_ref, slot_ref,
    mixed_out, dq_out, dk_out, dv_out, dw_out, mixed_ref, dw_ref, hidden_ref, w_ref,
    dm_full, qkv_in, slots_in, dp_send, do_in, q_main, d_cols,
    probs, place, place_t, k_t, v_t, dq_main, att_send, att_all, rs_send, rs_pass, rs_in,
    dk_acc, dv_acc, grad_send, grad_in,
    s_dm, s_qkv, s_slot, s_do, s_ca, s_cb, s_at, s_ag, s_rs, s_gr, s_in, s_out,
    r_dm, r_qkv, r_slot, r_do, r_ca, r_cb, r_at, r_ag, r_rs, r_gr,
):
    g = lax.axis_index("grp")
    b = lax.axis_index("blk")
    n_grp, blocks = dm_full.shape[0], qkv_in.shape[1]
    rows, feat = dm_ref.shape
    cols = d_cols.shape[3]
    quarter = rows // n_grp
    seq = rows * blocks
    chunks = 4
    per = blocks // chunks
    step = seq // chunks
    scale = 1.0 / math.sqrt(HD)
    c = g % 2
    z, x = b // 2, b % 2
    nz = blocks // 2
    mate = b + 1 - 2 * x
    core_mate, y_mate, diagonal = g + 1 - 2 * c, (g + 2) % n_grp, n_grp - 1 - g
    owners = [2 + 2 * c, 5 - 2 * c, 7 * c]
    mine = jnp.where(b == owners[1], 1, jnp.where(b == owners[2], 2, 0))
    is_owner = (b == owners[0]) | (b == owners[1]) | (b == owners[2])
    always = b >= 0
    pending = []
    writes = []

    def write(src, dst):
        copy = pltpu.make_async_copy(src, dst, s_out.at[len(writes)])
        copy.start()
        writes.append(copy)

    def remote(src, dst, ss, rs, dev):
        return pltpu.make_async_remote_copy(
            src_ref=src, dst_ref=dst, send_sem=ss, recv_sem=rs,
            device_id=dev, device_id_type=pl.DeviceIdType.MESH,
        )

    def send(cond, make):
        pl.when(cond)(lambda: make().start())
        pending.append((cond, make))

    def arrive(cond, make):
        pl.when(cond)(lambda: make().wait_recv())

    loads = [
        pltpu.make_async_copy(dm_ref, dm_full.at[g], s_in.at[0]),
        pltpu.make_async_copy(w_hbm, w_ref, s_in.at[1]),
        pltpu.make_async_copy(slot_ref, slots_in.at[b], s_in.at[2]),
        pltpu.make_async_copy(hidden_hbm, hidden_ref, s_in.at[3]),
    ]
    for load in loads:
        load.start()

    def own_tile(i, ref, tile):
        return pltpu.make_async_copy(ref.at[tile], qkv_in.at[i, b], s_in.at[4 + i])

    barrier = pltpu.get_barrier_semaphore()
    for d in range(1, n_grp):
        pl.semaphore_signal(
            barrier, inc=1, device_id={"grp": (g + d) % n_grp}, device_id_type=pl.DeviceIdType.MESH
        )
    for d in range(1, blocks):
        pl.semaphore_signal(
            barrier, inc=1, device_id={"blk": (b + d) % blocks}, device_id_type=pl.DeviceIdType.MESH
        )
    pl.semaphore_wait(barrier, n_grp + blocks - 2)

    def relay(src, buf, slot, dev, ss, rs):
        send(always, lambda: remote(src, buf.at[slot], ss, rs.at[slot], {"grp": dev}))

    def relayed(buf, slot, ss, rs):
        arrive(always, lambda: remote(buf.at[slot], buf.at[slot], ss.at[0], rs.at[slot], {"grp": y_mate}))

    relay(dm_ref, dm_full, g, y_mate, s_dm.at[0], r_dm)
    relay(dm_ref, dm_full, g, core_mate, s_dm.at[1], r_dm)
    for i, ref in enumerate((q_ref, k_ref, v_ref)):
        for h in range(HEAD_GRP):
            tile = (slice(None), slice(h * HD, (h + 1) * HD))
            send(
                b != owners[h],
                lambda i=i, ref=ref, h=h, tile=tile: remote(
                    ref.at[tile], qkv_in.at[i, b], s_qkv.at[i, h], r_qkv.at[i, b], {"blk": owners[h]}
                ),
            )

            @pl.when(b == owners[h])
            def _(i=i, ref=ref, tile=tile):
                own_tile(i, ref, tile).start()

    for h in range(HEAD_GRP):
        send(
            b != owners[h],
            lambda h=h: remote(
                slot_ref, slots_in.at[b], s_slot.at[h], r_slot.at[b], {"blk": owners[h]}
            ),
        )

    loads[2].wait()

    @pl.when(is_owner)
    def _():
        for t in range(blocks):

            @pl.when(b != t)
            def _(t=t):
                remote(slot_ref, slots_in.at[t], s_slot.at[0], r_slot.at[t], {"blk": t}).wait_recv()

        slot_row = jnp.concatenate([slots_in[t] for t in range(blocks)], axis=1)
        slot_col = jnp.transpose(jnp.broadcast_to(slot_row.astype(F32), (8, seq)))[:, :1]
        lane = lax.broadcasted_iota(jnp.int32, (step, seq), 1)
        for i in range(chunks):
            at = lax.broadcasted_iota(jnp.int32, (step, seq), 0) + i * step
            place[i] = jnp.where(at == slot_row, 1.0, 0.0).astype(BF16)
            want = slot_col[i * step : (i + 1) * step].astype(jnp.int32)
            place_t[i] = jnp.where(lane == want, 1.0, 0.0).astype(BF16)

    def features(p):
        lo = pl.multiple_of(p * feat, HD)
        return dot(dm_full[p], w_ref[:, pl.ds(lo, feat)], 1, 1)

    loads[0].wait()
    loads[1].wait()
    d_proj = features(g)
    relayed(dm_full, y_mate, s_dm, r_dm)
    relay(dm_full.at[y_mate], dm_full, y_mate, core_mate, s_dm.at[2], r_dm)
    d_proj = d_proj + features(y_mate)
    relayed(dm_full, core_mate, s_dm, r_dm)
    d_proj = d_proj + features(core_mate)
    relayed(dm_full, diagonal, s_dm, r_dm)
    d_proj = (d_proj + features(diagonal)).astype(BF16)
    for h in range(HEAD_GRP):
        dp_send[h] = d_proj[:, h * HD : (h + 1) * HD]
        send(
            b != owners[h],
            lambda h=h: remote(
                dp_send.at[h], do_in.at[b], s_do.at[h], r_do.at[b], {"blk": owners[h]}
            ),
        )

        @pl.when(b == owners[h])
        def _(h=h):
            do_in[b] = dp_send[h]

    my_rows = pl.ds(pl.multiple_of(g * quarter, quarter), quarter)
    for t in range(blocks):
        lo = t * cols
        view = (lo // feat, my_rows, slice(lo % feat, lo % feat + cols))
        send(
            b != t,
            lambda t=t, view=view: remote(
                dm_full.at[view], d_cols.at[g, b], s_ca.at[t], r_ca.at[b], {"blk": t}
            ),
        )

        @pl.when(b == t)
        def _(view=view):
            d_cols[g, b] = dm_full[view]

    def own_part(i, ref):
        for t in range(blocks):

            @pl.when(b != t)
            def _(t=t):
                remote(
                    qkv_in.at[i, t], qkv_in.at[i, t], s_qkv.at[i, 0], r_qkv.at[i, t], {"blk": t}
                ).wait_recv()

        own_tile(i, ref, (slice(None), slice(0, HD))).wait()

    @pl.when(is_owner)
    def _():
        own_part(0, q_ref)
        for i in range(chunks):
            q_main[i] = dot(place_t[i], qkv_in[0].reshape(seq, HD), 1, 0).astype(BF16)
        own_part(1, k_ref)
        k_t[...] = jnp.transpose(qkv_in[1].reshape(seq, HD).astype(F32)).astype(BF16)
        own_part(2, v_ref)
        v_t[...] = jnp.transpose(qkv_in[2].reshape(seq, HD).astype(F32)).astype(BF16)

    for i in range(chunks):

        @pl.when(is_owner)
        def _(i=i):
            raw = dot(qkv_in[1].reshape(seq, HD), q_main[i], 1, 1)
            peak = jnp.max(raw, axis=0, keepdims=True)
            e = jnp.exp2((raw - peak) * (scale * math.log2(math.e)))
            p = (e * (1.0 / jnp.sum(e, axis=0, keepdims=True))).astype(BF16)
            probs[i] = p
            att = dot(v_t[...], p, 1, 0).astype(BF16)
            for n in range(per):
                att_send[i * per + n] = att[:, n * rows : (n + 1) * rows]

        for t in range(i * per, (i + 1) * per):
            send(
                is_owner & (b != t),
                lambda t=t: remote(
                    att_send.at[t], att_all.at[t, mine], s_at.at[t], r_at.at[mine], {"blk": t}
                ),
            )

    @pl.when(is_owner)
    def _():
        att_all[b, mine] = att_send[b]

    for t in range(blocks):
        arrive(
            b != t,
            lambda t=t: remote(
                d_cols.at[g, t], d_cols.at[g, t], s_ca.at[t], r_ca.at[t], {"blk": t}
            ),
        )
    relay(d_cols.at[g], d_cols, g, y_mate, s_cb.at[0], r_cb)
    relay(d_cols.at[g], d_cols, g, core_mate, s_cb.at[1], r_cb)

    def backward(i):
        @pl.when(is_owner)
        def _():
            for t in range(i * per, (i + 1) * per):

                @pl.when(b != t)
                def _(t=t):
                    remote(do_in.at[t], do_in.at[t], s_do.at[0], r_do.at[t], {"blk": t}).wait_recv()

            do = do_in[i * per : (i + 1) * per].reshape(step, HD)
            delta = jnp.concatenate(
                [
                    jnp.sum(
                        jnp.transpose(do_in[t].astype(F32)) * att_send[t].astype(F32),
                        axis=0, keepdims=True,
                    )
                    for t in range(i * per, (i + 1) * per)
                ],
                axis=1,
            )
            p = probs[i]
            d_probs = dot(qkv_in[2].reshape(seq, HD), do, 1, 1)
            ds = (p.astype(F32) * (d_probs - delta)).astype(BF16)
            dq_main[i] = jnp.transpose(dot(k_t[...], ds, 1, 0) * scale).astype(BF16)
            dk = dot(ds, q_main[i], 1, 0)
            dv = dot(p, do, 1, 0)
            if i == 0:
                dk_acc[...] = dk
                dv_acc[...] = dv
            elif i < chunks - 1:
                dk_acc[...] += dk
                dv_acc[...] += dv
            else:
                dk = ((dk_acc[...] + dk) * scale).astype(BF16)
                grad_send[1] = dk.reshape(blocks, rows, HD)
                grad_send[2] = (dv_acc[...] + dv).astype(BF16).reshape(blocks, rows, HD)

    def send_grads(n):
        for t in range(blocks):
            send(
                is_owner & (b != t),
                lambda t=t: remote(
                    grad_send.at[n, t], grad_in.at[n, mine], s_gr.at[n, t], r_gr.at[n, mine], {"blk": t}
                ),
            )

    backward(0)
    for h in range(HEAD_GRP):
        arrive(
            b != owners[h],
            lambda h=h: remote(
                att_all.at[b, h], att_all.at[b, h], s_at.at[0], r_at.at[h], {"blk": owners[h]}
            ),
        )

    def pass_on(cond, slot, dev, sem):
        send(
            cond,
            lambda: remote(att_all.at[slot], att_all.at[slot], s_ag.at[sem], r_ag.at[slot], {"blk": dev}),
        )

    def landed(cond, slot):
        arrive(
            cond,
            lambda: remote(att_all.at[slot], att_all.at[slot], s_ag.at[0], r_ag.at[slot], {"blk": mate}),
        )

    pass_on(z < nz - 1, b, b + 2, 0)
    pass_on(z > 0, b, b - 2, 1)
    pass_on(always, b, mate, 2)

    def gather_step(s):
        if s >= nz:
            return
        low, high = z >= s, z + s < nz
        landed(low, b - 2 * s)
        pass_on(low & (z < nz - 1), b - 2 * s, b + 2, 4 * s)
        pass_on(low, b - 2 * s, mate, 4 * s + 1)
        landed(high, b + 2 * s)
        pass_on(high & (z > 0), b + 2 * s, b - 2, 4 * s + 2)
        pass_on(high, b + 2 * s, mate, 4 * s + 3)

    backward(1)
    gather_step(1)
    relayed(d_cols, y_mate, s_cb, r_cb)
    relay(d_cols.at[y_mate], d_cols, y_mate, core_mate, s_cb.at[2], r_cb)

    own = jnp.concatenate([att_all[b, h] for h in range(HEAD_GRP)], axis=0)
    own = jnp.transpose(own.astype(F32)).astype(BF16)
    for p in range(n_grp):
        rs_send[p] = dot(own, w_ref[:, p * feat : (p + 1) * feat], 1, 0).astype(BF16)
    for n, p in enumerate((diagonal, core_mate)):
        send(
            always,
            lambda n=n, p=p: remote(
                rs_send.at[p], rs_in.at[n], s_rs.at[n], r_rs.at[n], {"grp": core_mate}
            ),
        )

    def rs_landed(n):
        arrive(always, lambda: remote(rs_in.at[n], rs_in.at[n], s_rs.at[0], r_rs.at[n], {"grp": y_mate}))

    backward(2)
    gather_step(2)
    rs_landed(0)
    rs_pass[...] = (rs_send[y_mate].astype(F32) + rs_in[0].astype(F32)).astype(BF16)
    send(
        always,
        lambda: remote(rs_pass, rs_in.at[2], s_rs.at[2], r_rs.at[2], {"grp": y_mate}),
    )
    backward(3)
    send_grads(1)
    send_grads(2)

    @pl.when(is_owner)
    def _():
        turned = dot(place[...].reshape(seq, seq), dq_main[...].reshape(seq, HD), 1, 0)
        grad_send[0] = turned.astype(BF16).reshape(blocks, rows, HD)

    send_grads(0)
    gather_step(3)

    @pl.when(is_owner)
    def _():
        for n in range(3):
            grad_in[n, mine] = grad_send[n, b]

    rs_landed(1)
    rs_landed(2)
    loads[3].wait()
    total = rs_send[g].astype(F32) + rs_in[1].astype(F32) + rs_in[2].astype(F32)
    mixed_ref[...] = (hidden_ref[...].astype(F32) + total).astype(BF16)
    write(mixed_ref, mixed_out)

    relayed(d_cols, core_mate, s_cb, r_cb)
    relayed(d_cols, diagonal, s_cb, r_cb)
    for j in range(nz):
        landed(always, 2 * j + 1 - x)
    grads = jnp.concatenate(
        [d_cols[p, t] for t in range(blocks) for p in range(n_grp)], axis=0
    )
    for h in range(HEAD_GRP):
        att = jnp.concatenate([att_all[t, h] for t in range(blocks)], axis=1)
        dw_ref[h] = dot(att, grads, 1, 0)
        write(dw_ref.at[h], dw_out.at[h * HD : (h + 1) * HD])

    for n, out in enumerate((dq_out, dk_out, dv_out)):
        for h in range(HEAD_GRP):
            arrive(
                b != owners[h],
                lambda n=n, h=h: remote(
                    grad_in.at[n, h], grad_in.at[n, h], s_gr.at[n, 0], r_gr.at[n, h], {"blk": owners[h]}
                ),
            )
            write(grad_in.at[n, h], out.at[:, h * HD : (h + 1) * HD])

    for copy in writes:
        copy.wait()
    for cond, make in pending:
        pl.when(cond)(lambda make=make: make().wait_send())


def write_kernel(*refs):
    srcs, dsts, held, into, out = refs[:5], refs[5:10], refs[10:15], refs[15], refs[16]
    loads = [pltpu.make_async_copy(srcs[i], held[i], into.at[i]) for i in range(5)]
    stores = [pltpu.make_async_copy(held[i], dsts[i], out.at[i]) for i in range(5)]
    for load in loads:
        load.start()
    for load, store in zip(loads, stores):
        load.wait()
        store.start()
    for store in stores:
        store.wait()


def on_device_fused(main_hidden, ctrl_query, ctrl_key, ctrl_value, w_out, d_mixed, control_slot):
    n_grp, blocks = lax.axis_size("grp"), lax.axis_size("blk")
    rows, feat = d_mixed.shape
    width, model = w_out.shape
    cols = model // blocks
    seq = rows * blocks
    step = seq // 4
    dma = pltpu.SemaphoreType.DMA
    sems = [
        dma((n_grp,)), dma((3, HEAD_GRP)), dma((HEAD_GRP,)), dma((HEAD_GRP,)), dma((blocks,)),
        dma((n_grp,)), dma((blocks,)), dma((2 * blocks,)), dma((n_grp,)), dma((3, blocks)), dma((7,)), dma((16,)),
        dma((n_grp,)), dma((3, blocks)), dma((blocks,)), dma((blocks,)), dma((blocks,)),
        dma((n_grp,)), dma((HEAD_GRP,)), dma((blocks,)), dma((n_grp,)), dma((3, HEAD_GRP)),
    ]
    hbm = pl.BlockSpec(memory_space=pltpu.HBM)
    tile = jax.ShapeDtypeStruct((rows, width), BF16)
    results = pl.pallas_call(
        fused_kernel,
        out_shape=(
            jax.ShapeDtypeStruct((rows, feat), BF16), tile, tile, tile,
            jax.ShapeDtypeStruct((width, cols), F32),
        ),
        in_specs=[hbm] * 7,
        out_specs=[hbm] * 5,
        scratch_shapes=[
            pltpu.VMEM((rows, feat), BF16),
            pltpu.VMEM((HEAD_GRP, HD, cols), F32),
            pltpu.VMEM((rows, feat), BF16),
            pltpu.VMEM((width, model), BF16),
            pltpu.VMEM((n_grp, rows, feat), BF16),
            pltpu.VMEM((3, blocks, rows, HD), BF16),
            pltpu.VMEM((blocks, 1, rows), jnp.int32),
            pltpu.VMEM((HEAD_GRP, rows, HD), BF16),
            pltpu.VMEM((blocks, rows, HD), BF16),
            pltpu.VMEM((4, step, HD), BF16),
            pltpu.VMEM((n_grp, blocks, rows // n_grp, cols), BF16),
            pltpu.VMEM((4, seq, step), BF16),
            pltpu.VMEM((4, step, seq), BF16),
            pltpu.VMEM((4, step, seq), BF16),
            pltpu.VMEM((HD, seq), BF16),
            pltpu.VMEM((HD, seq), BF16),
            pltpu.VMEM((4, step, HD), BF16),
            pltpu.VMEM((blocks, rows, HD), BF16),
            pltpu.VMEM((blocks, HEAD_GRP, rows, HD), BF16),
            pltpu.VMEM((n_grp, rows, feat), BF16),
            pltpu.VMEM((rows, feat), BF16),
            pltpu.VMEM((3, rows, feat), BF16),
            pltpu.VMEM((seq, HD), F32),
            pltpu.VMEM((seq, HD), F32),
            pltpu.VMEM((3, blocks, rows, HD), BF16),
            pltpu.VMEM((3, HEAD_GRP, rows, HD), BF16),
        ] + sems,
        compiler_params=pltpu.CompilerParams(
            collective_id=0, has_side_effects=True, vmem_limit_bytes=60 * 2**20
        ),
        cost_estimate=pl.CostEstimate(
            flops=2 * 5 * seq * seq * HD, bytes_accessed=16 * 2**20, transcendentals=seq * seq
        ),
    )(
        main_hidden, ctrl_query, ctrl_key, ctrl_value, w_out, d_mixed,
        control_slot.reshape(1, rows),
    )
    return pl.pallas_call(
        write_kernel,
        out_shape=tuple(jax.ShapeDtypeStruct(r.shape, r.dtype) for r in results),
        in_specs=[hbm] * 5,
        out_specs=[hbm] * 5,
        scratch_shapes=[pltpu.VMEM(r.shape, r.dtype) for r in results] + [dma((5,)), dma((5,))],
        compiler_params=pltpu.CompilerParams(vmem_limit_bytes=60 * 2**20),
    )(*results)


def solution(mesh):
    in_specs = (
        P("blk", "grp"),
        P("blk", "grp"),
        P("blk", "grp"),
        P("blk", "grp"),
        P("grp", None),
        P("blk", "grp"),
        P("blk"),
    )
    out_specs = (
        P("blk", "grp"),
        P("blk", "grp"),
        P("blk", "grp"),
        P("blk", "grp"),
        P("grp", "blk"),
    )
    body = on_device_fused if mesh.shape["blk"] == 8 else on_device
    return jax.shard_map(
        body, mesh=mesh, in_specs=in_specs, out_specs=out_specs, check_vma=False
    )
```

```python
import functools
import math

import jax
import jax.numpy as jnp
from jax import lax
from jax.experimental import pallas as pl
from jax.experimental.pallas import tpu as pltpu
from jax.sharding import PartitionSpec as P

HD = 128
HEAD_GRP = 3


def on_device(main_hidden, ctrl_query, ctrl_key, ctrl_value, w_out, d_mixed, control_slot):
    rows_dev = ctrl_query.shape[0]
    feature_cols = d_mixed.shape[1]
    blocks = lax.axis_size("blk")
    per_peer = rows_dev // blocks
    score_scale = 1.0 / math.sqrt(HD)
    whole_key, whole_value = (
        lax.all_gather(ctrl_key, "blk", axis=0, tiled=True),
        lax.all_gather(ctrl_value, "blk", axis=0, tiled=True),
    )
    outputs = []
    norm_list = []
    for head_idx in range(HEAD_GRP):
        columns = slice(head_idx * HD, (head_idx + 1) * HD)
        scores = (
            jnp.dot(
                ctrl_query[:, columns], whole_key[:, columns].T, preferred_element_type=jnp.float32
            )
            * score_scale
        )
        row_peak = jnp.max(scores, axis=1, keepdims=True)
        log_norm = row_peak + jnp.log(jnp.sum(jnp.exp(scores - row_peak), axis=1, keepdims=True))
        soft_weights = jnp.exp(scores - log_norm).astype(jnp.bfloat16)
        outputs.append(
            jnp.dot(soft_weights, whole_value[:, columns], preferred_element_type=jnp.float32)
        )
        norm_list.append(log_norm[:, 0])
    attended = jnp.concatenate(outputs, axis=1).astype(jnp.bfloat16)
    log_norms = jnp.stack(norm_list, axis=1)
    target = control_slot // rows_dev
    within = control_slot % rows_dev
    sort_order = jnp.argsort(target)
    inverse = jnp.argsort(sort_order)
    send_within = within[sort_order].reshape(blocks, per_peer)
    arrived, arrived_grad = (
        lax.all_to_all(send_within, "blk", split_axis=0, concat_axis=0, tiled=True),
        lax.all_to_all(
            d_mixed[sort_order].reshape(blocks, per_peer, feature_cols),
            "blk",
            split_axis=0,
            concat_axis=0,
            tiled=True,
        ),
    )
    placed = arrived.reshape(rows_dev)
    grad_rows = jnp.zeros_like(d_mixed).at[placed].set(arrived_grad.reshape(rows_dev, feature_cols))
    residual = lax.psum_scatter(
        jnp.dot(attended, w_out, preferred_element_type=jnp.float32).astype(jnp.bfloat16),
        "grp",
        scatter_dimension=1,
        tiled=True,
    ).astype(jnp.float32)
    returned = lax.all_to_all(
        residual[placed].reshape(blocks, per_peer, feature_cols),
        "blk",
        split_axis=0,
        concat_axis=0,
        tiled=True,
    )
    residual = returned.reshape(rows_dev, feature_cols)[inverse]
    main_mixed = (main_hidden.astype(jnp.float32) + residual).astype(jnp.bfloat16)
    grad_full = lax.all_gather(grad_rows, "grp", axis=1, tiled=True)
    d_proj = jnp.dot(grad_full, w_out.T, preferred_element_type=jnp.float32).astype(jnp.bfloat16)
    d_w_out = lax.psum_scatter(
        jnp.dot(attended.T, grad_full, preferred_element_type=jnp.float32),
        "blk",
        scatter_dimension=1,
        tiled=True,
    )
    row_delta = jnp.sum(
        (d_proj.astype(jnp.float32) * attended.astype(jnp.float32)).reshape(rows_dev, HEAD_GRP, HD),
        axis=2,
    )
    all_norms, all_delta = (
        lax.all_gather(log_norms, "blk", axis=0, tiled=True),
        lax.all_gather(row_delta, "blk", axis=0, tiled=True),
    )
    query_grads = []
    for head_idx in range(HEAD_GRP):
        columns = slice(head_idx * HD, (head_idx + 1) * HD)
        scores = (
            jnp.dot(
                ctrl_query[:, columns], whole_key[:, columns].T, preferred_element_type=jnp.float32
            )
            * score_scale
        )
        soft_weights = jnp.exp(scores - log_norms[:, head_idx : head_idx + 1])
        d_probs = jnp.dot(
            d_proj[:, columns], whole_value[:, columns].T, preferred_element_type=jnp.float32
        )
        d_scores = (soft_weights * (d_probs - row_delta[:, head_idx : head_idx + 1])).astype(
            jnp.bfloat16
        )
        query_grads.append(
            jnp.dot(d_scores, whole_key[:, columns], preferred_element_type=jnp.float32)
            * score_scale
        )
    d_query = jnp.concatenate(query_grads, axis=1).astype(jnp.bfloat16)
    query_piece = lax.all_gather(ctrl_query, "blk", axis=0, tiled=True)
    grad_piece = lax.all_gather(d_proj, "blk", axis=0, tiled=True)
    key_terms = []
    value_terms = []
    for head_idx in range(HEAD_GRP):
        columns = slice(head_idx * HD, (head_idx + 1) * HD)
        scores = (
            jnp.dot(
                query_piece[:, columns], ctrl_key[:, columns].T, preferred_element_type=jnp.float32
            )
            * score_scale
        )
        soft_weights = jnp.exp(scores - all_norms[:, head_idx : head_idx + 1])
        d_probs = jnp.dot(
            grad_piece[:, columns], ctrl_value[:, columns].T, preferred_element_type=jnp.float32
        )
        d_scores = (soft_weights * (d_probs - all_delta[:, head_idx : head_idx + 1])).astype(
            jnp.bfloat16
        )
        key_terms.append(
            jnp.dot(d_scores.T, query_piece[:, columns], preferred_element_type=jnp.float32)
            * score_scale
        )
        value_terms.append(
            jnp.dot(
                soft_weights.astype(jnp.bfloat16).T,
                grad_piece[:, columns],
                preferred_element_type=jnp.float32,
            )
        )
    key_grad = jnp.concatenate(key_terms, axis=1)
    value_grad = jnp.concatenate(value_terms, axis=1)
    return (
        main_mixed,
        d_query,
        key_grad.astype(jnp.bfloat16),
        value_grad.astype(jnp.bfloat16),
        d_w_out,
    )


F32, BF16 = jnp.float32, jnp.bfloat16


def dot(a, b, ca, cb):
    return lax.dot_general(a, b, (((ca,), (cb,)), ((), ())), preferred_element_type=F32)


def fused_kernel(
    hidden_hbm, q_ref, k_ref, v_ref, w_hbm, dm_ref, slot_ref,
    mixed_out, dq_out, dk_out, dv_out, dw_out, mixed_ref, dw_ref, hidden_ref, w_ref,
    dm_full, qkv_in, slots_in, dp_send, do_in, q_main, d_cols,
    probs, place, place_t, k_t, v_t, dq_main, att_send, att_all, rs_send, rs_pass, rs_in,
    dq_acc, delta_row, grad_send, grad_in,
    s_dm, s_qkv, s_slot, s_do, s_ca, s_cb, s_at, s_ag, s_rs, s_gr, s_in, s_out,
    r_dm, r_qkv, r_slot, r_do, r_ca, r_cb, r_at, r_ag, r_rs, r_gr,
):
    g = lax.axis_index("grp")
    b = lax.axis_index("blk")
    n_grp, blocks = dm_full.shape[0], qkv_in.shape[1]
    rows, feat = dm_ref.shape
    cols = d_cols.shape[3]
    quarter = rows // n_grp
    seq = rows * blocks
    chunks = 4
    per = blocks // chunks
    step = seq // chunks
    scale = 1.0 / math.sqrt(HD)
    c = g % 2
    z, x = b // 2, b % 2
    nz = blocks // 2
    mate = b + 1 - 2 * x
    core_mate, y_mate, diagonal = g + 1 - 2 * c, (g + 2) % n_grp, n_grp - 1 - g
    owners = [2 + 2 * c, 5 - 2 * c, 7 * c]
    mine = jnp.where(b == owners[1], 1, jnp.where(b == owners[2], 2, 0))
    is_owner = (b == owners[0]) | (b == owners[1]) | (b == owners[2])
    always = b >= 0
    pending = []
    writes = []

    def write(src, dst):
        copy = pltpu.make_async_copy(src, dst, s_out.at[len(writes)])
        copy.start()
        writes.append(copy)

    def remote(src, dst, ss, rs, dev):
        return pltpu.make_async_remote_copy(
            src_ref=src, dst_ref=dst, send_sem=ss, recv_sem=rs,
            device_id=dev, device_id_type=pl.DeviceIdType.MESH,
        )

    def send(cond, make):
        pl.when(cond)(lambda: make().start())
        pending.append((cond, make))

    def arrive(cond, make):
        pl.when(cond)(lambda: make().wait_recv())

    loads = [
        pltpu.make_async_copy(dm_ref, dm_full.at[g], s_in.at[0]),
        pltpu.make_async_copy(w_hbm, w_ref, s_in.at[1]),
        pltpu.make_async_copy(slot_ref, slots_in.at[b], s_in.at[2]),
        pltpu.make_async_copy(hidden_hbm, hidden_ref, s_in.at[3]),
    ]
    for load in loads:
        load.start()

    def own_tile(i, ref, tile):
        return pltpu.make_async_copy(ref.at[tile], qkv_in.at[i, b], s_in.at[4 + i])

    barrier = pltpu.get_barrier_semaphore()
    for d in range(1, n_grp):
        pl.semaphore_signal(
            barrier, inc=1, device_id={"grp": (g + d) % n_grp}, device_id_type=pl.DeviceIdType.MESH
        )
    for d in range(1, blocks):
        pl.semaphore_signal(
            barrier, inc=1, device_id={"blk": (b + d) % blocks}, device_id_type=pl.DeviceIdType.MESH
        )
    pl.semaphore_wait(barrier, n_grp + blocks - 2)

    def relay(src, buf, slot, dev, ss, rs):
        send(always, lambda: remote(src, buf.at[slot], ss, rs.at[slot], {"grp": dev}))

    def relayed(buf, slot, ss, rs):
        arrive(always, lambda: remote(buf.at[slot], buf.at[slot], ss.at[0], rs.at[slot], {"grp": y_mate}))

    relay(dm_ref, dm_full, g, y_mate, s_dm.at[0], r_dm)
    relay(dm_ref, dm_full, g, core_mate, s_dm.at[1], r_dm)
    for i, ref in enumerate((q_ref, k_ref, v_ref)):
        for h in range(HEAD_GRP):
            tile = (slice(None), slice(h * HD, (h + 1) * HD))
            send(
                b != owners[h],
                lambda i=i, ref=ref, h=h, tile=tile: remote(
                    ref.at[tile], qkv_in.at[i, b], s_qkv.at[i, h], r_qkv.at[i, b], {"blk": owners[h]}
                ),
            )

            @pl.when(b == owners[h])
            def _(i=i, ref=ref, tile=tile):
                own_tile(i, ref, tile).start()

    for h in range(HEAD_GRP):
        send(
            b != owners[h],
            lambda h=h: remote(
                slot_ref, slots_in.at[b], s_slot.at[h], r_slot.at[b], {"blk": owners[h]}
            ),
        )

    loads[2].wait()

    @pl.when(is_owner)
    def _():
        for t in range(blocks):

            @pl.when(b != t)
            def _(t=t):
                remote(slot_ref, slots_in.at[t], s_slot.at[0], r_slot.at[t], {"blk": t}).wait_recv()

        slot_row = jnp.concatenate([slots_in[t] for t in range(blocks)], axis=1)
        slot_col = jnp.transpose(jnp.broadcast_to(slot_row.astype(F32), (8, seq)))[:, :1]
        lane = lax.broadcasted_iota(jnp.int32, (step, seq), 1)
        for i in range(chunks):
            at = lax.broadcasted_iota(jnp.int32, (step, seq), 0) + i * step
            place[i] = jnp.where(at == slot_row, 1.0, 0.0).astype(BF16)
            want = slot_col[i * step : (i + 1) * step].astype(jnp.int32)
            place_t[i] = jnp.where(lane == want, 1.0, 0.0).astype(BF16)

    def features(p):
        lo = pl.multiple_of(p * feat, HD)
        return dot(dm_full[p], w_ref[:, pl.ds(lo, feat)], 1, 1)

    loads[0].wait()
    loads[1].wait()
    d_proj = features(g)
    relayed(dm_full, y_mate, s_dm, r_dm)
    relay(dm_full.at[y_mate], dm_full, y_mate, core_mate, s_dm.at[2], r_dm)
    d_proj = d_proj + features(y_mate)
    relayed(dm_full, core_mate, s_dm, r_dm)
    d_proj = d_proj + features(core_mate)
    relayed(dm_full, diagonal, s_dm, r_dm)
    d_proj = (d_proj + features(diagonal)).astype(BF16)
    for h in range(HEAD_GRP):
        dp_send[h] = d_proj[:, h * HD : (h + 1) * HD]
        send(
            b != owners[h],
            lambda h=h: remote(
                dp_send.at[h], do_in.at[b], s_do.at[h], r_do.at[b], {"blk": owners[h]}
            ),
        )

        @pl.when(b == owners[h])
        def _(h=h):
            do_in[b] = dp_send[h]

    my_rows = pl.ds(pl.multiple_of(g * quarter, quarter), quarter)
    for t in range(blocks):
        lo = t * cols
        view = (lo // feat, my_rows, slice(lo % feat, lo % feat + cols))
        send(
            b != t,
            lambda t=t, view=view: remote(
                dm_full.at[view], d_cols.at[g, b], s_ca.at[t], r_ca.at[b], {"blk": t}
            ),
        )

        @pl.when(b == t)
        def _(view=view):
            d_cols[g, b] = dm_full[view]

    def own_part(i, ref):
        for t in range(blocks):

            @pl.when(b != t)
            def _(t=t):
                remote(
                    qkv_in.at[i, t], qkv_in.at[i, t], s_qkv.at[i, 0], r_qkv.at[i, t], {"blk": t}
                ).wait_recv()

        own_tile(i, ref, (slice(None), slice(0, HD))).wait()

    @pl.when(is_owner)
    def _():
        own_part(0, q_ref)
        for i in range(chunks):
            q_main[i] = dot(place_t[i], qkv_in[0].reshape(seq, HD), 1, 0).astype(BF16)
        own_part(1, k_ref)
        k_t[...] = jnp.transpose(qkv_in[1].reshape(seq, HD).astype(F32)).astype(BF16)
        own_part(2, v_ref)
        v_t[...] = jnp.transpose(qkv_in[2].reshape(seq, HD).astype(F32)).astype(BF16)

    for i in range(chunks):

        @pl.when(is_owner)
        def _(i=i):
            raw = dot(qkv_in[1].reshape(seq, HD), q_main[i], 1, 1)
            peak = jnp.max(raw, axis=0, keepdims=True)
            e = jnp.exp2((raw - peak) * (scale * math.log2(math.e)))
            p = (e * (1.0 / jnp.sum(e, axis=0, keepdims=True))).astype(BF16)
            probs[i] = p
            att = dot(v_t[...], p, 1, 0).astype(BF16)
            for n in range(per):
                att_send[i * per + n] = att[:, n * rows : (n + 1) * rows]

        for t in range(i * per, (i + 1) * per):
            send(
                is_owner & (b != t),
                lambda t=t: remote(
                    att_send.at[t], att_all.at[t, mine], s_at.at[t], r_at.at[mine], {"blk": t}
                ),
            )

    @pl.when(is_owner)
    def _():
        att_all[b, mine] = att_send[b]

    for t in range(blocks):
        arrive(
            b != t,
            lambda t=t: remote(
                d_cols.at[g, t], d_cols.at[g, t], s_ca.at[t], r_ca.at[t], {"blk": t}
            ),
        )
    relay(d_cols.at[g], d_cols, g, y_mate, s_cb.at[0], r_cb)
    relay(d_cols.at[g], d_cols, g, core_mate, s_cb.at[1], r_cb)

    def send_grads(n, first, count):
        for t in range(first, first + count):
            send(
                is_owner & (b != t),
                lambda t=t: remote(
                    grad_send.at[n, t], grad_in.at[n, mine], s_gr.at[n, t], r_gr.at[n, mine], {"blk": t}
                ),
            )

    def backward(j):
        @pl.when(is_owner)
        def _():
            if j == 0:
                for t in range(blocks):

                    @pl.when(b != t)
                    def _(t=t):
                        remote(
                            do_in.at[t], do_in.at[t], s_do.at[0], r_do.at[t], {"blk": t}
                        ).wait_recv()

                for t in range(blocks):
                    both = jnp.transpose(do_in[t].astype(F32)) * att_send[t].astype(F32)
                    delta_row[:, t * rows : (t + 1) * rows] = jnp.sum(both, axis=0, keepdims=True)
            do = do_in[...].reshape(seq, HD)
            p = jnp.concatenate(
                [probs[i, j * step : (j + 1) * step] for i in range(chunks)], axis=1
            )
            d_probs = dot(qkv_in[2, j * per : (j + 1) * per].reshape(step, HD), do, 1, 1)
            ds = (p.astype(F32) * (d_probs - delta_row[...])).astype(BF16)
            dk = (dot(ds, q_main[...].reshape(seq, HD), 1, 0) * scale).astype(BF16)
            dv = dot(p, do, 1, 0).astype(BF16)
            grad_send[1, j * per : (j + 1) * per] = dk.reshape(per, rows, HD)
            grad_send[2, j * per : (j + 1) * per] = dv.reshape(per, rows, HD)
            dq_t = dot(k_t[:, j * step : (j + 1) * step], ds, 1, 0)
            if j == 0:
                dq_acc[...] = dq_t
            elif j < chunks - 1:
                dq_acc[...] += dq_t
            else:
                dq_main[...] = jnp.transpose((dq_acc[...] + dq_t) * scale).astype(BF16)

        send_grads(1, j * per, per)
        send_grads(2, j * per, per)

    backward(0)
    for h in range(HEAD_GRP):
        arrive(
            b != owners[h],
            lambda h=h: remote(
                att_all.at[b, h], att_all.at[b, h], s_at.at[0], r_at.at[h], {"blk": owners[h]}
            ),
        )

    def pass_on(cond, slot, dev, sem):
        send(
            cond,
            lambda: remote(att_all.at[slot], att_all.at[slot], s_ag.at[sem], r_ag.at[slot], {"blk": dev}),
        )

    def landed(cond, slot):
        arrive(
            cond,
            lambda: remote(att_all.at[slot], att_all.at[slot], s_ag.at[0], r_ag.at[slot], {"blk": mate}),
        )

    pass_on(z < nz - 1, b, b + 2, 0)
    pass_on(z > 0, b, b - 2, 1)
    pass_on(always, b, mate, 2)

    def gather_step(s):
        if s >= nz:
            return
        low, high = z >= s, z + s < nz
        landed(low, b - 2 * s)
        pass_on(low & (z < nz - 1), b - 2 * s, b + 2, 4 * s)
        pass_on(low, b - 2 * s, mate, 4 * s + 1)
        landed(high, b + 2 * s)
        pass_on(high & (z > 0), b + 2 * s, b - 2, 4 * s + 2)
        pass_on(high, b + 2 * s, mate, 4 * s + 3)

    backward(1)
    gather_step(1)
    relayed(d_cols, y_mate, s_cb, r_cb)
    relay(d_cols.at[y_mate], d_cols, y_mate, core_mate, s_cb.at[2], r_cb)

    own = jnp.concatenate([att_all[b, h] for h in range(HEAD_GRP)], axis=0)
    own = jnp.transpose(own.astype(F32)).astype(BF16)
    for p in range(n_grp):
        rs_send[p] = dot(own, w_ref[:, p * feat : (p + 1) * feat], 1, 0).astype(BF16)
    for n, p in enumerate((diagonal, core_mate)):
        send(
            always,
            lambda n=n, p=p: remote(
                rs_send.at[p], rs_in.at[n], s_rs.at[n], r_rs.at[n], {"grp": core_mate}
            ),
        )

    def rs_landed(n):
        arrive(always, lambda: remote(rs_in.at[n], rs_in.at[n], s_rs.at[0], r_rs.at[n], {"grp": y_mate}))

    backward(2)
    gather_step(2)
    rs_landed(0)
    rs_pass[...] = (rs_send[y_mate].astype(F32) + rs_in[0].astype(F32)).astype(BF16)
    send(
        always,
        lambda: remote(rs_pass, rs_in.at[2], s_rs.at[2], r_rs.at[2], {"grp": y_mate}),
    )
    backward(3)

    @pl.when(is_owner)
    def _():
        turned = dot(place[...].reshape(seq, seq), dq_main[...], 1, 0)
        grad_send[0] = turned.astype(BF16).reshape(blocks, rows, HD)

    send_grads(0, 0, blocks)
    gather_step(3)

    @pl.when(is_owner)
    def _():
        for n in range(3):
            grad_in[n, mine] = grad_send[n, b]

    rs_landed(1)
    rs_landed(2)
    loads[3].wait()
    total = rs_send[g].astype(F32) + rs_in[1].astype(F32) + rs_in[2].astype(F32)
    mixed_ref[...] = (hidden_ref[...].astype(F32) + total).astype(BF16)
    write(mixed_ref, mixed_out)

    relayed(d_cols, core_mate, s_cb, r_cb)
    relayed(d_cols, diagonal, s_cb, r_cb)
    for j in range(nz):
        landed(always, 2 * j + 1 - x)
    grads = jnp.concatenate(
        [d_cols[p, t] for t in range(blocks) for p in range(n_grp)], axis=0
    )
    for h in range(HEAD_GRP):
        att = jnp.concatenate([att_all[t, h] for t in range(blocks)], axis=1)
        dw_ref[h] = dot(att, grads, 1, 0)
        write(dw_ref.at[h], dw_out.at[h * HD : (h + 1) * HD])

    for n, out in enumerate((dq_out, dk_out, dv_out)):
        for h in range(HEAD_GRP):
            arrive(
                b != owners[h],
                lambda n=n, h=h: remote(
                    grad_in.at[n, h], grad_in.at[n, h], s_gr.at[n, 0], r_gr.at[n, h], {"blk": owners[h]}
                ),
            )
            write(grad_in.at[n, h], out.at[:, h * HD : (h + 1) * HD])

    for copy in writes:
        copy.wait()
    for cond, make in pending:
        pl.when(cond)(lambda make=make: make().wait_send())


def write_kernel(*refs):
    srcs, dsts, held, into, out = refs[:5], refs[5:10], refs[10:15], refs[15], refs[16]
    loads = [pltpu.make_async_copy(srcs[i], held[i], into.at[i]) for i in range(5)]
    stores = [pltpu.make_async_copy(held[i], dsts[i], out.at[i]) for i in range(5)]
    for load in loads:
        load.start()
    for load, store in zip(loads, stores):
        load.wait()
        store.start()
    for store in stores:
        store.wait()


def on_device_fused(main_hidden, ctrl_query, ctrl_key, ctrl_value, w_out, d_mixed, control_slot):
    n_grp, blocks = lax.axis_size("grp"), lax.axis_size("blk")
    rows, feat = d_mixed.shape
    width, model = w_out.shape
    cols = model // blocks
    seq = rows * blocks
    step = seq // 4
    dma = pltpu.SemaphoreType.DMA
    sems = [
        dma((n_grp,)), dma((3, HEAD_GRP)), dma((HEAD_GRP,)), dma((HEAD_GRP,)), dma((blocks,)),
        dma((n_grp,)), dma((blocks,)), dma((2 * blocks,)), dma((n_grp,)), dma((3, blocks)), dma((7,)), dma((16,)),
        dma((n_grp,)), dma((3, blocks)), dma((blocks,)), dma((blocks,)), dma((blocks,)),
        dma((n_grp,)), dma((HEAD_GRP,)), dma((blocks,)), dma((n_grp,)), dma((3, HEAD_GRP)),
    ]
    hbm = pl.BlockSpec(memory_space=pltpu.HBM)
    tile = jax.ShapeDtypeStruct((rows, width), BF16)
    results = pl.pallas_call(
        fused_kernel,
        out_shape=(
            jax.ShapeDtypeStruct((rows, feat), BF16), tile, tile, tile,
            jax.ShapeDtypeStruct((width, cols), F32),
        ),
        in_specs=[hbm] * 7,
        out_specs=[hbm] * 5,
        scratch_shapes=[
            pltpu.VMEM((rows, feat), BF16),
            pltpu.VMEM((HEAD_GRP, HD, cols), F32),
            pltpu.VMEM((rows, feat), BF16),
            pltpu.VMEM((width, model), BF16),
            pltpu.VMEM((n_grp, rows, feat), BF16),
            pltpu.VMEM((3, blocks, rows, HD), BF16),
            pltpu.VMEM((blocks, 1, rows), jnp.int32),
            pltpu.VMEM((HEAD_GRP, rows, HD), BF16),
            pltpu.VMEM((blocks, rows, HD), BF16),
            pltpu.VMEM((4, step, HD), BF16),
            pltpu.VMEM((n_grp, blocks, rows // n_grp, cols), BF16),
            pltpu.VMEM((4, seq, step), BF16),
            pltpu.VMEM((4, step, seq), BF16),
            pltpu.VMEM((4, step, seq), BF16),
            pltpu.VMEM((HD, seq), BF16),
            pltpu.VMEM((HD, seq), BF16),
            pltpu.VMEM((seq, HD), BF16),
            pltpu.VMEM((blocks, rows, HD), BF16),
            pltpu.VMEM((blocks, HEAD_GRP, rows, HD), BF16),
            pltpu.VMEM((n_grp, rows, feat), BF16),
            pltpu.VMEM((rows, feat), BF16),
            pltpu.VMEM((3, rows, feat), BF16),
            pltpu.VMEM((HD, seq), F32),
            pltpu.VMEM((1, seq), F32),
            pltpu.VMEM((3, blocks, rows, HD), BF16),
            pltpu.VMEM((3, HEAD_GRP, rows, HD), BF16),
        ] + sems,
        compiler_params=pltpu.CompilerParams(
            collective_id=0, has_side_effects=True, vmem_limit_bytes=60 * 2**20
        ),
        cost_estimate=pl.CostEstimate(
            flops=2 * 5 * seq * seq * HD, bytes_accessed=16 * 2**20, transcendentals=seq * seq
        ),
    )(
        main_hidden, ctrl_query, ctrl_key, ctrl_value, w_out, d_mixed,
        control_slot.reshape(1, rows),
    )
    return pl.pallas_call(
        write_kernel,
        out_shape=tuple(jax.ShapeDtypeStruct(r.shape, r.dtype) for r in results),
        in_specs=[hbm] * 5,
        out_specs=[hbm] * 5,
        scratch_shapes=[pltpu.VMEM(r.shape, r.dtype) for r in results] + [dma((5,)), dma((5,))],
        compiler_params=pltpu.CompilerParams(vmem_limit_bytes=60 * 2**20),
    )(*results)


def solution(mesh):
    in_specs = (
        P("blk", "grp"),
        P("blk", "grp"),
        P("blk", "grp"),
        P("blk", "grp"),
        P("grp", None),
        P("blk", "grp"),
        P("blk"),
    )
    out_specs = (
        P("blk", "grp"),
        P("blk", "grp"),
        P("blk", "grp"),
        P("blk", "grp"),
        P("grp", "blk"),
    )
    body = on_device_fused if mesh.shape["blk"] == 8 else on_device
    return jax.shard_map(
        body, mesh=mesh, in_specs=in_specs, out_specs=out_specs, check_vma=False
    )
```

```python
import functools
import math

import jax
import jax.numpy as jnp
from jax import lax
from jax.experimental import pallas as pl
from jax.experimental.pallas import tpu as pltpu
from jax.sharding import PartitionSpec as P

HD = 128
HEAD_GRP = 3


def on_device(main_hidden, ctrl_query, ctrl_key, ctrl_value, w_out, d_mixed, control_slot):
    rows_dev = ctrl_query.shape[0]
    feature_cols = d_mixed.shape[1]
    blocks = lax.axis_size("blk")
    per_peer = rows_dev // blocks
    score_scale = 1.0 / math.sqrt(HD)
    whole_key, whole_value = (
        lax.all_gather(ctrl_key, "blk", axis=0, tiled=True),
        lax.all_gather(ctrl_value, "blk", axis=0, tiled=True),
    )
    outputs = []
    norm_list = []
    for head_idx in range(HEAD_GRP):
        columns = slice(head_idx * HD, (head_idx + 1) * HD)
        scores = (
            jnp.dot(
                ctrl_query[:, columns], whole_key[:, columns].T, preferred_element_type=jnp.float32
            )
            * score_scale
        )
        row_peak = jnp.max(scores, axis=1, keepdims=True)
        log_norm = row_peak + jnp.log(jnp.sum(jnp.exp(scores - row_peak), axis=1, keepdims=True))
        soft_weights = jnp.exp(scores - log_norm).astype(jnp.bfloat16)
        outputs.append(
            jnp.dot(soft_weights, whole_value[:, columns], preferred_element_type=jnp.float32)
        )
        norm_list.append(log_norm[:, 0])
    attended = jnp.concatenate(outputs, axis=1).astype(jnp.bfloat16)
    log_norms = jnp.stack(norm_list, axis=1)
    target = control_slot // rows_dev
    within = control_slot % rows_dev
    sort_order = jnp.argsort(target)
    inverse = jnp.argsort(sort_order)
    send_within = within[sort_order].reshape(blocks, per_peer)
    arrived, arrived_grad = (
        lax.all_to_all(send_within, "blk", split_axis=0, concat_axis=0, tiled=True),
        lax.all_to_all(
            d_mixed[sort_order].reshape(blocks, per_peer, feature_cols),
            "blk",
            split_axis=0,
            concat_axis=0,
            tiled=True,
        ),
    )
    placed = arrived.reshape(rows_dev)
    grad_rows = jnp.zeros_like(d_mixed).at[placed].set(arrived_grad.reshape(rows_dev, feature_cols))
    residual = lax.psum_scatter(
        jnp.dot(attended, w_out, preferred_element_type=jnp.float32).astype(jnp.bfloat16),
        "grp",
        scatter_dimension=1,
        tiled=True,
    ).astype(jnp.float32)
    returned = lax.all_to_all(
        residual[placed].reshape(blocks, per_peer, feature_cols),
        "blk",
        split_axis=0,
        concat_axis=0,
        tiled=True,
    )
    residual = returned.reshape(rows_dev, feature_cols)[inverse]
    main_mixed = (main_hidden.astype(jnp.float32) + residual).astype(jnp.bfloat16)
    grad_full = lax.all_gather(grad_rows, "grp", axis=1, tiled=True)
    d_proj = jnp.dot(grad_full, w_out.T, preferred_element_type=jnp.float32).astype(jnp.bfloat16)
    d_w_out = lax.psum_scatter(
        jnp.dot(attended.T, grad_full, preferred_element_type=jnp.float32),
        "blk",
        scatter_dimension=1,
        tiled=True,
    )
    row_delta = jnp.sum(
        (d_proj.astype(jnp.float32) * attended.astype(jnp.float32)).reshape(rows_dev, HEAD_GRP, HD),
        axis=2,
    )
    all_norms, all_delta = (
        lax.all_gather(log_norms, "blk", axis=0, tiled=True),
        lax.all_gather(row_delta, "blk", axis=0, tiled=True),
    )
    query_grads = []
    for head_idx in range(HEAD_GRP):
        columns = slice(head_idx * HD, (head_idx + 1) * HD)
        scores = (
            jnp.dot(
                ctrl_query[:, columns], whole_key[:, columns].T, preferred_element_type=jnp.float32
            )
            * score_scale
        )
        soft_weights = jnp.exp(scores - log_norms[:, head_idx : head_idx + 1])
        d_probs = jnp.dot(
            d_proj[:, columns], whole_value[:, columns].T, preferred_element_type=jnp.float32
        )
        d_scores = (soft_weights * (d_probs - row_delta[:, head_idx : head_idx + 1])).astype(
            jnp.bfloat16
        )
        query_grads.append(
            jnp.dot(d_scores, whole_key[:, columns], preferred_element_type=jnp.float32)
            * score_scale
        )
    d_query = jnp.concatenate(query_grads, axis=1).astype(jnp.bfloat16)
    query_piece = lax.all_gather(ctrl_query, "blk", axis=0, tiled=True)
    grad_piece = lax.all_gather(d_proj, "blk", axis=0, tiled=True)
    key_terms = []
    value_terms = []
    for head_idx in range(HEAD_GRP):
        columns = slice(head_idx * HD, (head_idx + 1) * HD)
        scores = (
            jnp.dot(
                query_piece[:, columns], ctrl_key[:, columns].T, preferred_element_type=jnp.float32
            )
            * score_scale
        )
        soft_weights = jnp.exp(scores - all_norms[:, head_idx : head_idx + 1])
        d_probs = jnp.dot(
            grad_piece[:, columns], ctrl_value[:, columns].T, preferred_element_type=jnp.float32
        )
        d_scores = (soft_weights * (d_probs - all_delta[:, head_idx : head_idx + 1])).astype(
            jnp.bfloat16
        )
        key_terms.append(
            jnp.dot(d_scores.T, query_piece[:, columns], preferred_element_type=jnp.float32)
            * score_scale
        )
        value_terms.append(
            jnp.dot(
                soft_weights.astype(jnp.bfloat16).T,
                grad_piece[:, columns],
                preferred_element_type=jnp.float32,
            )
        )
    key_grad = jnp.concatenate(key_terms, axis=1)
    value_grad = jnp.concatenate(value_terms, axis=1)
    return (
        main_mixed,
        d_query,
        key_grad.astype(jnp.bfloat16),
        value_grad.astype(jnp.bfloat16),
        d_w_out,
    )


F32, BF16 = jnp.float32, jnp.bfloat16


def dot(a, b, ca, cb):
    return lax.dot_general(a, b, (((ca,), (cb,)), ((), ())), preferred_element_type=F32)


def fused_kernel(
    hidden_hbm, q_ref, k_ref, v_ref, w_hbm, dm_ref, slot_ref,
    mixed_out, dq_out, dk_out, dv_out, dw_out, mixed_ref, dw_ref, hidden_ref, w_ref,
    dm_full, qkv_in, slots_in, dp_send, do_in, q_main, d_cols,
    probs, place, place_t, k_t, v_t, dq_main, att_send, att_all, rs_send, rs_pass, rs_in,
    dk_acc, dv_acc, grad_send, grad_in,
    s_dm, s_qkv, s_slot, s_do, s_ca, s_cb, s_at, s_ag, s_rs, s_gr, s_in, s_out,
    r_dm, r_qkv, r_slot, r_do, r_ca, r_cb, r_at, r_ag, r_rs, r_gr,
):
    g = lax.axis_index("grp")
    b = lax.axis_index("blk")
    n_grp, blocks = dm_full.shape[0], qkv_in.shape[1]
    rows, feat = dm_ref.shape
    cols = d_cols.shape[3]
    quarter = rows // n_grp
    seq = rows * blocks
    chunks = 4
    per = blocks // chunks
    step = seq // chunks
    scale = 1.0 / math.sqrt(HD)
    c = g % 2
    z, x = b // 2, b % 2
    nz = blocks // 2
    mate = b + 1 - 2 * x
    core_mate, y_mate, diagonal = g + 1 - 2 * c, (g + 2) % n_grp, n_grp - 1 - g
    owners = [2 + 2 * c, 5 - 5 * c, 3 + 4 * c]
    mine = jnp.where(b == owners[1], 1, jnp.where(b == owners[2], 2, 0))
    is_owner = (b == owners[0]) | (b == owners[1]) | (b == owners[2])
    always = b >= 0
    pending = []
    writes = []

    def write(src, dst):
        copy = pltpu.make_async_copy(src, dst, s_out.at[len(writes)])
        copy.start()
        writes.append(copy)

    def remote(src, dst, ss, rs, dev):
        return pltpu.make_async_remote_copy(
            src_ref=src, dst_ref=dst, send_sem=ss, recv_sem=rs,
            device_id=dev, device_id_type=pl.DeviceIdType.MESH,
        )

    def send(cond, make):
        pl.when(cond)(lambda: make().start())
        pending.append((cond, make))

    def arrive(cond, make):
        pl.when(cond)(lambda: make().wait_recv())

    loads = [
        pltpu.make_async_copy(dm_ref, dm_full.at[g], s_in.at[0]),
        pltpu.make_async_copy(w_hbm, w_ref, s_in.at[1]),
        pltpu.make_async_copy(slot_ref, slots_in.at[b], s_in.at[2]),
        pltpu.make_async_copy(hidden_hbm, hidden_ref, s_in.at[3]),
    ]
    for load in loads:
        load.start()

    def own_tile(i, ref, tile):
        return pltpu.make_async_copy(ref.at[tile], qkv_in.at[i, b], s_in.at[4 + i])

    barrier = pltpu.get_barrier_semaphore()
    for d in range(1, n_grp):
        pl.semaphore_signal(
            barrier, inc=1, device_id={"grp": (g + d) % n_grp}, device_id_type=pl.DeviceIdType.MESH
        )
    for d in range(1, blocks):
        pl.semaphore_signal(
            barrier, inc=1, device_id={"blk": (b + d) % blocks}, device_id_type=pl.DeviceIdType.MESH
        )
    pl.semaphore_wait(barrier, n_grp + blocks - 2)

    def relay(src, buf, slot, dev, ss, rs):
        send(always, lambda: remote(src, buf.at[slot], ss, rs.at[slot], {"grp": dev}))

    def relayed(buf, slot, ss, rs):
        arrive(always, lambda: remote(buf.at[slot], buf.at[slot], ss.at[0], rs.at[slot], {"grp": y_mate}))

    relay(dm_ref, dm_full, g, y_mate, s_dm.at[0], r_dm)
    relay(dm_ref, dm_full, g, core_mate, s_dm.at[1], r_dm)
    for i, ref in enumerate((q_ref, k_ref, v_ref)):
        for h in range(HEAD_GRP):
            tile = (slice(None), slice(h * HD, (h + 1) * HD))
            send(
                b != owners[h],
                lambda i=i, ref=ref, h=h, tile=tile: remote(
                    ref.at[tile], qkv_in.at[i, b], s_qkv.at[i, h], r_qkv.at[i, b], {"blk": owners[h]}
                ),
            )

            @pl.when(b == owners[h])
            def _(i=i, ref=ref, tile=tile):
                own_tile(i, ref, tile).start()

    for h in range(HEAD_GRP):
        send(
            b != owners[h],
            lambda h=h: remote(
                slot_ref, slots_in.at[b], s_slot.at[h], r_slot.at[b], {"blk": owners[h]}
            ),
        )

    loads[2].wait()

    @pl.when(is_owner)
    def _():
        for t in range(blocks):

            @pl.when(b != t)
            def _(t=t):
                remote(slot_ref, slots_in.at[t], s_slot.at[0], r_slot.at[t], {"blk": t}).wait_recv()

        slot_row = jnp.concatenate([slots_in[t] for t in range(blocks)], axis=1)
        slot_col = jnp.transpose(jnp.broadcast_to(slot_row.astype(F32), (8, seq)))[:, :1]
        lane = lax.broadcasted_iota(jnp.int32, (step, seq), 1)
        for i in range(chunks):
            at = lax.broadcasted_iota(jnp.int32, (step, seq), 0) + i * step
            place[i] = jnp.where(at == slot_row, 1.0, 0.0).astype(BF16)
            want = slot_col[i * step : (i + 1) * step].astype(jnp.int32)
            place_t[i] = jnp.where(lane == want, 1.0, 0.0).astype(BF16)

    def features(p):
        lo = pl.multiple_of(p * feat, HD)
        return dot(dm_full[p], w_ref[:, pl.ds(lo, feat)], 1, 1)

    loads[0].wait()
    loads[1].wait()
    d_proj = features(g)
    relayed(dm_full, y_mate, s_dm, r_dm)
    relay(dm_full.at[y_mate], dm_full, y_mate, core_mate, s_dm.at[2], r_dm)
    d_proj = d_proj + features(y_mate)
    relayed(dm_full, core_mate, s_dm, r_dm)
    d_proj = d_proj + features(core_mate)
    relayed(dm_full, diagonal, s_dm, r_dm)
    d_proj = (d_proj + features(diagonal)).astype(BF16)
    for h in range(HEAD_GRP):
        dp_send[h] = d_proj[:, h * HD : (h + 1) * HD]
        send(
            b != owners[h],
            lambda h=h: remote(
                dp_send.at[h], do_in.at[b], s_do.at[h], r_do.at[b], {"blk": owners[h]}
            ),
        )

        @pl.when(b == owners[h])
        def _(h=h):
            do_in[b] = dp_send[h]

    my_rows = pl.ds(pl.multiple_of(g * quarter, quarter), quarter)
    for t in range(blocks):
        lo = t * cols
        view = (lo // feat, my_rows, slice(lo % feat, lo % feat + cols))
        send(
            b != t,
            lambda t=t, view=view: remote(
                dm_full.at[view], d_cols.at[g, b], s_ca.at[t], r_ca.at[b], {"blk": t}
            ),
        )

        @pl.when(b == t)
        def _(view=view):
            d_cols[g, b] = dm_full[view]

    def own_part(i, ref):
        for t in range(blocks):

            @pl.when(b != t)
            def _(t=t):
                remote(
                    qkv_in.at[i, t], qkv_in.at[i, t], s_qkv.at[i, 0], r_qkv.at[i, t], {"blk": t}
                ).wait_recv()

        own_tile(i, ref, (slice(None), slice(0, HD))).wait()

    @pl.when(is_owner)
    def _():
        own_part(0, q_ref)
        for i in range(chunks):
            q_main[i] = dot(place_t[i], qkv_in[0].reshape(seq, HD), 1, 0).astype(BF16)
        own_part(1, k_ref)
        k_t[...] = jnp.transpose(qkv_in[1].reshape(seq, HD).astype(F32)).astype(BF16)
        own_part(2, v_ref)
        v_t[...] = jnp.transpose(qkv_in[2].reshape(seq, HD).astype(F32)).astype(BF16)

    for i in range(chunks):

        @pl.when(is_owner)
        def _(i=i):
            raw = dot(qkv_in[1].reshape(seq, HD), q_main[i], 1, 1)
            peak = jnp.max(raw, axis=0, keepdims=True)
            e = jnp.exp2((raw - peak) * (scale * math.log2(math.e)))
            p = (e * (1.0 / jnp.sum(e, axis=0, keepdims=True))).astype(BF16)
            probs[i] = p
            att = dot(v_t[...], p, 1, 0).astype(BF16)
            for n in range(per):
                att_send[i * per + n] = att[:, n * rows : (n + 1) * rows]

        for t in range(i * per, (i + 1) * per):
            send(
                is_owner & (b != t),
                lambda t=t: remote(
                    att_send.at[t], att_all.at[t, mine], s_at.at[t], r_at.at[mine], {"blk": t}
                ),
            )

    @pl.when(is_owner)
    def _():
        att_all[b, mine] = att_send[b]

    for t in range(blocks):
        arrive(
            b != t,
            lambda t=t: remote(
                d_cols.at[g, t], d_cols.at[g, t], s_ca.at[t], r_ca.at[t], {"blk": t}
            ),
        )
    relay(d_cols.at[g], d_cols, g, y_mate, s_cb.at[0], r_cb)
    relay(d_cols.at[g], d_cols, g, core_mate, s_cb.at[1], r_cb)

    def backward(i):
        @pl.when(is_owner)
        def _():
            for t in range(i * per, (i + 1) * per):

                @pl.when(b != t)
                def _(t=t):
                    remote(do_in.at[t], do_in.at[t], s_do.at[0], r_do.at[t], {"blk": t}).wait_recv()

            do = do_in[i * per : (i + 1) * per].reshape(step, HD)
            delta = jnp.concatenate(
                [
                    jnp.sum(
                        jnp.transpose(do_in[t].astype(F32)) * att_send[t].astype(F32),
                        axis=0, keepdims=True,
                    )
                    for t in range(i * per, (i + 1) * per)
                ],
                axis=1,
            )
            p = probs[i]
            d_probs = dot(qkv_in[2].reshape(seq, HD), do, 1, 1)
            ds = (p.astype(F32) * (d_probs - delta)).astype(BF16)
            dq_main[i] = jnp.transpose(dot(k_t[...], ds, 1, 0) * scale).astype(BF16)
            dk = dot(ds, q_main[i], 1, 0)
            dv = dot(p, do, 1, 0)
            if i == 0:
                dk_acc[...] = dk
                dv_acc[...] = dv
            elif i < chunks - 1:
                dk_acc[...] += dk
                dv_acc[...] += dv
            else:
                dk = ((dk_acc[...] + dk) * scale).astype(BF16)
                grad_send[1] = dk.reshape(blocks, rows, HD)
                grad_send[2] = (dv_acc[...] + dv).astype(BF16).reshape(blocks, rows, HD)

    def send_grads(n):
        for t in range(blocks):
            send(
                is_owner & (b != t),
                lambda t=t: remote(
                    grad_send.at[n, t], grad_in.at[n, mine], s_gr.at[n, t], r_gr.at[n, mine], {"blk": t}
                ),
            )

    backward(0)
    for h in range(HEAD_GRP):
        arrive(
            b != owners[h],
            lambda h=h: remote(
                att_all.at[b, h], att_all.at[b, h], s_at.at[0], r_at.at[h], {"blk": owners[h]}
            ),
        )

    def pass_on(cond, slot, dev, sem):
        send(
            cond,
            lambda: remote(att_all.at[slot], att_all.at[slot], s_ag.at[sem], r_ag.at[slot], {"blk": dev}),
        )

    def landed(cond, slot):
        arrive(
            cond,
            lambda: remote(att_all.at[slot], att_all.at[slot], s_ag.at[0], r_ag.at[slot], {"blk": mate}),
        )

    pass_on(z < nz - 1, b, b + 2, 0)
    pass_on(z > 0, b, b - 2, 1)
    pass_on(always, b, mate, 2)

    def gather_step(s):
        if s >= nz:
            return
        low, high = z >= s, z + s < nz
        landed(low, b - 2 * s)
        pass_on(low & (z < nz - 1), b - 2 * s, b + 2, 4 * s)
        pass_on(low, b - 2 * s, mate, 4 * s + 1)
        landed(high, b + 2 * s)
        pass_on(high & (z > 0), b + 2 * s, b - 2, 4 * s + 2)
        pass_on(high, b + 2 * s, mate, 4 * s + 3)

    gather_step(1)
    backward(1)
    relayed(d_cols, y_mate, s_cb, r_cb)
    relay(d_cols.at[y_mate], d_cols, y_mate, core_mate, s_cb.at[2], r_cb)

    own = jnp.concatenate([att_all[b, h] for h in range(HEAD_GRP)], axis=0)
    own = jnp.transpose(own.astype(F32)).astype(BF16)
    for p in range(n_grp):
        rs_send[p] = dot(own, w_ref[:, p * feat : (p + 1) * feat], 1, 0).astype(BF16)
    for n, p in enumerate((diagonal, core_mate)):
        send(
            always,
            lambda n=n, p=p: remote(
                rs_send.at[p], rs_in.at[n], s_rs.at[n], r_rs.at[n], {"grp": core_mate}
            ),
        )

    def rs_landed(n):
        arrive(always, lambda: remote(rs_in.at[n], rs_in.at[n], s_rs.at[0], r_rs.at[n], {"grp": y_mate}))

    gather_step(2)
    backward(2)
    rs_landed(0)
    rs_pass[...] = (rs_send[y_mate].astype(F32) + rs_in[0].astype(F32)).astype(BF16)
    send(
        always,
        lambda: remote(rs_pass, rs_in.at[2], s_rs.at[2], r_rs.at[2], {"grp": y_mate}),
    )
    gather_step(3)
    backward(3)
    send_grads(1)
    send_grads(2)

    @pl.when(is_owner)
    def _():
        turned = dot(place[...].reshape(seq, seq), dq_main[...].reshape(seq, HD), 1, 0)
        grad_send[0] = turned.astype(BF16).reshape(blocks, rows, HD)

    send_grads(0)

    @pl.when(is_owner)
    def _():
        for n in range(3):
            grad_in[n, mine] = grad_send[n, b]

    rs_landed(1)
    rs_landed(2)
    loads[3].wait()
    total = rs_send[g].astype(F32) + rs_in[1].astype(F32) + rs_in[2].astype(F32)
    mixed_ref[...] = (hidden_ref[...].astype(F32) + total).astype(BF16)
    write(mixed_ref, mixed_out)

    relayed(d_cols, core_mate, s_cb, r_cb)
    relayed(d_cols, diagonal, s_cb, r_cb)
    for j in range(nz):
        landed(always, 2 * j + 1 - x)
    grads = jnp.concatenate(
        [d_cols[p, t] for t in range(blocks) for p in range(n_grp)], axis=0
    )
    for h in range(HEAD_GRP):
        att = jnp.concatenate([att_all[t, h] for t in range(blocks)], axis=1)
        dw_ref[h] = dot(att, grads, 1, 0)
        write(dw_ref.at[h], dw_out.at[h * HD : (h + 1) * HD])

    for n, out in enumerate((dq_out, dk_out, dv_out)):
        for h in range(HEAD_GRP):
            arrive(
                b != owners[h],
                lambda n=n, h=h: remote(
                    grad_in.at[n, h], grad_in.at[n, h], s_gr.at[n, 0], r_gr.at[n, h], {"blk": owners[h]}
                ),
            )
            write(grad_in.at[n, h], out.at[:, h * HD : (h + 1) * HD])

    for copy in writes:
        copy.wait()
    for cond, make in pending:
        pl.when(cond)(lambda make=make: make().wait_send())


def write_kernel(*refs):
    srcs, dsts, held, into, out = refs[:5], refs[5:10], refs[10:15], refs[15], refs[16]
    loads = [pltpu.make_async_copy(srcs[i], held[i], into.at[i]) for i in range(5)]
    stores = [pltpu.make_async_copy(held[i], dsts[i], out.at[i]) for i in range(5)]
    for load in loads:
        load.start()
    for load, store in zip(loads, stores):
        load.wait()
        store.start()
    for store in stores:
        store.wait()


def on_device_fused(main_hidden, ctrl_query, ctrl_key, ctrl_value, w_out, d_mixed, control_slot):
    n_grp, blocks = lax.axis_size("grp"), lax.axis_size("blk")
    rows, feat = d_mixed.shape
    width, model = w_out.shape
    cols = model // blocks
    seq = rows * blocks
    step = seq // 4
    dma = pltpu.SemaphoreType.DMA
    sems = [
        dma((n_grp,)), dma((3, HEAD_GRP)), dma((HEAD_GRP,)), dma((HEAD_GRP,)), dma((blocks,)),
        dma((n_grp,)), dma((blocks,)), dma((2 * blocks,)), dma((n_grp,)), dma((3, blocks)), dma((7,)), dma((16,)),
        dma((n_grp,)), dma((3, blocks)), dma((blocks,)), dma((blocks,)), dma((blocks,)),
        dma((n_grp,)), dma((HEAD_GRP,)), dma((blocks,)), dma((n_grp,)), dma((3, HEAD_GRP)),
    ]
    hbm = pl.BlockSpec(memory_space=pltpu.HBM)
    tile = jax.ShapeDtypeStruct((rows, width), BF16)
    results = pl.pallas_call(
        fused_kernel,
        out_shape=(
            jax.ShapeDtypeStruct((rows, feat), BF16), tile, tile, tile,
            jax.ShapeDtypeStruct((width, cols), F32),
        ),
        in_specs=[hbm] * 7,
        out_specs=[hbm] * 5,
        scratch_shapes=[
            pltpu.VMEM((rows, feat), BF16),
            pltpu.VMEM((HEAD_GRP, HD, cols), F32),
            pltpu.VMEM((rows, feat), BF16),
            pltpu.VMEM((width, model), BF16),
            pltpu.VMEM((n_grp, rows, feat), BF16),
            pltpu.VMEM((3, blocks, rows, HD), BF16),
            pltpu.VMEM((blocks, 1, rows), jnp.int32),
            pltpu.VMEM((HEAD_GRP, rows, HD), BF16),
            pltpu.VMEM((blocks, rows, HD), BF16),
            pltpu.VMEM((4, step, HD), BF16),
            pltpu.VMEM((n_grp, blocks, rows // n_grp, cols), BF16),
            pltpu.VMEM((4, seq, step), BF16),
            pltpu.VMEM((4, step, seq), BF16),
            pltpu.VMEM((4, step, seq), BF16),
            pltpu.VMEM((HD, seq), BF16),
            pltpu.VMEM((HD, seq), BF16),
            pltpu.VMEM((4, step, HD), BF16),
            pltpu.VMEM((blocks, rows, HD), BF16),
            pltpu.VMEM((blocks, HEAD_GRP, rows, HD), BF16),
            pltpu.VMEM((n_grp, rows, feat), BF16),
            pltpu.VMEM((rows, feat), BF16),
            pltpu.VMEM((3, rows, feat), BF16),
            pltpu.VMEM((seq, HD), F32),
            pltpu.VMEM((seq, HD), F32),
            pltpu.VMEM((3, blocks, rows, HD), BF16),
            pltpu.VMEM((3, HEAD_GRP, rows, HD), BF16),
        ] + sems,
        compiler_params=pltpu.CompilerParams(
            collective_id=0, has_side_effects=True, vmem_limit_bytes=60 * 2**20
        ),
        cost_estimate=pl.CostEstimate(
            flops=2 * 5 * seq * seq * HD, bytes_accessed=16 * 2**20, transcendentals=seq * seq
        ),
    )(
        main_hidden, ctrl_query, ctrl_key, ctrl_value, w_out, d_mixed,
        control_slot.reshape(1, rows),
    )
    return pl.pallas_call(
        write_kernel,
        out_shape=tuple(jax.ShapeDtypeStruct(r.shape, r.dtype) for r in results),
        in_specs=[hbm] * 5,
        out_specs=[hbm] * 5,
        scratch_shapes=[pltpu.VMEM(r.shape, r.dtype) for r in results] + [dma((5,)), dma((5,))],
        compiler_params=pltpu.CompilerParams(vmem_limit_bytes=60 * 2**20),
    )(*results)


def solution(mesh):
    in_specs = (
        P("blk", "grp"),
        P("blk", "grp"),
        P("blk", "grp"),
        P("blk", "grp"),
        P("grp", None),
        P("blk", "grp"),
        P("blk"),
    )
    out_specs = (
        P("blk", "grp"),
        P("blk", "grp"),
        P("blk", "grp"),
        P("blk", "grp"),
        P("grp", "blk"),
    )
    body = on_device_fused if mesh.shape["blk"] == 8 else on_device
    return jax.shard_map(
        body, mesh=mesh, in_specs=in_specs, out_specs=out_specs, check_vma=False
    )
```

```python
import functools
import math

import jax
import jax.numpy as jnp
from jax import lax
from jax.experimental import pallas as pl
from jax.experimental.pallas import tpu as pltpu
from jax.sharding import PartitionSpec as P

HD = 128
HEAD_GRP = 3


def on_device(main_hidden, ctrl_query, ctrl_key, ctrl_value, w_out, d_mixed, control_slot):
    rows_dev = ctrl_query.shape[0]
    feature_cols = d_mixed.shape[1]
    blocks = lax.axis_size("blk")
    per_peer = rows_dev // blocks
    score_scale = 1.0 / math.sqrt(HD)
    whole_key, whole_value = (
        lax.all_gather(ctrl_key, "blk", axis=0, tiled=True),
        lax.all_gather(ctrl_value, "blk", axis=0, tiled=True),
    )
    outputs = []
    norm_list = []
    for head_idx in range(HEAD_GRP):
        columns = slice(head_idx * HD, (head_idx + 1) * HD)
        scores = (
            jnp.dot(
                ctrl_query[:, columns], whole_key[:, columns].T, preferred_element_type=jnp.float32
            )
            * score_scale
        )
        row_peak = jnp.max(scores, axis=1, keepdims=True)
        log_norm = row_peak + jnp.log(jnp.sum(jnp.exp(scores - row_peak), axis=1, keepdims=True))
        soft_weights = jnp.exp(scores - log_norm).astype(jnp.bfloat16)
        outputs.append(
            jnp.dot(soft_weights, whole_value[:, columns], preferred_element_type=jnp.float32)
        )
        norm_list.append(log_norm[:, 0])
    attended = jnp.concatenate(outputs, axis=1).astype(jnp.bfloat16)
    log_norms = jnp.stack(norm_list, axis=1)
    target = control_slot // rows_dev
    within = control_slot % rows_dev
    sort_order = jnp.argsort(target)
    inverse = jnp.argsort(sort_order)
    send_within = within[sort_order].reshape(blocks, per_peer)
    arrived, arrived_grad = (
        lax.all_to_all(send_within, "blk", split_axis=0, concat_axis=0, tiled=True),
        lax.all_to_all(
            d_mixed[sort_order].reshape(blocks, per_peer, feature_cols),
            "blk",
            split_axis=0,
            concat_axis=0,
            tiled=True,
        ),
    )
    placed = arrived.reshape(rows_dev)
    grad_rows = jnp.zeros_like(d_mixed).at[placed].set(arrived_grad.reshape(rows_dev, feature_cols))
    residual = lax.psum_scatter(
        jnp.dot(attended, w_out, preferred_element_type=jnp.float32).astype(jnp.bfloat16),
        "grp",
        scatter_dimension=1,
        tiled=True,
    ).astype(jnp.float32)
    returned = lax.all_to_all(
        residual[placed].reshape(blocks, per_peer, feature_cols),
        "blk",
        split_axis=0,
        concat_axis=0,
        tiled=True,
    )
    residual = returned.reshape(rows_dev, feature_cols)[inverse]
    main_mixed = (main_hidden.astype(jnp.float32) + residual).astype(jnp.bfloat16)
    grad_full = lax.all_gather(grad_rows, "grp", axis=1, tiled=True)
    d_proj = jnp.dot(grad_full, w_out.T, preferred_element_type=jnp.float32).astype(jnp.bfloat16)
    d_w_out = lax.psum_scatter(
        jnp.dot(attended.T, grad_full, preferred_element_type=jnp.float32),
        "blk",
        scatter_dimension=1,
        tiled=True,
    )
    row_delta = jnp.sum(
        (d_proj.astype(jnp.float32) * attended.astype(jnp.float32)).reshape(rows_dev, HEAD_GRP, HD),
        axis=2,
    )
    all_norms, all_delta = (
        lax.all_gather(log_norms, "blk", axis=0, tiled=True),
        lax.all_gather(row_delta, "blk", axis=0, tiled=True),
    )
    query_grads = []
    for head_idx in range(HEAD_GRP):
        columns = slice(head_idx * HD, (head_idx + 1) * HD)
        scores = (
            jnp.dot(
                ctrl_query[:, columns], whole_key[:, columns].T, preferred_element_type=jnp.float32
            )
            * score_scale
        )
        soft_weights = jnp.exp(scores - log_norms[:, head_idx : head_idx + 1])
        d_probs = jnp.dot(
            d_proj[:, columns], whole_value[:, columns].T, preferred_element_type=jnp.float32
        )
        d_scores = (soft_weights * (d_probs - row_delta[:, head_idx : head_idx + 1])).astype(
            jnp.bfloat16
        )
        query_grads.append(
            jnp.dot(d_scores, whole_key[:, columns], preferred_element_type=jnp.float32)
            * score_scale
        )
    d_query = jnp.concatenate(query_grads, axis=1).astype(jnp.bfloat16)
    query_piece = lax.all_gather(ctrl_query, "blk", axis=0, tiled=True)
    grad_piece = lax.all_gather(d_proj, "blk", axis=0, tiled=True)
    key_terms = []
    value_terms = []
    for head_idx in range(HEAD_GRP):
        columns = slice(head_idx * HD, (head_idx + 1) * HD)
        scores = (
            jnp.dot(
                query_piece[:, columns], ctrl_key[:, columns].T, preferred_element_type=jnp.float32
            )
            * score_scale
        )
        soft_weights = jnp.exp(scores - all_norms[:, head_idx : head_idx + 1])
        d_probs = jnp.dot(
            grad_piece[:, columns], ctrl_value[:, columns].T, preferred_element_type=jnp.float32
        )
        d_scores = (soft_weights * (d_probs - all_delta[:, head_idx : head_idx + 1])).astype(
            jnp.bfloat16
        )
        key_terms.append(
            jnp.dot(d_scores.T, query_piece[:, columns], preferred_element_type=jnp.float32)
            * score_scale
        )
        value_terms.append(
            jnp.dot(
                soft_weights.astype(jnp.bfloat16).T,
                grad_piece[:, columns],
                preferred_element_type=jnp.float32,
            )
        )
    key_grad = jnp.concatenate(key_terms, axis=1)
    value_grad = jnp.concatenate(value_terms, axis=1)
    return (
        main_mixed,
        d_query,
        key_grad.astype(jnp.bfloat16),
        value_grad.astype(jnp.bfloat16),
        d_w_out,
    )


F32, BF16 = jnp.float32, jnp.bfloat16


def dot(a, b, ca, cb):
    return lax.dot_general(a, b, (((ca,), (cb,)), ((), ())), preferred_element_type=F32)


def fused_kernel(
    hidden_hbm, q_ref, k_ref, v_ref, w_hbm, dm_ref, slot_ref,
    mixed_out, dq_out, dk_out, dv_out, dw_out, mixed_ref, dw_ref, hidden_ref, w_ref,
    dm_full, qkv_in, slots_in, dp_send, do_in, q_main, d_cols,
    probs, place, place_t, k_t, v_t, dq_main, att_send, att_all, rs_send, rs_pass, rs_in,
    dq_acc, delta_row, grad_send, grad_in,
    s_dm, s_qkv, s_slot, s_do, s_ca, s_cb, s_at, s_ag, s_rs, s_gr, s_in, s_out,
    r_dm, r_qkv, r_slot, r_do, r_ca, r_cb, r_at, r_ag, r_rs, r_gr,
):
    g = lax.axis_index("grp")
    b = lax.axis_index("blk")
    n_grp, blocks = dm_full.shape[0], qkv_in.shape[1]
    rows, feat = dm_ref.shape
    cols = d_cols.shape[3]
    quarter = rows // n_grp
    seq = rows * blocks
    chunks = 4
    per = blocks // chunks
    step = seq // chunks
    scale = 1.0 / math.sqrt(HD)
    c = g % 2
    z, x = b // 2, b % 2
    nz = blocks // 2
    mate = b + 1 - 2 * x
    core_mate, y_mate, diagonal = g + 1 - 2 * c, (g + 2) % n_grp, n_grp - 1 - g
    owners = [2 + 2 * c, 5 - 5 * c, 3 + 4 * c]
    mine = jnp.where(b == owners[1], 1, jnp.where(b == owners[2], 2, 0))
    is_owner = (b == owners[0]) | (b == owners[1]) | (b == owners[2])
    always = b >= 0
    pending = []
    writes = []

    def write(src, dst):
        copy = pltpu.make_async_copy(src, dst, s_out.at[len(writes)])
        copy.start()
        writes.append(copy)

    def remote(src, dst, ss, rs, dev):
        return pltpu.make_async_remote_copy(
            src_ref=src, dst_ref=dst, send_sem=ss, recv_sem=rs,
            device_id=dev, device_id_type=pl.DeviceIdType.MESH,
        )

    def send(cond, make):
        pl.when(cond)(lambda: make().start())
        pending.append((cond, make))

    def arrive(cond, make):
        pl.when(cond)(lambda: make().wait_recv())

    loads = [
        pltpu.make_async_copy(dm_ref, dm_full.at[g], s_in.at[0]),
        pltpu.make_async_copy(w_hbm, w_ref, s_in.at[1]),
        pltpu.make_async_copy(slot_ref, slots_in.at[b], s_in.at[2]),
        pltpu.make_async_copy(hidden_hbm, hidden_ref, s_in.at[3]),
    ]
    for load in loads:
        load.start()

    def own_tile(i, ref, tile):
        return pltpu.make_async_copy(ref.at[tile], qkv_in.at[i, b], s_in.at[4 + i])

    barrier = pltpu.get_barrier_semaphore()
    for d in range(1, n_grp):
        pl.semaphore_signal(
            barrier, inc=1, device_id={"grp": (g + d) % n_grp}, device_id_type=pl.DeviceIdType.MESH
        )
    for d in range(1, blocks):
        pl.semaphore_signal(
            barrier, inc=1, device_id={"blk": (b + d) % blocks}, device_id_type=pl.DeviceIdType.MESH
        )
    pl.semaphore_wait(barrier, n_grp + blocks - 2)

    def relay(src, buf, slot, dev, ss, rs):
        send(always, lambda: remote(src, buf.at[slot], ss, rs.at[slot], {"grp": dev}))

    def relayed(buf, slot, ss, rs):
        arrive(always, lambda: remote(buf.at[slot], buf.at[slot], ss.at[0], rs.at[slot], {"grp": y_mate}))

    relay(dm_ref, dm_full, g, y_mate, s_dm.at[0], r_dm)
    relay(dm_ref, dm_full, g, core_mate, s_dm.at[1], r_dm)
    for i, ref in enumerate((q_ref, k_ref, v_ref)):
        for h in range(HEAD_GRP):
            tile = (slice(None), slice(h * HD, (h + 1) * HD))
            send(
                b != owners[h],
                lambda i=i, ref=ref, h=h, tile=tile: remote(
                    ref.at[tile], qkv_in.at[i, b], s_qkv.at[i, h], r_qkv.at[i, b], {"blk": owners[h]}
                ),
            )

            @pl.when(b == owners[h])
            def _(i=i, ref=ref, tile=tile):
                own_tile(i, ref, tile).start()

    for h in range(HEAD_GRP):
        send(
            b != owners[h],
            lambda h=h: remote(
                slot_ref, slots_in.at[b], s_slot.at[h], r_slot.at[b], {"blk": owners[h]}
            ),
        )

    loads[2].wait()

    @pl.when(is_owner)
    def _():
        for t in range(blocks):

            @pl.when(b != t)
            def _(t=t):
                remote(slot_ref, slots_in.at[t], s_slot.at[0], r_slot.at[t], {"blk": t}).wait_recv()

        slot_row = jnp.concatenate([slots_in[t] for t in range(blocks)], axis=1)
        slot_col = jnp.transpose(jnp.broadcast_to(slot_row.astype(F32), (8, seq)))[:, :1]
        lane = lax.broadcasted_iota(jnp.int32, (step, seq), 1)
        for i in range(chunks):
            at = lax.broadcasted_iota(jnp.int32, (step, seq), 0) + i * step
            place[i] = jnp.where(at == slot_row, 1.0, 0.0).astype(BF16)
            want = slot_col[i * step : (i + 1) * step].astype(jnp.int32)
            place_t[i] = jnp.where(lane == want, 1.0, 0.0).astype(BF16)

    def features(p):
        lo = pl.multiple_of(p * feat, HD)
        return dot(dm_full[p], w_ref[:, pl.ds(lo, feat)], 1, 1)

    loads[0].wait()
    loads[1].wait()
    d_proj = features(g)
    relayed(dm_full, y_mate, s_dm, r_dm)
    relay(dm_full.at[y_mate], dm_full, y_mate, core_mate, s_dm.at[2], r_dm)
    d_proj = d_proj + features(y_mate)
    relayed(dm_full, core_mate, s_dm, r_dm)
    d_proj = d_proj + features(core_mate)
    relayed(dm_full, diagonal, s_dm, r_dm)
    d_proj = (d_proj + features(diagonal)).astype(BF16)
    for h in range(HEAD_GRP):
        dp_send[h] = d_proj[:, h * HD : (h + 1) * HD]
        send(
            b != owners[h],
            lambda h=h: remote(
                dp_send.at[h], do_in.at[b], s_do.at[h], r_do.at[b], {"blk": owners[h]}
            ),
        )

        @pl.when(b == owners[h])
        def _(h=h):
            do_in[b] = dp_send[h]

    my_rows = pl.ds(pl.multiple_of(g * quarter, quarter), quarter)
    for t in range(blocks):
        lo = t * cols
        view = (lo // feat, my_rows, slice(lo % feat, lo % feat + cols))
        send(
            b != t,
            lambda t=t, view=view: remote(
                dm_full.at[view], d_cols.at[g, b], s_ca.at[t], r_ca.at[b], {"blk": t}
            ),
        )

        @pl.when(b == t)
        def _(view=view):
            d_cols[g, b] = dm_full[view]

    def own_part(i, ref):
        for t in range(blocks):

            @pl.when(b != t)
            def _(t=t):
                remote(
                    qkv_in.at[i, t], qkv_in.at[i, t], s_qkv.at[i, 0], r_qkv.at[i, t], {"blk": t}
                ).wait_recv()

        own_tile(i, ref, (slice(None), slice(0, HD))).wait()

    @pl.when(is_owner)
    def _():
        own_part(0, q_ref)
        for i in range(chunks):
            q_main[i] = dot(place_t[i], qkv_in[0].reshape(seq, HD), 1, 0).astype(BF16)
        own_part(1, k_ref)
        k_t[...] = jnp.transpose(qkv_in[1].reshape(seq, HD).astype(F32)).astype(BF16)
        own_part(2, v_ref)
        v_t[...] = jnp.transpose(qkv_in[2].reshape(seq, HD).astype(F32)).astype(BF16)

    for i in range(chunks):

        @pl.when(is_owner)
        def _(i=i):
            raw = dot(qkv_in[1].reshape(seq, HD), q_main[i], 1, 1)
            peak = jnp.max(raw, axis=0, keepdims=True)
            e = jnp.exp2((raw - peak) * (scale * math.log2(math.e)))
            p = (e * (1.0 / jnp.sum(e, axis=0, keepdims=True))).astype(BF16)
            probs[i] = p
            att = dot(v_t[...], p, 1, 0).astype(BF16)
            for n in range(per):
                att_send[i * per + n] = att[:, n * rows : (n + 1) * rows]

        for t in range(i * per, (i + 1) * per):
            send(
                is_owner & (b != t),
                lambda t=t: remote(
                    att_send.at[t], att_all.at[t, mine], s_at.at[t], r_at.at[mine], {"blk": t}
                ),
            )

    @pl.when(is_owner)
    def _():
        att_all[b, mine] = att_send[b]

    for t in range(blocks):
        arrive(
            b != t,
            lambda t=t: remote(
                d_cols.at[g, t], d_cols.at[g, t], s_ca.at[t], r_ca.at[t], {"blk": t}
            ),
        )
    relay(d_cols.at[g], d_cols, g, y_mate, s_cb.at[0], r_cb)
    relay(d_cols.at[g], d_cols, g, core_mate, s_cb.at[1], r_cb)

    def send_grads(n, first, count):
        for t in range(first, first + count):
            send(
                is_owner & (b != t),
                lambda t=t: remote(
                    grad_send.at[n, t], grad_in.at[n, mine], s_gr.at[n, t], r_gr.at[n, mine], {"blk": t}
                ),
            )

    def backward(j):
        @pl.when(is_owner)
        def _():
            if j == 0:
                for t in range(blocks):

                    @pl.when(b != t)
                    def _(t=t):
                        remote(
                            do_in.at[t], do_in.at[t], s_do.at[0], r_do.at[t], {"blk": t}
                        ).wait_recv()

                for t in range(blocks):
                    both = jnp.transpose(do_in[t].astype(F32)) * att_send[t].astype(F32)
                    delta_row[:, t * rows : (t + 1) * rows] = jnp.sum(both, axis=0, keepdims=True)
            do = do_in[...].reshape(seq, HD)
            p = jnp.concatenate(
                [probs[i, j * step : (j + 1) * step] for i in range(chunks)], axis=1
            )
            d_probs = dot(qkv_in[2, j * per : (j + 1) * per].reshape(step, HD), do, 1, 1)
            ds = (p.astype(F32) * (d_probs - delta_row[...])).astype(BF16)
            dk = (dot(ds, q_main[...].reshape(seq, HD), 1, 0) * scale).astype(BF16)
            dv = dot(p, do, 1, 0).astype(BF16)
            grad_send[1, j * per : (j + 1) * per] = dk.reshape(per, rows, HD)
            grad_send[2, j * per : (j + 1) * per] = dv.reshape(per, rows, HD)
            dq_t = dot(k_t[:, j * step : (j + 1) * step], ds, 1, 0)
            if j == 0:
                dq_acc[...] = dq_t
            elif j < chunks - 1:
                dq_acc[...] += dq_t
            else:
                dq_main[...] = jnp.transpose((dq_acc[...] + dq_t) * scale).astype(BF16)

    def send_block(j):
        send_grads(1, j * per, per)
        send_grads(2, j * per, per)

    backward(0)
    for h in range(HEAD_GRP):
        arrive(
            b != owners[h],
            lambda h=h: remote(
                att_all.at[b, h], att_all.at[b, h], s_at.at[0], r_at.at[h], {"blk": owners[h]}
            ),
        )

    def pass_on(cond, slot, dev, sem):
        send(
            cond,
            lambda: remote(att_all.at[slot], att_all.at[slot], s_ag.at[sem], r_ag.at[slot], {"blk": dev}),
        )

    def landed(cond, slot):
        arrive(
            cond,
            lambda: remote(att_all.at[slot], att_all.at[slot], s_ag.at[0], r_ag.at[slot], {"blk": mate}),
        )

    pass_on(z < nz - 1, b, b + 2, 0)
    pass_on(z > 0, b, b - 2, 1)
    pass_on(always, b, mate, 2)

    def gather_step(s):
        if s >= nz:
            return
        low, high = z >= s, z + s < nz
        landed(low, b - 2 * s)
        pass_on(low & (z < nz - 1), b - 2 * s, b + 2, 4 * s)
        pass_on(low, b - 2 * s, mate, 4 * s + 1)
        landed(high, b + 2 * s)
        pass_on(high & (z > 0), b + 2 * s, b - 2, 4 * s + 2)
        pass_on(high, b + 2 * s, mate, 4 * s + 3)

    gather_step(1)
    backward(1)
    relayed(d_cols, y_mate, s_cb, r_cb)
    relay(d_cols.at[y_mate], d_cols, y_mate, core_mate, s_cb.at[2], r_cb)

    own = jnp.concatenate([att_all[b, h] for h in range(HEAD_GRP)], axis=0)
    own = jnp.transpose(own.astype(F32)).astype(BF16)
    for p in range(n_grp):
        rs_send[p] = dot(own, w_ref[:, p * feat : (p + 1) * feat], 1, 0).astype(BF16)
    for n, p in enumerate((diagonal, core_mate)):
        send(
            always,
            lambda n=n, p=p: remote(
                rs_send.at[p], rs_in.at[n], s_rs.at[n], r_rs.at[n], {"grp": core_mate}
            ),
        )

    def rs_landed(n):
        arrive(always, lambda: remote(rs_in.at[n], rs_in.at[n], s_rs.at[0], r_rs.at[n], {"grp": y_mate}))

    gather_step(2)
    send_block(0)
    send_block(1)
    backward(2)
    rs_landed(0)
    rs_pass[...] = (rs_send[y_mate].astype(F32) + rs_in[0].astype(F32)).astype(BF16)
    send(
        always,
        lambda: remote(rs_pass, rs_in.at[2], s_rs.at[2], r_rs.at[2], {"grp": y_mate}),
    )
    gather_step(3)
    send_block(2)
    backward(3)
    send_block(3)

    @pl.when(is_owner)
    def _():
        turned = dot(place[...].reshape(seq, seq), dq_main[...], 1, 0)
        grad_send[0] = turned.astype(BF16).reshape(blocks, rows, HD)

    send_grads(0, 0, blocks)

    @pl.when(is_owner)
    def _():
        for n in range(3):
            grad_in[n, mine] = grad_send[n, b]

    rs_landed(1)
    rs_landed(2)
    loads[3].wait()
    total = rs_send[g].astype(F32) + rs_in[1].astype(F32) + rs_in[2].astype(F32)
    mixed_ref[...] = (hidden_ref[...].astype(F32) + total).astype(BF16)
    write(mixed_ref, mixed_out)

    relayed(d_cols, core_mate, s_cb, r_cb)
    relayed(d_cols, diagonal, s_cb, r_cb)
    for j in range(nz):
        landed(always, 2 * j + 1 - x)
    grads = jnp.concatenate(
        [d_cols[p, t] for t in range(blocks) for p in range(n_grp)], axis=0
    )
    for h in range(HEAD_GRP):
        att = jnp.concatenate([att_all[t, h] for t in range(blocks)], axis=1)
        dw_ref[h] = dot(att, grads, 1, 0)
        write(dw_ref.at[h], dw_out.at[h * HD : (h + 1) * HD])

    for n, out in enumerate((dq_out, dk_out, dv_out)):
        for h in range(HEAD_GRP):
            arrive(
                b != owners[h],
                lambda n=n, h=h: remote(
                    grad_in.at[n, h], grad_in.at[n, h], s_gr.at[n, 0], r_gr.at[n, h], {"blk": owners[h]}
                ),
            )
            write(grad_in.at[n, h], out.at[:, h * HD : (h + 1) * HD])

    for copy in writes:
        copy.wait()
    for cond, make in pending:
        pl.when(cond)(lambda make=make: make().wait_send())


def write_kernel(*refs):
    srcs, dsts, held, into, out = refs[:5], refs[5:10], refs[10:15], refs[15], refs[16]
    loads = [pltpu.make_async_copy(srcs[i], held[i], into.at[i]) for i in range(5)]
    stores = [pltpu.make_async_copy(held[i], dsts[i], out.at[i]) for i in range(5)]
    for load in loads:
        load.start()
    for load, store in zip(loads, stores):
        load.wait()
        store.start()
    for store in stores:
        store.wait()


def on_device_fused(main_hidden, ctrl_query, ctrl_key, ctrl_value, w_out, d_mixed, control_slot):
    n_grp, blocks = lax.axis_size("grp"), lax.axis_size("blk")
    rows, feat = d_mixed.shape
    width, model = w_out.shape
    cols = model // blocks
    seq = rows * blocks
    step = seq // 4
    dma = pltpu.SemaphoreType.DMA
    sems = [
        dma((n_grp,)), dma((3, HEAD_GRP)), dma((HEAD_GRP,)), dma((HEAD_GRP,)), dma((blocks,)),
        dma((n_grp,)), dma((blocks,)), dma((2 * blocks,)), dma((n_grp,)), dma((3, blocks)), dma((7,)), dma((16,)),
        dma((n_grp,)), dma((3, blocks)), dma((blocks,)), dma((blocks,)), dma((blocks,)),
        dma((n_grp,)), dma((HEAD_GRP,)), dma((blocks,)), dma((n_grp,)), dma((3, HEAD_GRP)),
    ]
    hbm = pl.BlockSpec(memory_space=pltpu.HBM)
    tile = jax.ShapeDtypeStruct((rows, width), BF16)
    results = pl.pallas_call(
        fused_kernel,
        out_shape=(
            jax.ShapeDtypeStruct((rows, feat), BF16), tile, tile, tile,
            jax.ShapeDtypeStruct((width, cols), F32),
        ),
        in_specs=[hbm] * 7,
        out_specs=[hbm] * 5,
        scratch_shapes=[
            pltpu.VMEM((rows, feat), BF16),
            pltpu.VMEM((HEAD_GRP, HD, cols), F32),
            pltpu.VMEM((rows, feat), BF16),
            pltpu.VMEM((width, model), BF16),
            pltpu.VMEM((n_grp, rows, feat), BF16),
            pltpu.VMEM((3, blocks, rows, HD), BF16),
            pltpu.VMEM((blocks, 1, rows), jnp.int32),
            pltpu.VMEM((HEAD_GRP, rows, HD), BF16),
            pltpu.VMEM((blocks, rows, HD), BF16),
            pltpu.VMEM((4, step, HD), BF16),
            pltpu.VMEM((n_grp, blocks, rows // n_grp, cols), BF16),
            pltpu.VMEM((4, seq, step), BF16),
            pltpu.VMEM((4, step, seq), BF16),
            pltpu.VMEM((4, step, seq), BF16),
            pltpu.VMEM((HD, seq), BF16),
            pltpu.VMEM((HD, seq), BF16),
            pltpu.VMEM((seq, HD), BF16),
            pltpu.VMEM((blocks, rows, HD), BF16),
            pltpu.VMEM((blocks, HEAD_GRP, rows, HD), BF16),
            pltpu.VMEM((n_grp, rows, feat), BF16),
            pltpu.VMEM((rows, feat), BF16),
            pltpu.VMEM((3, rows, feat), BF16),
            pltpu.VMEM((HD, seq), F32),
            pltpu.VMEM((1, seq), F32),
            pltpu.VMEM((3, blocks, rows, HD), BF16),
            pltpu.VMEM((3, HEAD_GRP, rows, HD), BF16),
        ] + sems,
        compiler_params=pltpu.CompilerParams(
            collective_id=0, has_side_effects=True, vmem_limit_bytes=60 * 2**20
        ),
        cost_estimate=pl.CostEstimate(
            flops=2 * 5 * seq * seq * HD, bytes_accessed=16 * 2**20, transcendentals=seq * seq
        ),
    )(
        main_hidden, ctrl_query, ctrl_key, ctrl_value, w_out, d_mixed,
        control_slot.reshape(1, rows),
    )
    return pl.pallas_call(
        write_kernel,
        out_shape=tuple(jax.ShapeDtypeStruct(r.shape, r.dtype) for r in results),
        in_specs=[hbm] * 5,
        out_specs=[hbm] * 5,
        scratch_shapes=[pltpu.VMEM(r.shape, r.dtype) for r in results] + [dma((5,)), dma((5,))],
        compiler_params=pltpu.CompilerParams(vmem_limit_bytes=60 * 2**20),
    )(*results)


def solution(mesh):
    in_specs = (
        P("blk", "grp"),
        P("blk", "grp"),
        P("blk", "grp"),
        P("blk", "grp"),
        P("grp", None),
        P("blk", "grp"),
        P("blk"),
    )
    out_specs = (
        P("blk", "grp"),
        P("blk", "grp"),
        P("blk", "grp"),
        P("blk", "grp"),
        P("grp", "blk"),
    )
    body = on_device_fused if mesh.shape["blk"] == 8 else on_device
    return jax.shard_map(
        body, mesh=mesh, in_specs=in_specs, out_specs=out_specs, check_vma=False
    )
```
